32 devices in a mesh: groups: 2 (over x), chan: 16 (over z, y, core).
Axes of the slice: x: 2, y: 2, z: 4, core: 2. Of those that a mesh axis runs over, the one named last changes fastest.
Arguments:
- spectra: bfloat16 [2, 8, 512, 512], P(None, 'groups', 'chan'), parts along dimension 1, may hold values from -6 to 6
- filter_bank: float32 [2, 8, 65], replicated, may hold values from -0.5 to 0.5
- band_index: int32 [512], replicated, may hold values from 0 to 7
- window_mask: int32 [8, 512], P('groups', 'chan'), parts along dimension 0, may hold values 0 or 1
- owner_order: int32 [8], P('groups'), parts along dimension 0, may hold values from 0 to 15, as said below
- source_offset: int32 [8, 32], P('groups'), parts along dimension 0, may hold values from 0 to 31, each once within a row
Outputs:
- cross: bfloat16 [2, 256, 512, 512], P(None, 'groups', 'chan'), parts along dimension 1
The draws below stay inside these ranges and needn't reach their ends.
There are 2 independent parts, one for each index of `groups`. The reference program is written for one: setup_inputs(seed, part) draws one part's arguments, and reference() takes and returns one part's arrays. A program takes and returns all parts, laid end to end along the dimension named above; an argument that names none is the same for every part. Nothing has to cross between parts.
Inputs may be any that keep to these rules, and one draw needn't show every extreme that they name: `owner_order`: 4 distinct device indices, below 16.
All inputs are finite; a program needn't handle non-finite values. No bound on the sum of `window_mask` on one device may be relied on, other than what follows from the above.
Results may differ from the reference program's by a relative error of at most 0.0057.
Values may be sent and summed in bfloat16 or wider, within the bound.
No kernel may reach another device: no remote copies, remote signals or barrier semaphores. Data moves between devices by JAX's collectives and lax.ppermute only.
A program may use at most 192 MiB of HBM per device.

```python
import jax
import jax.numpy as jnp
from jax import lax

F = 512
CH_DEV = 32
WIN = 4
TAPS = 65
NBANK = 8
SMOOTH = 17
ROUNDS = 4
CHANNELS = 512
N_CHAN = 16


def draw_owner_order(key, part):
    devices = CHANNELS // CH_DEV
    first, second = jax.random.split(key)
    middle = 1 + jax.random.permutation(first, devices - 2)[:ROUNDS - 2]
    chosen = jnp.concatenate([jnp.array([0, devices - 1], jnp.int32), middle.astype(jnp.int32)])
    order = jax.random.permutation(second, ROUNDS)
    return chosen[order].astype(jnp.int32)


def plant(entries, key, least, largest):
    index_at = [jax.random.randint(jax.random.fold_in(key, axis), (), 0, length) for axis, length in enumerate(entries.shape)]
    longest = entries.shape.index(max(entries.shape))
    beside = index_at[:longest] + [(index_at[longest] + 1) % entries.shape[longest]] + index_at[longest + 1:]
    return entries.at[tuple(index_at)].set(least).at[tuple(beside)].set(largest)


def level_of(stream_key, dims, cuts, smallest, top_value):
    def one(dim, parts):
        steps = jax.random.uniform(jax.random.fold_in(jax.random.fold_in(stream_key, 6), dim), (parts,), jnp.float32, smallest / len(cuts), top_value / len(cuts))
        return jnp.repeat(jnp.exp(steps), dims[dim] // parts).reshape((-1,) + (1,) * (len(dims) - dim - 1))

    factor_of = one(*cuts[0])
    for cut in cuts[1:]:
        factor_of = factor_of * one(*cut)
    return factor_of


def gaussian(key, dims, deviation, limit, cuts=(), kind=jnp.bfloat16):
    entries = jax.random.normal(key, dims, jnp.float32) * deviation
    if len(cuts) > 0:
        entries = level_of(key, dims, cuts, -0.22, 0.18) * entries
    return jnp.clip(entries, min=-limit, max=limit).astype(kind)


def setup_inputs(seed: int = 0, part: int = 0) -> dict:
    key_of = jax.random.split(jax.random.key(seed), 7)
    part_splits = jax.random.split(jax.random.fold_in(key_of[6], part), 7)
    return {
        "spectra": gaussian(part_splits[0], (2, WIN, CHANNELS, F), 1.0, 6.0, ((2, 16),)),
        "filter_bank": gaussian(key_of[1], (2, NBANK, TAPS), (2 * TAPS) ** -0.5, 0.5, (), jnp.float32),
        "band_index": plant(jax.random.randint(key_of[2], (F,), 0, NBANK), jax.random.fold_in(key_of[2], 1), 0, NBANK - 1).astype(jnp.int32),
        "window_mask": plant((jax.random.randint(part_splits[3], (WIN, CHANNELS), 0, 8) < 7).astype(jnp.int32), jax.random.fold_in(part_splits[3], 1), 0, 1),
        "owner_order": draw_owner_order(jax.random.fold_in(jax.random.fold_in(key_of[6], part), 71), part),
        "source_offset": jax.vmap(lambda own: jax.random.permutation(own, CH_DEV))(jax.random.split(part_splits[5], ROUNDS)).reshape((ROUNDS, CH_DEV)).astype(jnp.int32),
    }


water_level = 0.05

def filter_taps(filter_bank, band_index):
    choose = (band_index[:, None] == jnp.arange(NBANK, dtype=jnp.int32)[None, :]).astype(jnp.float32)
    return jnp.einsum('fb,pbk->pkf', choose, filter_bank, precision=lax.Precision.HIGHEST)

def velocity_whiten(padded, taps, window_mask):
    count = padded.shape[2] - (TAPS - 1)
    real_sum = jnp.zeros((padded.shape[1], count, padded.shape[3]), jnp.float32)
    imag_sum = jnp.zeros((padded.shape[1], count, padded.shape[3]), jnp.float32)
    for tap_pos in range(TAPS):
        real_in = padded[0, :, tap_pos:tap_pos + count]
        imag_in = padded[1, :, tap_pos:tap_pos + count]
        real_sum = real_sum + taps[0, tap_pos] * real_in - taps[1, tap_pos] * imag_in
        imag_sum = imag_sum + taps[0, tap_pos] * imag_in + taps[1, tap_pos] * real_in
    power = real_sum * real_sum + imag_sum * imag_sum
    reach = SMOOTH // 2
    padded_power = jnp.pad(power, ((0, 0), (0, 0), (reach, reach)))
    smooth = jnp.zeros_like(power)
    for shift_pos in range(SMOOTH):
        smooth = smooth + padded_power[:, :, shift_pos:shift_pos + power.shape[2]]
    smooth = smooth / SMOOTH
    scale = lax.rsqrt(smooth + water_level) * window_mask.astype(jnp.float32)[:, :, None]
    return jnp.stack([real_sum * scale, imag_sum * scale]).astype(jnp.bfloat16)

def cross_block(source, whitened):
    src_real = source[0].astype(jnp.float32)
    src_imag = source[1].astype(jnp.float32)
    loc_real = whitened[0].astype(jnp.float32)
    loc_imag = whitened[1].astype(jnp.float32)
    real_out = jnp.einsum('wsf,wcf->scf', src_real, loc_real) + jnp.einsum('wsf,wcf->scf', src_imag, loc_imag)
    imag_out = jnp.einsum('wsf,wcf->scf', src_real, loc_imag) - jnp.einsum('wsf,wcf->scf', src_imag, loc_real)
    return (jnp.stack([real_out, imag_out]) / WIN).astype(jnp.bfloat16)

def reference(spectra, filter_bank, band_index, window_mask, owner_order, source_offset):
    half_width = TAPS // 2
    taps = filter_taps(filter_bank, band_index)
    padded = jnp.pad(spectra.astype(jnp.float32), ((0, 0), (0, 0), (half_width, half_width), (0, 0)))
    whitened = velocity_whiten(padded, taps, window_mask)
    channel_index = (owner_order[:, None] * CH_DEV + source_offset).reshape(-1).astype(jnp.int32)
    picked = whitened[:, :, channel_index, :]
    picked = picked.reshape(2, WIN, ROUNDS, CH_DEV, F).transpose(2, 0, 1, 3, 4)
    blocks = lax.map(lambda source: cross_block(source, whitened), picked)
    return blocks.transpose(1, 0, 2, 3, 4).reshape(2, ROUNDS * CH_DEV, CH_DEV * N_CHAN, F)
```

```python
import functools

import jax
import jax.numpy as jnp
from jax import lax
from jax.experimental import pallas as pl
from jax.experimental.pallas import tpu as pltpu
from jax.sharding import PartitionSpec as P

SMOOTH = 17
LANES = 128
WATER = 0.05
SRC_STEP = 8


def prep_kernel(bank_ref, whi_ref, wlo_ref, band_ref):
    banks = bank_ref.shape[1]
    ch = whi_ref.shape[0] // (2 * banks)

    def skewed(row):
        tile = jnp.broadcast_to(row, (ch, LANES))
        return pltpu.roll(tile, 0, 1, stride=1, stride_axis=0)

    for b in range(banks):
        real = skewed(bank_ref[0, b : b + 1, :])
        imag = skewed(bank_ref[1, b : b + 1, :])
        base = b * 2 * ch
        for row, left, right in ((base, real, -imag), (base + ch, imag, real)):
            for col, val in ((0, left), (LANES, right)):
                high = val.astype(jnp.bfloat16)
                low = (val - high.astype(jnp.float32)).astype(jnp.bfloat16)
                whi_ref[row : row + ch, col : col + LANES] = high
                wlo_ref[row : row + ch, col : col + LANES] = low
    rows = lax.broadcasted_iota(jnp.int32, band_ref.shape, 0)
    cols = lax.broadcasted_iota(jnp.int32, band_ref.shape, 1)
    near = jnp.abs(rows - cols) <= SMOOTH // 2
    band_ref[...] = jnp.where(near, 1.0, 0.0).astype(jnp.bfloat16)


def main_kernel(
    item_ref, offset_ref, prev_ref, cur_ref, next_ref, whi_ref, wlo_ref, band_ref, index_ref,
    out_ref, filt_ref, local_ref, source_ref, *, n_chan, win, ch, rounds,
):
    step = pl.program_id(0)
    items = rounds + 1
    freq = index_ref.shape[1]
    banks = whi_ref.shape[0] // (2 * ch)

    @pl.when(step < items)
    def _():
        block = item_ref[step]
        zero = jnp.zeros((), jnp.bfloat16)
        has_prev = block > 0
        has_next = block < n_chan - 1
        gap = jnp.zeros((LANES - 3 * ch, freq), jnp.bfloat16)

        def one_window(w, _):
            parts = []
            for p in range(2):
                at = pl.ds(pl.multiple_of((p * win + w) * ch, ch), ch)
                parts.append(jnp.where(has_prev, prev_ref[0, at, :], zero))
                parts.append(cur_ref[0, at, :])
                parts.append(jnp.where(has_next, next_ref[0, at, :], zero))
                parts.append(gap)
            x = jnp.concatenate(parts, axis=0)
            y = jnp.dot(whi_ref[...], x, preferred_element_type=jnp.float32)
            y = y + jnp.dot(wlo_ref[...], x, preferred_element_type=jnp.float32)
            pick = y[: 2 * ch]
            for b in range(1, banks):
                pick = jnp.where(index_ref[...] == b, y[b * 2 * ch : (b + 1) * 2 * ch], pick)
            at = pl.ds(pl.multiple_of(w * ch, ch), ch)
            filt_ref[0, at, :] = pick[:ch]
            filt_ref[1, at, :] = pick[ch:]
            return 0

        lax.fori_loop(0, win, one_window, 0)
        real = filt_ref[0]
        imag = filt_ref[1]
        power = real * real + imag * imag
        high = power.astype(jnp.bfloat16)
        low = (power - high.astype(jnp.float32)).astype(jnp.bfloat16)
        total = jnp.dot(high, band_ref[...], preferred_element_type=jnp.float32)
        total = total + jnp.dot(low, band_ref[...], preferred_element_type=jnp.float32)
        count = win * ch
        flags = cur_ref[0, 2 * count : 2 * count + 16, :LANES].astype(jnp.float32)[:1]
        rows = lax.broadcasted_iota(jnp.int32, (count, LANES), 0)
        cols = lax.broadcasted_iota(jnp.int32, (count, LANES), 1)
        valid = jnp.sum(jnp.where(rows == cols, flags, 0.0), axis=1, keepdims=True)
        scale = lax.rsqrt(total / SMOOTH + WATER) * valid
        real = (real * scale).astype(jnp.bfloat16).astype(jnp.float32)
        imag = (imag * scale).astype(jnp.bfloat16).astype(jnp.float32)

        @pl.when(step == 0)
        def _():
            for t in range(freq // LANES):
                local_ref[0, t] = real[:, t * LANES : (t + 1) * LANES]
                local_ref[1, t] = imag[:, t * LANES : (t + 1) * LANES]

        @pl.when(step > 0)
        def _():
            for t in range(freq // LANES):
                source_ref[step - 1, 0, t] = real[:, t * LANES : (t + 1) * LANES] / win
                source_ref[step - 1, 1, t] = imag[:, t * LANES : (t + 1) * LANES] / win

    @pl.when(step >= items)
    def _():
        first = (step - items) * SRC_STEP
        r = first // ch
        j0 = first % ch

        def one_tile(ft, _):
            at = pl.ds(pl.multiple_of(ft * LANES, LANES), LANES)
            mine = [
                (local_ref[0, ft, w * ch : (w + 1) * ch, :], local_ref[1, ft, w * ch : (w + 1) * ch, :])
                for w in range(win)
            ]
            for j in range(SRC_STEP):
                row = offset_ref[r, j0 + j]
                re = im = None
                for w in range(win):
                    sr = source_ref[r, 0, ft, pl.ds(w * ch + row, 8, stride=0), :]
                    si = source_ref[r, 1, ft, pl.ds(w * ch + row, 8, stride=0), :]
                    sr = jnp.concatenate([sr] * (ch // 8), axis=0)
                    si = jnp.concatenate([si] * (ch // 8), axis=0)
                    lr, li = mine[w]
                    a = sr * lr + si * li
                    b = sr * li - si * lr
                    re = a if re is None else re + a
                    im = b if im is None else im + b
                out_ref[0, j, :, at] = re.astype(jnp.bfloat16)
                out_ref[1, j, :, at] = im.astype(jnp.bfloat16)
            return 0

        lax.fori_loop(0, freq // LANES, one_tile, 0)


def body(spectra, filter_bank, band_index, window_mask, owner_order, source_offset):
    n_chan = lax.axis_size("chan")
    me = lax.axis_index("chan")
    _, win, ch, freq = spectra.shape
    banks, taps = filter_bank.shape[1:]
    rounds = owner_order.shape[0]
    count = win * ch

    flags = window_mask.astype(jnp.bfloat16).reshape(1, count)
    flags = jnp.pad(flags, ((0, 15), (0, freq - count)))
    payload = jnp.concatenate([spectra.reshape(2 * count, freq), flags], axis=0)
    gathered = lax.all_gather(payload, "chan")

    padded_bank = jnp.pad(filter_bank, ((0, 0), (0, 0), (0, LANES - taps)))
    whi, wlo, band = pl.pallas_call(
        prep_kernel,
        out_shape=(
            jax.ShapeDtypeStruct((banks * 2 * ch, 2 * LANES), jnp.bfloat16),
            jax.ShapeDtypeStruct((banks * 2 * ch, 2 * LANES), jnp.bfloat16),
            jax.ShapeDtypeStruct((freq, freq), jnp.bfloat16),
        ),
        name="prep",
    )(padded_bank)

    items = jnp.concatenate([me[None].astype(jnp.int32), owner_order])
    n_items = rounds + 1
    rows = payload.shape[0]
    sources = rounds * ch
    last = n_items - 1
    grid_spec = pltpu.PrefetchScalarGridSpec(
        num_scalar_prefetch=2,
        grid=(n_items + sources // SRC_STEP,),
        in_specs=[
            pl.BlockSpec(
                (1, rows, freq),
                lambda s, it, of: (jnp.maximum(it[jnp.minimum(s, last)] - 1, 0), 0, 0),
            ),
            pl.BlockSpec((1, rows, freq), lambda s, it, of: (it[jnp.minimum(s, last)], 0, 0)),
            pl.BlockSpec(
                (1, rows, freq),
                lambda s, it, of: (jnp.minimum(it[jnp.minimum(s, last)] + 1, n_chan - 1), 0, 0),
            ),
            pl.BlockSpec((banks * 2 * ch, 2 * LANES), lambda s, it, of: (0, 0)),
            pl.BlockSpec((banks * 2 * ch, 2 * LANES), lambda s, it, of: (0, 0)),
            pl.BlockSpec((freq, freq), lambda s, it, of: (0, 0)),
            pl.BlockSpec((1, freq), lambda s, it, of: (0, 0)),
        ],
        out_specs=pl.BlockSpec(
            (2, SRC_STEP, ch, freq), lambda s, it, of: (0, jnp.maximum(s - n_items, 0), 0, 0)
        ),
        scratch_shapes=[
            pltpu.VMEM((2, count, freq), jnp.float32),
            pltpu.VMEM((2, freq // LANES, count, LANES), jnp.float32),
            pltpu.VMEM((rounds, 2, freq // LANES, count, LANES), jnp.float32),
        ],
    )
    return pl.pallas_call(
        functools.partial(main_kernel, n_chan=n_chan, win=win, ch=ch, rounds=rounds),
        grid_spec=grid_spec,
        out_shape=jax.ShapeDtypeStruct((2, sources, ch, freq), jnp.bfloat16),
        compiler_params=pltpu.CompilerParams(vmem_limit_bytes=48 * 1024 * 1024),
        name="whiten_cross",
    )(
        items, source_offset, gathered, gathered, gathered, whi, wlo, band,
        band_index.reshape(1, freq),
    )


def solution(mesh):
    in_specs = (
        P(None, "groups", "chan", None),
        P(),
        P(),
        P("groups", "chan"),
        P("groups"),
        P("groups", None),
    )
    out_specs = P(None, "groups", "chan", None)
    return jax.shard_map(body, mesh=mesh, in_specs=in_specs, out_specs=out_specs, check_vma=False)
```

```python
import functools

import jax
import jax.numpy as jnp
from jax import lax
from jax.experimental import pallas as pl
from jax.experimental.pallas import tpu as pltpu
from jax.sharding import PartitionSpec as P

SMOOTH = 17
LANES = 128
WATER = 0.05
SRC_STEP = 8
VMEM = pltpu.CompilerParams(vmem_limit_bytes=56 * 1024 * 1024)


def split_kernel(spectra_ref, piece_ref):
    _, win, _, freq = spectra_ref.shape
    tiles = freq // LANES
    for w in range(win):
        for t in range(tiles):
            piece_ref[w * tiles + t] = spectra_ref[:, w, :, t * LANES : (t + 1) * LANES]


def prep_kernel(bank_ref, whi_ref, wlo_ref, band_ref):
    banks = bank_ref.shape[1]
    ch = whi_ref.shape[0] // (2 * banks)

    def skewed(row):
        tile = jnp.broadcast_to(row, (ch, LANES))
        return pltpu.roll(tile, 0, 1, stride=1, stride_axis=0)

    for b in range(banks):
        real = skewed(bank_ref[0, b : b + 1, :])
        imag = skewed(bank_ref[1, b : b + 1, :])
        base = b * 2 * ch
        for row, left, right in ((base, real, -imag), (base + ch, imag, real)):
            for col, val in ((0, left), (LANES, right)):
                high = val.astype(jnp.bfloat16)
                low = (val - high.astype(jnp.float32)).astype(jnp.bfloat16)
                whi_ref[row : row + ch, col : col + LANES] = high
                wlo_ref[row : row + ch, col : col + LANES] = low
    rows = lax.broadcasted_iota(jnp.int32, band_ref.shape, 0)
    cols = lax.broadcasted_iota(jnp.int32, band_ref.shape, 1)
    near = jnp.abs(rows - cols) <= SMOOTH // 2
    band_ref[...] = jnp.where(near, 1.0, 0.0).astype(jnp.bfloat16)


def filtered_block(x, whi_ref, wlo_ref, index, ch):
    banks = whi_ref.shape[0] // (2 * ch)
    y = jnp.dot(whi_ref[...], x, preferred_element_type=jnp.float32)
    y = y + jnp.dot(wlo_ref[...], x, preferred_element_type=jnp.float32)
    pick = y[: 2 * ch]
    for b in range(1, banks):
        pick = jnp.where(index == b, y[b * 2 * ch : (b + 1) * 2 * ch], pick)
    return pick


def whitened_block(real, imag, flags, band_ref):
    count = real.shape[0]
    power = real * real + imag * imag
    high = power.astype(jnp.bfloat16)
    low = (power - high.astype(jnp.float32)).astype(jnp.bfloat16)
    total = jnp.dot(high, band_ref[...], preferred_element_type=jnp.float32)
    total = total + jnp.dot(low, band_ref[...], preferred_element_type=jnp.float32)
    rows = lax.broadcasted_iota(jnp.int32, (count, count), 0)
    cols = lax.broadcasted_iota(jnp.int32, (count, count), 1)
    valid = jnp.sum(jnp.where(rows == cols, flags, 0.0), axis=1, keepdims=True)
    scale = lax.rsqrt(total / SMOOTH + WATER) * valid
    real = (real * scale).astype(jnp.bfloat16).astype(jnp.float32)
    imag = (imag * scale).astype(jnp.bfloat16).astype(jnp.float32)
    return real, imag


def source_kernel(piece_id_ref, owner_ref, x_ref, whi_ref, wlo_ref, index_ref, out_ref):
    n_chan, _, _, ch, _ = x_ref.shape
    rounds = out_ref.shape[1]
    tiles = index_ref.shape[0]
    tile = lax.rem(piece_id_ref[0] + pl.program_id(0), tiles)
    zero = jnp.zeros((), jnp.bfloat16)
    gap = jnp.zeros((LANES - 3 * ch, LANES), jnp.bfloat16)
    columns = []
    for r in range(rounds):
        block = owner_ref[r]
        before = jnp.maximum(block - 1, 0)
        after = jnp.minimum(block + 1, n_chan - 1)
        parts = []
        for p in range(2):
            parts.append(jnp.where(block > 0, x_ref[before, 0, p], zero))
            parts.append(x_ref[block, 0, p])
            parts.append(jnp.where(block < n_chan - 1, x_ref[after, 0, p], zero))
            parts.append(gap)
        columns.append(jnp.concatenate(parts, axis=0))
    x = jnp.concatenate(columns, axis=1)
    index = jnp.concatenate([index_ref[tile]] * rounds, axis=1)
    pick = filtered_block(x, whi_ref, wlo_ref, index, ch).astype(jnp.bfloat16)
    for r in range(rounds):
        for p in range(2):
            out_ref[0, r, p] = pick[p * ch : (p + 1) * ch, r * LANES : (r + 1) * LANES]


def own_kernel(
    prev_ref, cur_ref, next_ref, whi_ref, wlo_ref, band_ref, index_ref, flags_ref, out_ref, filt_ref
):
    _, win, ch, freq = cur_ref.shape
    gap = jnp.zeros((LANES - 3 * ch, freq), jnp.bfloat16)

    def one_window(w, _):
        parts = []
        for p in range(2):
            parts += [prev_ref[p, w], cur_ref[p, w], next_ref[p, w], gap]
        x = jnp.concatenate(parts, axis=0)
        pick = filtered_block(x, whi_ref, wlo_ref, index_ref[...], ch)
        at = pl.ds(pl.multiple_of(w * ch, ch), ch)
        filt_ref[0, at, :] = pick[:ch]
        filt_ref[1, at, :] = pick[ch:]
        return 0

    lax.fori_loop(0, win, one_window, 0)
    flags = flags_ref[...].astype(jnp.float32)
    real, imag = whitened_block(filt_ref[0], filt_ref[1], flags, band_ref)
    for t in range(freq // LANES):
        out_ref[0, t] = real[:, t * LANES : (t + 1) * LANES]
        out_ref[1, t] = imag[:, t * LANES : (t + 1) * LANES]


def cross_kernel(
    owner_ref, offset_ref, filt_ref, local_ref, band_ref, flags_ref, out_ref, source_ref
):
    pieces, _, _, ch, _ = filt_ref.shape
    tiles = local_ref.shape[1]
    win = pieces // tiles
    per_round = ch // SRC_STEP
    step = pl.program_id(0)
    r = step // per_round
    j0 = lax.rem(step, per_round) * SRC_STEP

    @pl.when(j0 == 0)
    def _():
        parts = []
        for p in range(2):
            rows = [
                jnp.concatenate([filt_ref[w * tiles + t, 0, p] for t in range(tiles)], axis=1)
                for w in range(win)
            ]
            parts.append(jnp.concatenate(rows, axis=0).astype(jnp.float32))
        flags = flags_ref[owner_ref[r]].astype(jnp.float32)
        real, imag = whitened_block(parts[0], parts[1], flags, band_ref)
        for t in range(tiles):
            source_ref[0, t] = real[:, t * LANES : (t + 1) * LANES] / win
            source_ref[1, t] = imag[:, t * LANES : (t + 1) * LANES] / win

    def one_tile(ft, _):
        at = pl.ds(pl.multiple_of(ft * LANES, LANES), LANES)
        mine = [
            (local_ref[0, ft, w * ch : (w + 1) * ch, :], local_ref[1, ft, w * ch : (w + 1) * ch, :])
            for w in range(win)
        ]
        for j in range(SRC_STEP):
            row = offset_ref[r, j0 + j]
            re = im = None
            for w in range(win):
                sr = source_ref[0, ft, pl.ds(w * ch + row, 8, stride=0), :]
                si = source_ref[1, ft, pl.ds(w * ch + row, 8, stride=0), :]
                sr = jnp.concatenate([sr] * (ch // 8), axis=0)
                si = jnp.concatenate([si] * (ch // 8), axis=0)
                lr, li = mine[w]
                a = sr * lr + si * li
                b = sr * li - si * lr
                re = a if re is None else re + a
                im = b if im is None else im + b
            out_ref[0, j, :, at] = re.astype(jnp.bfloat16)
            out_ref[1, j, :, at] = im.astype(jnp.bfloat16)
        return 0

    lax.fori_loop(0, tiles, one_tile, 0)


def body(spectra, filter_bank, band_index, window_mask, owner_order, source_offset):
    n_chan = lax.axis_size("chan")
    me = lax.axis_index("chan").astype(jnp.int32)
    _, win, ch, freq = spectra.shape
    banks, taps = filter_bank.shape[1:]
    rounds = owner_order.shape[0]
    count = win * ch
    tiles = freq // LANES
    pieces = win * tiles
    sources = rounds * ch
    smem = pl.BlockSpec(memory_space=pltpu.SMEM)
    vmem = pl.BlockSpec(memory_space=pltpu.VMEM)

    split = pl.pallas_call(
        split_kernel,
        out_shape=jax.ShapeDtypeStruct((pieces, 2, ch, LANES), jnp.bfloat16),
        name="split",
    )(spectra)
    if n_chan == pieces:
        held = lax.all_to_all(split, "chan", 0, 0)[:, None]
        first = me
    else:
        held = lax.all_gather(split, "chan")
        first = jnp.int32(0)

    ends = n_chan - 1
    before = lax.ppermute(spectra, "chan", [(i, i + 1) for i in range(ends)])
    after = lax.ppermute(spectra, "chan", [(i + 1, i) for i in range(ends)])
    flags = window_mask.reshape(1, count)
    all_flags = lax.all_gather(flags, "chan")

    padded_bank = jnp.pad(filter_bank, ((0, 0), (0, 0), (0, LANES - taps)))
    weights = jax.ShapeDtypeStruct((banks * 2 * ch, 2 * LANES), jnp.bfloat16)
    whi, wlo, band = pl.pallas_call(
        prep_kernel,
        out_shape=(weights, weights, jax.ShapeDtypeStruct((freq, freq), jnp.bfloat16)),
        name="prep",
    )(padded_bank)

    count_here = held.shape[1]
    filtered = pl.pallas_call(
        source_kernel,
        grid=(count_here,),
        in_specs=[
            smem,
            smem,
            pl.BlockSpec((n_chan, 1, 2, ch, LANES), lambda s: (0, s, 0, 0, 0)),
            vmem,
            vmem,
            vmem,
        ],
        out_specs=pl.BlockSpec((1, rounds, 2, ch, LANES), lambda s: (s, 0, 0, 0, 0)),
        out_shape=jax.ShapeDtypeStruct((count_here, rounds, 2, ch, LANES), jnp.bfloat16),
        compiler_params=VMEM,
        name="source_filter",
    )(first[None], owner_order, held, whi, wlo, band_index.reshape(tiles, 1, LANES))
    if n_chan == pieces:
        filtered = lax.all_gather(filtered, "chan", tiled=True)

    local = pl.pallas_call(
        own_kernel,
        out_shape=jax.ShapeDtypeStruct((2, tiles, count, LANES), jnp.float32),
        in_specs=[vmem] * 8,
        out_specs=vmem,
        scratch_shapes=[pltpu.VMEM((2, count, freq), jnp.float32)],
        compiler_params=VMEM,
        cost_estimate=pl.CostEstimate(
            flops=4 * banks * 2 * ch * 2 * LANES * win * freq, bytes_accessed=3 << 20, transcendentals=0
        ),
        name="own_whiten",
    )(before, spectra, after, whi, wlo, band, band_index.reshape(1, freq), flags)

    per_round = ch // SRC_STEP
    return pl.pallas_call(
        cross_kernel,
        grid=(sources // SRC_STEP,),
        in_specs=[
            smem,
            smem,
            pl.BlockSpec((pieces, 1, 2, ch, LANES), lambda s: (0, s // per_round, 0, 0, 0)),
            vmem,
            vmem,
            vmem,
        ],
        out_specs=pl.BlockSpec((2, SRC_STEP, ch, freq), lambda s: (0, s, 0, 0)),
        out_shape=jax.ShapeDtypeStruct((2, sources, ch, freq), jnp.bfloat16),
        scratch_shapes=[pltpu.VMEM((2, tiles, count, LANES), jnp.float32)],
        compiler_params=VMEM,
        name="cross",
    )(owner_order, source_offset, filtered, local, band, all_flags)


def solution(mesh):
    in_specs = (
        P(None, "groups", "chan", None),
        P(),
        P(),
        P("groups", "chan"),
        P("groups"),
        P("groups", None),
    )
    out_specs = P(None, "groups", "chan", None)
    return jax.shard_map(body, mesh=mesh, in_specs=in_specs, out_specs=out_specs, check_vma=False)
```

```python
import functools

import jax
import jax.numpy as jnp
from jax import lax
from jax.experimental import pallas as pl
from jax.experimental.pallas import tpu as pltpu
from jax.sharding import PartitionSpec as P

SMOOTH = 17
LANES = 128
WATER = 0.05
SRC_STEP = 8
VMEM = pltpu.CompilerParams(vmem_limit_bytes=56 * 1024 * 1024)


def split_kernel(spectra_ref, flags_ref, piece_ref):
    _, win, ch, freq = spectra_ref.shape
    tiles = freq // LANES
    extra = piece_ref.shape[1] - 2 * ch
    for w in range(win):
        flags = jnp.broadcast_to(flags_ref[w : w + 1, :], (extra, ch)).astype(jnp.float32)
        for t in range(tiles):
            at = slice(t * LANES, (t + 1) * LANES)
            piece_ref[w * tiles + t, :ch] = spectra_ref[0, w, :, at]
            piece_ref[w * tiles + t, ch : 2 * ch] = spectra_ref[1, w, :, at]
            piece_ref[w * tiles + t, 2 * ch :] = jnp.zeros((extra, LANES), jnp.bfloat16)
            piece_ref[w * tiles + t, 2 * ch :, :ch] = flags.astype(jnp.bfloat16)


def prep_kernel(bank_ref, whi_ref, wlo_ref, band_ref, padded_ref):
    _, banks, taps = bank_ref.shape
    ch = whi_ref.shape[0] // (2 * banks)
    padded_ref[...] = jnp.zeros(padded_ref.shape, jnp.float32)
    padded_ref[:, :, :taps] = bank_ref[...]

    def skewed(row):
        tile = jnp.broadcast_to(row, (ch, LANES))
        return pltpu.roll(tile, 0, 1, stride=1, stride_axis=0)

    for b in range(banks):
        real = skewed(padded_ref[0, b : b + 1, :])
        imag = skewed(padded_ref[1, b : b + 1, :])
        base = b * 2 * ch
        for row, left, right in ((base, real, -imag), (base + ch, imag, real)):
            for col, val in ((0, left), (LANES, right)):
                high = val.astype(jnp.bfloat16)
                low = (val - high.astype(jnp.float32)).astype(jnp.bfloat16)
                whi_ref[row : row + ch, col : col + LANES] = high
                wlo_ref[row : row + ch, col : col + LANES] = low
    rows = lax.broadcasted_iota(jnp.int32, band_ref.shape, 0)
    cols = lax.broadcasted_iota(jnp.int32, band_ref.shape, 1)
    near = jnp.abs(rows - cols) <= SMOOTH // 2
    band_ref[...] = jnp.where(near, 1.0, 0.0).astype(jnp.bfloat16)


def flag_column(row):
    ch = row.shape[1]
    rows = lax.broadcasted_iota(jnp.int32, (ch, ch), 0)
    cols = lax.broadcasted_iota(jnp.int32, (ch, ch), 1)
    return jnp.sum(jnp.where(rows == cols, row.astype(jnp.float32), 0.0), axis=1, keepdims=True)


def filtered_block(x, whi_ref, wlo_ref, index, ch):
    banks = whi_ref.shape[0] // (2 * ch)
    y = jnp.dot(whi_ref[...], x, preferred_element_type=jnp.float32)
    y = y + jnp.dot(wlo_ref[...], x, preferred_element_type=jnp.float32)
    pick = y[: 2 * ch]
    for b in range(1, banks):
        pick = jnp.where(index == b, y[b * 2 * ch : (b + 1) * 2 * ch], pick)
    return pick


def whitened_block(real, imag, band_ref):
    power = real * real + imag * imag
    high = power.astype(jnp.bfloat16)
    low = (power - high.astype(jnp.float32)).astype(jnp.bfloat16)
    total = jnp.dot(high, band_ref[...], preferred_element_type=jnp.float32)
    total = total + jnp.dot(low, band_ref[...], preferred_element_type=jnp.float32)
    scale = lax.rsqrt(total / SMOOTH + WATER)
    real = (real * scale).astype(jnp.bfloat16).astype(jnp.float32)
    imag = (imag * scale).astype(jnp.bfloat16).astype(jnp.float32)
    return real, imag


def source_kernel(piece_id_ref, owner_ref, x_ref, whi_ref, wlo_ref, index_ref, out_ref):
    n_chan = x_ref.shape[0]
    _, rounds, _, ch, _ = out_ref.shape
    tiles = index_ref.shape[0]
    tile = lax.rem(piece_id_ref[0] + pl.program_id(0), tiles)
    zero = jnp.zeros((), jnp.bfloat16)
    gap = jnp.zeros((LANES - 3 * ch, LANES), jnp.bfloat16)
    columns = []
    for r in range(rounds):
        block = owner_ref[r]
        before = jnp.maximum(block - 1, 0)
        after = jnp.minimum(block + 1, n_chan - 1)
        parts = []
        for p in range(2):
            at = slice(p * ch, (p + 1) * ch)
            parts.append(jnp.where(block > 0, x_ref[before, 0, at], zero))
            parts.append(x_ref[block, 0, at])
            parts.append(jnp.where(block < n_chan - 1, x_ref[after, 0, at], zero))
            parts.append(gap)
        columns.append(jnp.concatenate(parts, axis=0))
    x = jnp.concatenate(columns, axis=1)
    index = jnp.concatenate([index_ref[tile]] * rounds, axis=1)
    pick = filtered_block(x, whi_ref, wlo_ref, index, ch)
    for r in range(rounds):
        flags = x_ref[owner_ref[r], 0, 2 * ch :].astype(jnp.float32)[:1, :ch]
        valid = flag_column(flags)
        for p in range(2):
            part = pick[p * ch : (p + 1) * ch, r * LANES : (r + 1) * LANES] * valid
            out_ref[0, r, p] = part.astype(jnp.bfloat16)


def own_kernel(
    prev_ref, cur_ref, next_ref, whi_ref, wlo_ref, band_ref, index_ref, flags_ref, out_ref, filt_ref
):
    _, win, ch, freq = cur_ref.shape
    gap = jnp.zeros((LANES - 3 * ch, freq), jnp.bfloat16)

    def one_window(w, _):
        parts = []
        for p in range(2):
            parts += [prev_ref[p, w], cur_ref[p, w], next_ref[p, w], gap]
        x = jnp.concatenate(parts, axis=0)
        pick = filtered_block(x, whi_ref, wlo_ref, index_ref[...], ch)
        at = pl.ds(pl.multiple_of(w * ch, ch), ch)
        filt_ref[0, at, :] = pick[:ch]
        filt_ref[1, at, :] = pick[ch:]
        return 0

    lax.fori_loop(0, win, one_window, 0)
    valid = jnp.concatenate([flag_column(flags_ref[w : w + 1, :]) for w in range(win)], axis=0)
    real, imag = whitened_block(filt_ref[0] * valid, filt_ref[1] * valid, band_ref)
    for t in range(freq // LANES):
        out_ref[0, t] = real[:, t * LANES : (t + 1) * LANES]
        out_ref[1, t] = imag[:, t * LANES : (t + 1) * LANES]


def cross_kernel(me_ref, offset_ref, *refs, masks):
    filt_refs = refs[: len(masks)]
    local_ref, band_ref, out_ref, piece_ref, source_ref = refs[len(masks) :]
    ch = out_ref.shape[2]
    pieces = piece_ref.shape[0]
    tiles = local_ref.shape[1]
    win = pieces // tiles
    per_round = ch // SRC_STEP
    step = pl.program_id(0)
    r = step // per_round
    j0 = lax.rem(step, per_round) * SRC_STEP

    @pl.when(j0 == 0)
    def _():
        stride = pieces // filt_refs[0].shape[0]
        for mask, ref in zip(masks, filt_refs):
            for k in range(ref.shape[0]):
                piece_ref[me_ref[0] ^ (mask ^ (k * stride))] = ref[k, 0]
        parts = []
        for p in range(2):
            rows = [
                jnp.concatenate([piece_ref[w * tiles + t, p] for t in range(tiles)], axis=1)
                for w in range(win)
            ]
            parts.append(jnp.concatenate(rows, axis=0).astype(jnp.float32))
        real, imag = whitened_block(parts[0], parts[1], band_ref)
        for t in range(tiles):
            source_ref[0, t] = real[:, t * LANES : (t + 1) * LANES] / win
            source_ref[1, t] = imag[:, t * LANES : (t + 1) * LANES] / win

    def one_tile(ft, _):
        at = pl.ds(pl.multiple_of(ft * LANES, LANES), LANES)
        mine = [
            (local_ref[0, ft, w * ch : (w + 1) * ch, :], local_ref[1, ft, w * ch : (w + 1) * ch, :])
            for w in range(win)
        ]
        for j in range(SRC_STEP):
            row = offset_ref[r, j0 + j]
            re = im = None
            for w in range(win):
                sr = source_ref[0, ft, pl.ds(w * ch + row, 8, stride=0), :]
                si = source_ref[1, ft, pl.ds(w * ch + row, 8, stride=0), :]
                sr = jnp.concatenate([sr] * (ch // 8), axis=0)
                si = jnp.concatenate([si] * (ch // 8), axis=0)
                lr, li = mine[w]
                a = sr * lr + si * li
                b = sr * li - si * lr
                re = a if re is None else re + a
                im = b if im is None else im + b
            out_ref[0, j, :, at] = re.astype(jnp.bfloat16)
            out_ref[1, j, :, at] = im.astype(jnp.bfloat16)
        return 0

    lax.fori_loop(0, tiles, one_tile, 0)


def spread(part, n_chan):
    def swap(x, mask):
        return lax.ppermute(x, "chan", [(i, i ^ mask) for i in range(n_chan)])

    column = jnp.concatenate([part] + [swap(part, m) for m in range(4, n_chan, 4)], axis=0)
    far = swap(column, 2)
    beside = swap(column, 1)
    return (0, 2, 1, 3), (column, far, beside, swap(far, 1))


def body(spectra, filter_bank, band_index, window_mask, owner_order, source_offset):
    n_chan = lax.axis_size("chan")
    me = lax.axis_index("chan").astype(jnp.int32)
    _, win, ch, freq = spectra.shape
    banks, taps = filter_bank.shape[1:]
    rounds = owner_order.shape[0]
    count = win * ch
    tiles = freq // LANES
    pieces = win * tiles
    sources = rounds * ch
    in_parts = n_chan == pieces and n_chan >= 4 and n_chan & (n_chan - 1) == 0
    smem = pl.BlockSpec(memory_space=pltpu.SMEM)
    vmem = pl.BlockSpec(memory_space=pltpu.VMEM)

    split = pl.pallas_call(
        split_kernel,
        out_shape=jax.ShapeDtypeStruct((pieces, 2 * ch + 16, LANES), jnp.bfloat16),
        name="split",
    )(spectra, window_mask)
    if in_parts:
        held = lax.all_to_all(split, "chan", 0, 0)[:, None]
        first = me
    else:
        held = lax.all_gather(split, "chan")
        first = jnp.int32(0)

    ends = n_chan - 1
    before = lax.ppermute(spectra, "chan", [(i, i + 1) for i in range(ends)])
    after = lax.ppermute(spectra, "chan", [(i + 1, i) for i in range(ends)])
    held, before, after = lax.optimization_barrier((held, before, after))

    weights = jax.ShapeDtypeStruct((banks * 2 * ch, 2 * LANES), jnp.bfloat16)
    whi, wlo, band = pl.pallas_call(
        prep_kernel,
        out_shape=(weights, weights, jax.ShapeDtypeStruct((freq, freq), jnp.bfloat16)),
        scratch_shapes=[pltpu.VMEM((2, banks, LANES), jnp.float32)],
        name="prep",
    )(filter_bank)

    count_here = held.shape[1]
    filtered = pl.pallas_call(
        source_kernel,
        grid=(count_here,),
        in_specs=[
            smem,
            smem,
            pl.BlockSpec((n_chan, 1, 2 * ch + 16, LANES), lambda s: (0, s, 0, 0)),
            vmem,
            vmem,
            vmem,
        ],
        out_specs=pl.BlockSpec((1, rounds, 2, ch, LANES), lambda s: (s, 0, 0, 0, 0)),
        out_shape=jax.ShapeDtypeStruct((count_here, rounds, 2, ch, LANES), jnp.bfloat16),
        compiler_params=VMEM,
        name="source_filter",
    )(first[None], owner_order, held, whi, wlo, band_index.reshape(tiles, 1, LANES))
    if in_parts:
        masks, filtered = spread(filtered, n_chan)
        base = me
    else:
        masks, filtered = (0,), (filtered,)
        base = jnp.int32(0)

    local = pl.pallas_call(
        own_kernel,
        out_shape=jax.ShapeDtypeStruct((2, tiles, count, LANES), jnp.float32),
        in_specs=[vmem] * 8,
        out_specs=vmem,
        scratch_shapes=[pltpu.VMEM((2, count, freq), jnp.float32)],
        compiler_params=VMEM,
        cost_estimate=pl.CostEstimate(
            flops=4 * banks * 2 * ch * 2 * LANES * win * freq, bytes_accessed=3 << 20, transcendentals=0
        ),
        name="own_whiten",
    )(before, spectra, after, whi, wlo, band, band_index.reshape(1, freq), window_mask)

    per_round = ch // SRC_STEP
    return pl.pallas_call(
        functools.partial(cross_kernel, masks=masks),
        grid=(sources // SRC_STEP,),
        in_specs=[smem, smem]
        + [
            pl.BlockSpec((f.shape[0], 1, 2, ch, LANES), lambda s: (0, s // per_round, 0, 0, 0))
            for f in filtered
        ]
        + [vmem, vmem],
        out_specs=pl.BlockSpec((2, SRC_STEP, ch, freq), lambda s: (0, s, 0, 0)),
        out_shape=jax.ShapeDtypeStruct((2, sources, ch, freq), jnp.bfloat16),
        scratch_shapes=[
            pltpu.VMEM((pieces, 2, ch, LANES), jnp.bfloat16),
            pltpu.VMEM((2, tiles, count, LANES), jnp.float32),
        ],
        compiler_params=VMEM,
        name="cross",
    )(base[None], source_offset, *filtered, local, band)


def solution(mesh):
    in_specs = (
        P(None, "groups", "chan", None),
        P(),
        P(),
        P("groups", "chan"),
        P("groups"),
        P("groups", None),
    )
    out_specs = P(None, "groups", "chan", None)
    return jax.shard_map(body, mesh=mesh, in_specs=in_specs, out_specs=out_specs, check_vma=False)
```

```python
import functools

import jax
import jax.numpy as jnp
from jax import lax
from jax.experimental import pallas as pl
from jax.experimental.pallas import tpu as pltpu
from jax.sharding import PartitionSpec as P

SMOOTH = 17
LANES = 128
WATER = 0.05
SRC_STEP = 8
VMEM = pltpu.CompilerParams(vmem_limit_bytes=20 * 1024 * 1024)


def split_kernel(spectra_ref, flags_ref, piece_ref):
    _, win, ch, freq = spectra_ref.shape
    tiles = freq // LANES
    extra = piece_ref.shape[1] - 2 * ch
    for w in range(win):
        flags = jnp.broadcast_to(flags_ref[w : w + 1, :], (extra, ch)).astype(jnp.float32)
        for t in range(tiles):
            at = slice(t * LANES, (t + 1) * LANES)
            piece_ref[w * tiles + t, :ch] = spectra_ref[0, w, :, at]
            piece_ref[w * tiles + t, ch : 2 * ch] = spectra_ref[1, w, :, at]
            piece_ref[w * tiles + t, 2 * ch :] = jnp.zeros((extra, LANES), jnp.bfloat16)
            piece_ref[w * tiles + t, 2 * ch :, :ch] = flags.astype(jnp.bfloat16)


def prep_kernel(bank_ref, whi_ref, wlo_ref, band_ref, padded_ref):
    _, banks, taps = bank_ref.shape
    ch = whi_ref.shape[0] // (2 * banks)
    padded_ref[...] = jnp.zeros(padded_ref.shape, jnp.float32)
    padded_ref[:, :, :taps] = bank_ref[...]

    def skewed(row):
        tile = jnp.broadcast_to(row, (ch, LANES))
        return pltpu.roll(tile, 0, 1, stride=1, stride_axis=0)

    for b in range(banks):
        real = skewed(padded_ref[0, b : b + 1, :])
        imag = skewed(padded_ref[1, b : b + 1, :])
        base = b * 2 * ch
        for row, left, right in ((base, real, -imag), (base + ch, imag, real)):
            for col, val in ((0, left), (LANES, right)):
                high = val.astype(jnp.bfloat16)
                low = (val - high.astype(jnp.float32)).astype(jnp.bfloat16)
                whi_ref[row : row + ch, col : col + LANES] = high
                wlo_ref[row : row + ch, col : col + LANES] = low
    rows = lax.broadcasted_iota(jnp.int32, band_ref.shape, 0)
    cols = lax.broadcasted_iota(jnp.int32, band_ref.shape, 1)
    near = jnp.abs(rows - cols) <= SMOOTH // 2
    band_ref[...] = jnp.where(near, 1.0, 0.0).astype(jnp.bfloat16)


def flag_column(row):
    ch = row.shape[1]
    rows = lax.broadcasted_iota(jnp.int32, (ch, ch), 0)
    cols = lax.broadcasted_iota(jnp.int32, (ch, ch), 1)
    return jnp.sum(jnp.where(rows == cols, row.astype(jnp.float32), 0.0), axis=1, keepdims=True)


def filtered_block(x, whi_ref, wlo_ref, index, ch):
    banks = whi_ref.shape[0] // (2 * ch)
    y = jnp.dot(whi_ref[...], x, preferred_element_type=jnp.float32)
    y = y + jnp.dot(wlo_ref[...], x, preferred_element_type=jnp.float32)
    pick = y[: 2 * ch]
    for b in range(1, banks):
        pick = jnp.where(index == b, y[b * 2 * ch : (b + 1) * 2 * ch], pick)
    return pick


def whitened_block(real, imag, band_ref):
    power = real * real + imag * imag
    high = power.astype(jnp.bfloat16)
    low = (power - high.astype(jnp.float32)).astype(jnp.bfloat16)
    total = jnp.dot(high, band_ref[...], preferred_element_type=jnp.float32)
    total = total + jnp.dot(low, band_ref[...], preferred_element_type=jnp.float32)
    scale = lax.rsqrt(total / SMOOTH + WATER)
    real = (real * scale).astype(jnp.bfloat16).astype(jnp.float32)
    imag = (imag * scale).astype(jnp.bfloat16).astype(jnp.float32)
    return real, imag


def source_kernel(piece_id_ref, owner_ref, x_ref, whi_ref, wlo_ref, index_ref, out_ref):
    n_chan = x_ref.shape[0]
    _, rounds, _, ch, _ = out_ref.shape
    tiles = index_ref.shape[0]
    tile = lax.rem(piece_id_ref[0] + pl.program_id(0), tiles)
    zero = jnp.zeros((), jnp.bfloat16)
    gap = jnp.zeros((LANES - 3 * ch, LANES), jnp.bfloat16)
    columns = []
    for r in range(rounds):
        block = owner_ref[r]
        before = jnp.maximum(block - 1, 0)
        after = jnp.minimum(block + 1, n_chan - 1)
        parts = []
        for p in range(2):
            at = slice(p * ch, (p + 1) * ch)
            parts.append(jnp.where(block > 0, x_ref[before, 0, at], zero))
            parts.append(x_ref[block, 0, at])
            parts.append(jnp.where(block < n_chan - 1, x_ref[after, 0, at], zero))
            parts.append(gap)
        columns.append(jnp.concatenate(parts, axis=0))
    x = jnp.concatenate(columns, axis=1)
    index = jnp.concatenate([index_ref[tile]] * rounds, axis=1)
    pick = filtered_block(x, whi_ref, wlo_ref, index, ch)
    for r in range(rounds):
        flags = x_ref[owner_ref[r], 0, 2 * ch :].astype(jnp.float32)[:1, :ch]
        valid = flag_column(flags)
        for p in range(2):
            part = pick[p * ch : (p + 1) * ch, r * LANES : (r + 1) * LANES] * valid
            out_ref[0, r, p] = part.astype(jnp.bfloat16)


def own_kernel(
    prev_ref, cur_ref, next_ref, whi_ref, wlo_ref, band_ref, index_ref, flags_ref, out_ref, filt_ref
):
    _, win, ch, freq = cur_ref.shape
    gap = jnp.zeros((LANES - 3 * ch, freq), jnp.bfloat16)

    def one_window(w, _):
        parts = []
        for p in range(2):
            parts += [prev_ref[p, w], cur_ref[p, w], next_ref[p, w], gap]
        x = jnp.concatenate(parts, axis=0)
        pick = filtered_block(x, whi_ref, wlo_ref, index_ref[...], ch)
        at = pl.ds(pl.multiple_of(w * ch, ch), ch)
        filt_ref[0, at, :] = pick[:ch]
        filt_ref[1, at, :] = pick[ch:]
        return 0

    lax.fori_loop(0, win, one_window, 0)
    valid = jnp.concatenate([flag_column(flags_ref[w : w + 1, :]) for w in range(win)], axis=0)
    real, imag = whitened_block(filt_ref[0] * valid, filt_ref[1] * valid, band_ref)
    for t in range(freq // LANES):
        out_ref[0, t] = real[:, t * LANES : (t + 1) * LANES].astype(jnp.bfloat16)
        out_ref[1, t] = imag[:, t * LANES : (t + 1) * LANES].astype(jnp.bfloat16)


def spread_row(ref, p, ft, row, ch):
    eight = ref[p, ft, pl.ds(row, 8, stride=0), :]
    pair = jnp.concatenate([eight, eight], axis=0).astype(jnp.bfloat16)
    return jnp.concatenate([pair] * (ch // 16), axis=0)


def pairwise(terms):
    while len(terms) > 1:
        half = (len(terms) + 1) // 2
        terms = [terms[i] + terms[i + half] if i + half < len(terms) else terms[i] for i in range(half)]
    return terms[0]


def cross_kernel(me_ref, offset_ref, *refs, masks):
    filt_refs = refs[: len(masks)]
    local_ref, band_ref, out_ref, piece_ref, source_ref = refs[len(masks) :]
    ch = out_ref.shape[2]
    pieces = piece_ref.shape[0]
    tiles = local_ref.shape[1]
    win = pieces // tiles
    per_round = ch // SRC_STEP
    step = pl.program_id(0)
    r = step // per_round
    j0 = lax.rem(step, per_round) * SRC_STEP

    @pl.when(j0 == 0)
    def _():
        stride = pieces // filt_refs[0].shape[0]
        for mask, ref in zip(masks, filt_refs):
            for k in range(ref.shape[0]):
                piece_ref[me_ref[0] ^ (mask ^ (k * stride))] = ref[k, 0]
        parts = []
        for p in range(2):
            rows = [
                jnp.concatenate([piece_ref[w * tiles + t, p] for t in range(tiles)], axis=1)
                for w in range(win)
            ]
            parts.append(jnp.concatenate(rows, axis=0).astype(jnp.float32))
        real, imag = whitened_block(parts[0], parts[1], band_ref)
        for t in range(tiles):
            source_ref[0, t] = real[:, t * LANES : (t + 1) * LANES] / win
            source_ref[1, t] = imag[:, t * LANES : (t + 1) * LANES] / win

    def one_tile(ft, _):
        at = pl.ds(pl.multiple_of(ft * LANES, LANES), LANES)
        mine = [
            (local_ref[0, ft, w * ch : (w + 1) * ch, :], local_ref[1, ft, w * ch : (w + 1) * ch, :])
            for w in range(win)
        ]
        for j in range(SRC_STEP):
            row = offset_ref[r, j0 + j]
            re = []
            im = []
            for w in range(win):
                sr, si = (spread_row(source_ref, p, ft, w * ch + row, ch) for p in range(2))
                lr, li = mine[w]
                re.append(sr * lr + si * li)
                im.append(sr * li - si * lr)
            out_ref[0, j, :, at] = pairwise(re)
            out_ref[1, j, :, at] = pairwise(im)
        return 0

    lax.fori_loop(0, tiles, one_tile, 0)


def spread(part, n_chan):
    def swap(x, mask):
        return lax.ppermute(x, "chan", [(i, i ^ mask) for i in range(n_chan)])

    column = jnp.concatenate([part] + [swap(part, m) for m in range(4, n_chan, 4)], axis=0)
    far = swap(column, 2)
    beside = swap(column, 1)
    return (0, 2, 1, 3), (column, far, beside, swap(far, 1))


def body(spectra, filter_bank, band_index, window_mask, owner_order, source_offset):
    n_chan = lax.axis_size("chan")
    me = lax.axis_index("chan").astype(jnp.int32)
    _, win, ch, freq = spectra.shape
    banks, taps = filter_bank.shape[1:]
    rounds = owner_order.shape[0]
    count = win * ch
    tiles = freq // LANES
    pieces = win * tiles
    sources = rounds * ch
    in_parts = n_chan == pieces and n_chan >= 4 and n_chan & (n_chan - 1) == 0
    smem = pl.BlockSpec(memory_space=pltpu.SMEM)
    vmem = pl.BlockSpec(memory_space=pltpu.VMEM)

    split = pl.pallas_call(
        split_kernel,
        out_shape=jax.ShapeDtypeStruct((pieces, 2 * ch + 16, LANES), jnp.bfloat16),
        name="split",
    )(spectra, window_mask)
    if in_parts:
        held = lax.all_to_all(split, "chan", 0, 0)[:, None]
        first = me
    else:
        held = lax.all_gather(split, "chan")
        first = jnp.int32(0)

    ends = n_chan - 1
    before = lax.ppermute(spectra, "chan", [(i, i + 1) for i in range(ends)])
    after = lax.ppermute(spectra, "chan", [(i + 1, i) for i in range(ends)])

    weights = jax.ShapeDtypeStruct((banks * 2 * ch, 2 * LANES), jnp.bfloat16)
    whi, wlo, band = pl.pallas_call(
        prep_kernel,
        out_shape=(weights, weights, jax.ShapeDtypeStruct((freq, freq), jnp.bfloat16)),
        scratch_shapes=[pltpu.VMEM((2, banks, LANES), jnp.float32)],
        name="prep",
    )(filter_bank)

    local = pl.pallas_call(
        own_kernel,
        out_shape=jax.ShapeDtypeStruct((2, tiles, count, LANES), jnp.bfloat16),
        in_specs=[vmem] * 8,
        out_specs=vmem,
        scratch_shapes=[pltpu.VMEM((2, count, freq), jnp.float32)],
        compiler_params=VMEM,
        cost_estimate=pl.CostEstimate(
            flops=4 * banks * 2 * ch * 2 * LANES * win * freq, bytes_accessed=3 << 20, transcendentals=0
        ),
        name="own_whiten",
    )(before, spectra, after, whi, wlo, band, band_index.reshape(1, freq), window_mask)

    held, local = lax.optimization_barrier((held, local))

    count_here = held.shape[1]
    filtered = pl.pallas_call(
        source_kernel,
        grid=(count_here,),
        in_specs=[
            smem,
            smem,
            pl.BlockSpec((n_chan, 1, 2 * ch + 16, LANES), lambda s: (0, s, 0, 0)),
            vmem,
            vmem,
            vmem,
        ],
        out_specs=pl.BlockSpec((1, rounds, 2, ch, LANES), lambda s: (s, 0, 0, 0, 0)),
        out_shape=jax.ShapeDtypeStruct((count_here, rounds, 2, ch, LANES), jnp.bfloat16),
        compiler_params=VMEM,
        name="source_filter",
    )(first[None], owner_order, held, whi, wlo, band_index.reshape(tiles, 1, LANES))
    if in_parts:
        masks, filtered = spread(filtered, n_chan)
        base = me
    else:
        masks, filtered = (0,), (filtered,)
        base = jnp.int32(0)

    per_round = ch // SRC_STEP
    return pl.pallas_call(
        functools.partial(cross_kernel, masks=masks),
        grid=(sources // SRC_STEP,),
        in_specs=[smem, smem]
        + [
            pl.BlockSpec((f.shape[0], 1, 2, ch, LANES), lambda s: (0, s // per_round, 0, 0, 0))
            for f in filtered
        ]
        + [vmem, vmem],
        out_specs=pl.BlockSpec((2, SRC_STEP, ch, freq), lambda s: (0, s, 0, 0)),
        out_shape=jax.ShapeDtypeStruct((2, sources, ch, freq), jnp.bfloat16),
        scratch_shapes=[
            pltpu.VMEM((pieces, 2, ch, LANES), jnp.bfloat16),
            pltpu.VMEM((2, tiles, count, LANES), jnp.float32),
        ],
        compiler_params=VMEM,
        name="cross",
    )(base[None], source_offset, *filtered, local, band)


def solution(mesh):
    in_specs = (
        P(None, "groups", "chan", None),
        P(),
        P(),
        P("groups", "chan"),
        P("groups"),
        P("groups", None),
    )
    out_specs = P(None, "groups", "chan", None)
    return jax.shard_map(body, mesh=mesh, in_specs=in_specs, out_specs=out_specs, check_vma=False)
```

```python
import functools

import jax
import jax.numpy as jnp
from jax import lax
from jax.experimental import pallas as pl
from jax.experimental.pallas import tpu as pltpu
from jax.sharding import PartitionSpec as P

SMOOTH = 17
LANES = 128
WATER = 0.05
SRC_STEP = 16


def room(mib):
    return pltpu.CompilerParams(vmem_limit_bytes=mib * 1024 * 1024)


def split_kernel(spectra_ref, flags_ref, piece_ref):
    _, win, ch, freq = spectra_ref.shape
    tiles = freq // LANES
    extra = piece_ref.shape[1] - 2 * ch
    for w in range(win):
        flags = jnp.broadcast_to(flags_ref[w : w + 1, :], (extra, ch)).astype(jnp.float32)
        for t in range(tiles):
            at = slice(t * LANES, (t + 1) * LANES)
            piece_ref[w * tiles + t, :ch] = spectra_ref[0, w, :, at]
            piece_ref[w * tiles + t, ch : 2 * ch] = spectra_ref[1, w, :, at]
            piece_ref[w * tiles + t, 2 * ch :] = jnp.zeros((extra, LANES), jnp.bfloat16)
            piece_ref[w * tiles + t, 2 * ch :, :ch] = flags.astype(jnp.bfloat16)


def prep_kernel(bank_ref, bins_ref, flags_ref, weight_ref, band_ref, index_ref, valid_ref, padded_ref):
    _, banks, taps = bank_ref.shape
    half = weight_ref.shape[0] // 2
    ch = half // (2 * banks)
    index_ref[...] = bins_ref[...]
    for w in range(flags_ref.shape[0]):
        column = flag_column(flags_ref[w : w + 1, :])
        valid_ref[w * ch : (w + 1) * ch, :] = jnp.broadcast_to(column, (ch, LANES))
    padded_ref[...] = jnp.zeros(padded_ref.shape, jnp.float32)
    padded_ref[:, :, :taps] = bank_ref[...]

    def skewed(row):
        tile = jnp.broadcast_to(row, (ch, LANES))
        return pltpu.roll(tile, 0, 1, stride=1, stride_axis=0)

    for b in range(banks):
        real = skewed(padded_ref[0, b : b + 1, :])
        imag = skewed(padded_ref[1, b : b + 1, :])
        base = b * 2 * ch
        for row, left, right in ((base, real, -imag), (base + ch, imag, real)):
            for col, val in ((0, left), (LANES, right)):
                high = val.astype(jnp.bfloat16)
                low = (val - high.astype(jnp.float32)).astype(jnp.bfloat16)
                weight_ref[row : row + ch, col : col + LANES] = high
                weight_ref[half + row : half + row + ch, col : col + LANES] = low
    rows = lax.broadcasted_iota(jnp.int32, band_ref.shape, 0)
    cols = lax.broadcasted_iota(jnp.int32, band_ref.shape, 1)
    near = jnp.abs(rows - cols) <= SMOOTH // 2
    band_ref[...] = jnp.where(near, 1.0, 0.0).astype(jnp.bfloat16)


def flag_column(row):
    ch = row.shape[1]
    rows = lax.broadcasted_iota(jnp.int32, (ch, ch), 0)
    cols = lax.broadcasted_iota(jnp.int32, (ch, ch), 1)
    return jnp.sum(jnp.where(rows == cols, row.astype(jnp.float32), 0.0), axis=1, keepdims=True)


def filtered_block(x, weight_ref, index, ch):
    half = weight_ref.shape[0] // 2
    y = jnp.dot(weight_ref[...], x, preferred_element_type=jnp.float32)
    rows = 2 * ch
    pick = y[:rows] + y[half : half + rows]
    for at in range(rows, half, rows):
        here = y[at : at + rows] + y[half + at : half + at + rows]
        pick = jnp.where(index == at // rows, here, pick)
    return pick


def running_scale(real, imag, band_ref):
    count = real.shape[0]
    power = real * real + imag * imag
    high = power.astype(jnp.bfloat16)
    low = (power - high.astype(jnp.float32)).astype(jnp.bfloat16)
    both = jnp.concatenate([high, low], axis=0)
    total = jnp.dot(both, band_ref[...], preferred_element_type=jnp.float32)
    return lax.rsqrt((total[:count] + total[count:]) * (1.0 / SMOOTH) + WATER)


def source_kernel(params_ref, x_ref, weight_ref, index_ref, out_ref):
    n_chan = x_ref.shape[0]
    _, rounds, _, ch, _ = out_ref.shape
    tiles = index_ref.shape[0]
    tile = lax.rem(params_ref[0] + pl.program_id(0), tiles)
    zero = jnp.zeros((), jnp.bfloat16)
    gap = jnp.zeros((LANES - 3 * ch, LANES), jnp.bfloat16)
    columns = []
    for r in range(rounds):
        block = params_ref[1 + r]
        before = jnp.maximum(block - 1, 0)
        after = jnp.minimum(block + 1, n_chan - 1)
        parts = []
        for p in range(2):
            at = slice(p * ch, (p + 1) * ch)
            parts.append(jnp.where(block > 0, x_ref[before, 0, at], zero))
            parts.append(x_ref[block, 0, at])
            parts.append(jnp.where(block < n_chan - 1, x_ref[after, 0, at], zero))
            parts.append(gap)
        columns.append(jnp.concatenate(parts, axis=0))
    x = jnp.concatenate(columns, axis=1)
    index = jnp.concatenate([index_ref[tile]] * rounds, axis=1)
    pick = filtered_block(x, weight_ref, index, ch)
    for r in range(rounds):
        flags = x_ref[params_ref[1 + r], 0, 2 * ch :].astype(jnp.float32)[:1, :ch]
        valid = flag_column(flags)
        for p in range(2):
            part = pick[p * ch : (p + 1) * ch, r * LANES : (r + 1) * LANES] * valid
            out_ref[0, r, p] = part.astype(jnp.bfloat16)


def own_kernel(prev_ref, cur_ref, next_ref, weight_ref, band_ref, index_ref, valid_ref, out_ref, filt_ref):
    _, win, ch, freq = cur_ref.shape
    tiles = freq // LANES
    gap = jnp.zeros((LANES - 3 * ch, freq), jnp.bfloat16)
    index = jnp.concatenate([index_ref[t] for t in range(tiles)], axis=1)

    def one_window(w, _):
        parts = []
        for p in range(2):
            parts += [prev_ref[p, w], cur_ref[p, w], next_ref[p, w], gap]
        x = jnp.concatenate(parts, axis=0)
        pick = filtered_block(x, weight_ref, index, ch)
        at = pl.ds(pl.multiple_of(w * ch, ch), ch)
        filt_ref[0, at, :] = pick[:ch]
        filt_ref[1, at, :] = pick[ch:]
        return 0

    lax.fori_loop(0, win, one_window, 0)
    valid = jnp.concatenate([valid_ref[...]] * tiles, axis=1)
    scale = running_scale(filt_ref[0], filt_ref[1], band_ref) * valid
    for p in range(2):
        white = (filt_ref[p] * scale).astype(jnp.bfloat16)
        for t in range(tiles):
            out_ref[p, t] = white[:, t * LANES : (t + 1) * LANES]


def spread_row(ref, r, p, ft, row, ch):
    eight = ref[r, p, ft, pl.ds(row, 8, stride=0), :]
    pair = jnp.concatenate([eight, eight], axis=0).astype(jnp.bfloat16)
    return jnp.concatenate([pair] * (ch // 16), axis=0)


def pairwise(terms):
    while len(terms) > 1:
        half = (len(terms) + 1) // 2
        terms = [terms[i] + terms[i + half] if i + half < len(terms) else terms[i] for i in range(half)]
    return terms[0]


def cross_kernel(params_ref, *refs, masks):
    filt_refs = refs[: len(masks)]
    local_ref, band_ref, out_ref, piece_ref, source_ref = refs[len(masks) :]
    ch = out_ref.shape[2]
    pieces, rounds = piece_ref.shape[:2]
    tiles = local_ref.shape[1]
    win = pieces // tiles
    per_round = ch // SRC_STEP
    step = pl.program_id(0)
    r = step // per_round
    first = 1 + rounds + step * SRC_STEP

    @pl.when(step == 0)
    def _():
        stride = pieces // filt_refs[0].shape[0]
        for mask, ref in zip(masks, filt_refs):
            for k in range(ref.shape[0]):
                piece_ref[params_ref[0] ^ (mask ^ (k * stride))] = ref[k]

        def one_round(rr, _):
            parts = []
            for p in range(2):
                rows = [
                    jnp.concatenate([piece_ref[w * tiles + t, rr, p] for t in range(tiles)], axis=1)
                    for w in range(win)
                ]
                parts.append(jnp.concatenate(rows, axis=0).astype(jnp.float32))
            scale = running_scale(parts[0], parts[1], band_ref)
            for p in range(2):
                white = (parts[p] * scale).astype(jnp.bfloat16).astype(jnp.float32) * (1.0 / win)
                for t in range(tiles):
                    source_ref[rr, p, t] = white[:, t * LANES : (t + 1) * LANES]
            return 0

        lax.fori_loop(0, rounds, one_round, 0)

    def one_tile(ft, _):
        at = pl.ds(pl.multiple_of(ft * LANES, LANES), LANES)
        mine = [
            (local_ref[0, ft, w * ch : (w + 1) * ch, :], local_ref[1, ft, w * ch : (w + 1) * ch, :])
            for w in range(win)
        ]
        for j in range(SRC_STEP):
            row = params_ref[first + j]
            re = []
            im = []
            for w in range(win):
                sr, si = (spread_row(source_ref, r, p, ft, w * ch + row, ch) for p in range(2))
                lr, li = mine[w]
                re.append(sr * lr + si * li)
                im.append(sr * li - si * lr)
            out_ref[0, j, :, at] = pairwise(re)
            out_ref[1, j, :, at] = pairwise(im)
        return 0

    lax.fori_loop(0, tiles, one_tile, 0)


def swap(x, mask, n_chan):
    return lax.ppermute(x, "chan", [(i, i ^ mask) for i in range(n_chan)])


def body(spectra, filter_bank, band_index, window_mask, owner_order, source_offset):
    n_chan = lax.axis_size("chan")
    me = lax.axis_index("chan").astype(jnp.int32)
    _, win, ch, freq = spectra.shape
    banks, taps = filter_bank.shape[1:]
    rounds = owner_order.shape[0]
    count = win * ch
    tiles = freq // LANES
    pieces = win * tiles
    sources = rounds * ch
    in_parts = n_chan == pieces and n_chan >= 4 and n_chan & (n_chan - 1) == 0
    smem = pl.BlockSpec(memory_space=pltpu.SMEM)
    vmem = pl.BlockSpec(memory_space=pltpu.VMEM)

    split = pl.pallas_call(
        split_kernel,
        out_shape=jax.ShapeDtypeStruct((pieces, 2 * ch + 16, LANES), jnp.bfloat16),
        compiler_params=room(6),
        name="split",
    )(spectra, window_mask)
    if in_parts:
        held = lax.all_to_all(split, "chan", 0, 0)[:, None]
        first = me
    else:
        held = lax.all_gather(split, "chan")
        first = jnp.int32(0)
    params = jnp.concatenate([first[None], owner_order, source_offset.reshape(-1)])

    weight, band, index, valid = pl.pallas_call(
        prep_kernel,
        out_shape=(
            jax.ShapeDtypeStruct((2 * banks * 2 * ch, 2 * LANES), jnp.bfloat16),
            jax.ShapeDtypeStruct((freq, freq), jnp.bfloat16),
            jax.ShapeDtypeStruct((tiles, 1, LANES), jnp.int32),
            jax.ShapeDtypeStruct((count, LANES), jnp.float32),
        ),
        scratch_shapes=[pltpu.VMEM((2, banks, LANES), jnp.float32)],
        compiler_params=room(8),
        name="prep",
    )(filter_bank, band_index.reshape(tiles, 1, LANES), window_mask)

    count_here = held.shape[1]
    filtered = pl.pallas_call(
        source_kernel,
        grid=(count_here,),
        in_specs=[
            smem,
            pl.BlockSpec((n_chan, 1, 2 * ch + 16, LANES), lambda s: (0, s, 0, 0)),
            vmem,
            vmem,
        ],
        out_specs=pl.BlockSpec((1, rounds, 2, ch, LANES), lambda s: (s, 0, 0, 0, 0)),
        out_shape=jax.ShapeDtypeStruct((count_here, rounds, 2, ch, LANES), jnp.bfloat16),
        compiler_params=room(16),
        name="source_filter",
    )(params, held, weight, index)

    spectra, filtered = lax.optimization_barrier((spectra, filtered))
    if in_parts:
        masks = (0, 2, 1, 3)
        column = [filtered] + [swap(filtered, m, n_chan) for m in range(4, n_chan, 4)]
    ends = n_chan - 1
    before = lax.ppermute(spectra, "chan", [(i, i + 1) for i in range(ends)])
    after = lax.ppermute(spectra, "chan", [(i + 1, i) for i in range(ends)])

    local = pl.pallas_call(
        own_kernel,
        out_shape=jax.ShapeDtypeStruct((2, tiles, count, LANES), jnp.bfloat16),
        in_specs=[vmem] * 7,
        out_specs=vmem,
        scratch_shapes=[pltpu.VMEM((2, count, freq), jnp.float32)],
        compiler_params=room(16),
        cost_estimate=pl.CostEstimate(
            flops=4 * banks * 2 * ch * 2 * LANES * win * freq, bytes_accessed=3 << 20, transcendentals=0
        ),
        name="own_whiten",
    )(before, spectra, after, weight, band, index, valid)

    if in_parts:
        column = jnp.concatenate(column, axis=0)
        far = swap(column, 2, n_chan)
        beside = swap(column, 1, n_chan)
        far, local = lax.optimization_barrier((far, local))
        parts = (column, far, beside, swap(far, 1, n_chan))
    else:
        masks = (0,)
        parts = (filtered,)

    return pl.pallas_call(
        functools.partial(cross_kernel, masks=masks),
        grid=(sources // SRC_STEP,),
        in_specs=[smem] + [vmem] * (len(parts) + 2),
        out_specs=pl.BlockSpec((2, SRC_STEP, ch, freq), lambda s: (0, s, 0, 0)),
        out_shape=jax.ShapeDtypeStruct((2, sources, ch, freq), jnp.bfloat16),
        scratch_shapes=[
            pltpu.VMEM((pieces, rounds, 2, ch, LANES), jnp.bfloat16),
            pltpu.VMEM((rounds, 2, tiles, count, LANES), jnp.float32),
        ],
        compiler_params=room(24),
        name="cross",
    )(params, *parts, local, band)


def solution(mesh):
    in_specs = (
        P(None, "groups", "chan", None),
        P(),
        P(),
        P("groups", "chan"),
        P("groups"),
        P("groups", None),
    )
    out_specs = P(None, "groups", "chan", None)
    return jax.shard_map(body, mesh=mesh, in_specs=in_specs, out_specs=out_specs, check_vma=False)
```

```python
import functools

import jax
import jax.numpy as jnp
from jax import lax
from jax.experimental import pallas as pl
from jax.experimental.pallas import tpu as pltpu
from jax.sharding import PartitionSpec as P

SMOOTH = 17
LANES = 128
WATER = 0.05
SRC_STEP = 16


def room(mib):
    return pltpu.CompilerParams(vmem_limit_bytes=mib * 1024 * 1024)


def split_kernel(spectra_ref, flags_ref, piece_ref):
    _, win, ch, freq = spectra_ref.shape
    tiles = freq // LANES
    extra = piece_ref.shape[1] - 2 * ch
    for w in range(win):
        flags = jnp.broadcast_to(flags_ref[w : w + 1, :], (extra, ch)).astype(jnp.float32)
        for t in range(tiles):
            at = slice(t * LANES, (t + 1) * LANES)
            piece_ref[t * win + w, :ch] = spectra_ref[0, w, :, at]
            piece_ref[t * win + w, ch : 2 * ch] = spectra_ref[1, w, :, at]
            piece_ref[t * win + w, 2 * ch :] = jnp.zeros((extra, LANES), jnp.bfloat16)
            piece_ref[t * win + w, 2 * ch :, :ch] = flags.astype(jnp.bfloat16)


def prep_kernel(bank_ref, bins_ref, flags_ref, weight_ref, band_ref, index_ref, valid_ref, padded_ref):
    _, banks, taps = bank_ref.shape
    half = weight_ref.shape[0] // 2
    ch = half // (2 * banks)
    index_ref[...] = bins_ref[...]
    for w in range(flags_ref.shape[0]):
        column = flag_column(flags_ref[w : w + 1, :])
        valid_ref[w * ch : (w + 1) * ch, :] = jnp.broadcast_to(column, (ch, LANES))
    padded_ref[...] = jnp.zeros(padded_ref.shape, jnp.float32)
    padded_ref[:, :, :taps] = bank_ref[...]

    def skewed(row):
        tile = jnp.broadcast_to(row, (ch, LANES))
        return pltpu.roll(tile, 0, 1, stride=1, stride_axis=0)

    for b in range(banks):
        real = skewed(padded_ref[0, b : b + 1, :])
        imag = skewed(padded_ref[1, b : b + 1, :])
        base = b * 2 * ch
        for row, left, right in ((base, real, -imag), (base + ch, imag, real)):
            for col, val in ((0, left), (LANES, right)):
                high = val.astype(jnp.bfloat16)
                low = (val - high.astype(jnp.float32)).astype(jnp.bfloat16)
                weight_ref[row : row + ch, col : col + LANES] = high
                weight_ref[half + row : half + row + ch, col : col + LANES] = low
    rows = lax.broadcasted_iota(jnp.int32, band_ref.shape, 0)
    cols = lax.broadcasted_iota(jnp.int32, band_ref.shape, 1)
    near = jnp.abs(rows - cols) <= SMOOTH // 2
    band_ref[...] = jnp.where(near, 1.0, 0.0).astype(jnp.bfloat16)


def flag_column(row):
    ch = row.shape[1]
    rows = lax.broadcasted_iota(jnp.int32, (ch, ch), 0)
    cols = lax.broadcasted_iota(jnp.int32, (ch, ch), 1)
    return jnp.sum(jnp.where(rows == cols, row.astype(jnp.float32), 0.0), axis=1, keepdims=True)


def filtered_block(x, weight_ref, index, ch):
    half = weight_ref.shape[0] // 2
    y = jnp.dot(weight_ref[...], x, preferred_element_type=jnp.float32)
    rows = 2 * ch
    pick = y[:rows] + y[half : half + rows]
    for at in range(rows, half, rows):
        here = y[at : at + rows] + y[half + at : half + at + rows]
        pick = jnp.where(index == at // rows, here, pick)
    return pick


def running_scale(real, imag, band_ref):
    count = real.shape[0]
    power = real * real + imag * imag
    high = power.astype(jnp.bfloat16)
    low = (power - high.astype(jnp.float32)).astype(jnp.bfloat16)
    both = jnp.concatenate([high, low], axis=0)
    total = jnp.dot(both, band_ref[...], preferred_element_type=jnp.float32)
    return lax.rsqrt((total[:count] + total[count:]) * (1.0 / SMOOTH) + WATER)


def source_kernel(params_ref, x_ref, weight_ref, index_ref, out_ref, *, win):
    n_chan = x_ref.shape[0]
    _, rounds, _, ch, _ = out_ref.shape
    tile = lax.div(params_ref[0] + pl.program_id(0), win)
    zero = jnp.zeros((), jnp.bfloat16)
    gap = jnp.zeros((LANES - 3 * ch, LANES), jnp.bfloat16)
    columns = []
    for r in range(rounds):
        block = params_ref[2 + r]
        before = jnp.maximum(block - 1, 0)
        after = jnp.minimum(block + 1, n_chan - 1)
        parts = []
        for p in range(2):
            at = slice(p * ch, (p + 1) * ch)
            parts.append(jnp.where(block > 0, x_ref[before, 0, at], zero))
            parts.append(x_ref[block, 0, at])
            parts.append(jnp.where(block < n_chan - 1, x_ref[after, 0, at], zero))
            parts.append(gap)
        columns.append(jnp.concatenate(parts, axis=0))
    x = jnp.concatenate(columns, axis=1)
    index = jnp.concatenate([index_ref[tile]] * rounds, axis=1)
    pick = filtered_block(x, weight_ref, index, ch)
    for r in range(rounds):
        flags = x_ref[params_ref[2 + r], 0, 2 * ch :].astype(jnp.float32)[:1, :ch]
        valid = flag_column(flags)
        for p in range(2):
            part = pick[p * ch : (p + 1) * ch, r * LANES : (r + 1) * LANES] * valid
            out_ref[0, r, p] = part.astype(jnp.bfloat16)


def own_kernel(prev_ref, cur_ref, next_ref, weight_ref, band_ref, index_ref, valid_ref, out_ref, filt_ref):
    _, win, ch, freq = cur_ref.shape
    tiles = freq // LANES
    gap = jnp.zeros((LANES - 3 * ch, freq), jnp.bfloat16)
    index = jnp.concatenate([index_ref[t] for t in range(tiles)], axis=1)

    def one_window(w, _):
        parts = []
        for p in range(2):
            parts += [prev_ref[p, w], cur_ref[p, w], next_ref[p, w], gap]
        x = jnp.concatenate(parts, axis=0)
        pick = filtered_block(x, weight_ref, index, ch)
        at = pl.ds(pl.multiple_of(w * ch, ch), ch)
        filt_ref[0, at, :] = pick[:ch]
        filt_ref[1, at, :] = pick[ch:]
        return 0

    lax.fori_loop(0, win, one_window, 0)
    valid = jnp.concatenate([valid_ref[...]] * tiles, axis=1)
    scale = running_scale(filt_ref[0], filt_ref[1], band_ref) * valid
    for p in range(2):
        white = (filt_ref[p] * scale).astype(jnp.bfloat16)
        for t in range(tiles):
            for w in range(win):
                out_ref[p, t, w] = white[w * ch : (w + 1) * ch, t * LANES : (t + 1) * LANES]


def column_kernel(params_ref, *refs):
    band_ref, out_ref, piece_ref = refs[-3:]
    parts = refs[:-3]
    tiles, rounds, _, ch, _ = piece_ref.shape
    if len(parts) == tiles:
        place = params_ref[1]
        for k, ref in enumerate(parts):
            piece_ref[place ^ k] = ref[0]
    else:
        piece_ref[...] = parts[0][:, 0]
    both = []
    for p in range(2):
        rows = [
            jnp.concatenate([piece_ref[t, r, p] for t in range(tiles)], axis=1) for r in range(rounds)
        ]
        both.append(jnp.concatenate(rows, axis=0).astype(jnp.float32))
    scale = running_scale(both[0], both[1], band_ref)
    for p in range(2):
        white = (both[p] * scale).astype(jnp.bfloat16)
        for t in range(tiles):
            for r in range(rounds):
                out_ref[0, t, r, p] = white[r * ch : (r + 1) * ch, t * LANES : (t + 1) * LANES]


def spread_row(ref, at, row, ch):
    eight = ref[(*at, pl.ds(row, 8, stride=0), slice(None))]
    pair = jnp.concatenate([eight, eight], axis=0).astype(jnp.bfloat16)
    return jnp.concatenate([pair] * (ch // 16), axis=0)


def pairwise(terms):
    while len(terms) > 1:
        half = (len(terms) + 1) // 2
        terms = [terms[i] + terms[i + half] if i + half < len(terms) else terms[i] for i in range(half)]
    return terms[0]


def cross_kernel(params_ref, *refs, masks, added):
    column_refs = refs[: len(masks)]
    local_ref, out_ref, source_ref = refs[len(masks)], refs[-2], refs[-1]
    ch = out_ref.shape[2]
    tiles, win = local_ref.shape[1:3]
    rounds = source_ref.shape[2]
    per_round = ch // SRC_STEP
    step = pl.program_id(0)
    r = step // per_round
    first = 2 + rounds + step * SRC_STEP
    here = lax.rem(params_ref[0], win)

    @pl.when(step == 0)
    def _():
        for i, ref in enumerate(column_refs):
            for t in range(tiles):
                source_ref[i, t] = ref[0, t].astype(jnp.float32) * (1.0 / win)

    def one_tile(ft, _):
        at = pl.ds(pl.multiple_of(ft * LANES, LANES), LANES)
        mine = [(local_ref[0, ft, here ^ mask], local_ref[1, ft, here ^ mask]) for mask in masks]
        for j in range(SRC_STEP):
            row = params_ref[first + j]
            re = []
            im = []
            for i in range(len(masks)):
                sr, si = (spread_row(source_ref, (i, ft, r, p), row, ch) for p in range(2))
                lr, li = mine[i]
                re.append(sr * lr + si * li)
                im.append(sr * li - si * lr)
            re = pairwise(re)
            im = pairwise(im)
            if added:
                re = re + refs[-3][0, j, :, at]
                im = im + refs[-3][1, j, :, at]
            out_ref[0, j, :, at] = re
            out_ref[1, j, :, at] = im
        return 0

    lax.fori_loop(0, tiles, one_tile, 0)


def swap(x, mask, n_chan):
    return lax.ppermute(x, "chan", [(i, i ^ mask) for i in range(n_chan)])


def body(spectra, filter_bank, band_index, window_mask, owner_order, source_offset):
    n_chan = lax.axis_size("chan")
    me = lax.axis_index("chan").astype(jnp.int32)
    _, win, ch, freq = spectra.shape
    banks, taps = filter_bank.shape[1:]
    rounds = owner_order.shape[0]
    count = win * ch
    tiles = freq // LANES
    pieces = win * tiles
    sources = rounds * ch
    in_parts = n_chan == pieces and win == 4 and tiles & (tiles - 1) == 0
    smem = pl.BlockSpec(memory_space=pltpu.SMEM)
    vmem = pl.BlockSpec(memory_space=pltpu.VMEM)

    split = pl.pallas_call(
        split_kernel,
        out_shape=jax.ShapeDtypeStruct((pieces, 2 * ch + 16, LANES), jnp.bfloat16),
        compiler_params=room(56),
        name="split",
    )(spectra, window_mask)
    if in_parts:
        held = lax.all_to_all(split, "chan", 0, 0)[:, None]
        first = me
    else:
        held = lax.all_gather(split, "chan")
        first = jnp.int32(0)
    params = jnp.concatenate([first[None], lax.div(first, jnp.int32(win))[None], owner_order, source_offset.reshape(-1)])

    ends = n_chan - 1
    before = lax.ppermute(spectra, "chan", [(i, i + 1) for i in range(ends)])
    after = lax.ppermute(spectra, "chan", [(i + 1, i) for i in range(ends)])
    held, before, after = lax.optimization_barrier((held, before, after))

    weight, band, index, valid = pl.pallas_call(
        prep_kernel,
        out_shape=(
            jax.ShapeDtypeStruct((2 * banks * 2 * ch, 2 * LANES), jnp.bfloat16),
            jax.ShapeDtypeStruct((freq, freq), jnp.bfloat16),
            jax.ShapeDtypeStruct((tiles, 1, LANES), jnp.int32),
            jax.ShapeDtypeStruct((count, LANES), jnp.float32),
        ),
        scratch_shapes=[pltpu.VMEM((2, banks, LANES), jnp.float32)],
        compiler_params=room(8),
        name="prep",
    )(filter_bank, band_index.reshape(tiles, 1, LANES), window_mask)

    count_here = held.shape[1]
    filtered = pl.pallas_call(
        functools.partial(source_kernel, win=win),
        grid=(count_here,),
        in_specs=[
            smem,
            pl.BlockSpec((n_chan, 1, 2 * ch + 16, LANES), lambda s: (0, s, 0, 0)),
            vmem,
            vmem,
        ],
        out_specs=pl.BlockSpec((1, rounds, 2, ch, LANES), lambda s: (s, 0, 0, 0, 0)),
        out_shape=jax.ShapeDtypeStruct((count_here, rounds, 2, ch, LANES), jnp.bfloat16),
        compiler_params=room(16),
        name="source_filter",
    )(params, held, weight, index)

    if in_parts:
        zparts = [filtered] + [swap(filtered, win * k, n_chan) for k in range(1, tiles)]

    local = pl.pallas_call(
        own_kernel,
        out_shape=jax.ShapeDtypeStruct((2, tiles, win, ch, LANES), jnp.bfloat16),
        in_specs=[vmem] * 7,
        out_specs=vmem,
        scratch_shapes=[pltpu.VMEM((2, count, freq), jnp.float32)],
        compiler_params=room(16),
        cost_estimate=pl.CostEstimate(
            flops=4 * banks * 2 * ch * 2 * LANES * win * freq, bytes_accessed=3 << 20, transcendentals=0
        ),
        name="own_whiten",
    )(before, spectra, after, weight, band, index, valid)

    shape = (tiles, rounds, 2, ch, LANES)
    if in_parts:
        zparts[-1], local = lax.optimization_barrier((zparts[-1], local))
        windows = 1
        specs = [vmem] * tiles
    else:
        windows = win
        zparts = [filtered.reshape((tiles, win) + shape[1:])]
        specs = [pl.BlockSpec((tiles, 1) + shape[1:], lambda s: (0, s, 0, 0, 0, 0))]
    column = pl.pallas_call(
        column_kernel,
        grid=(windows,),
        in_specs=[smem] + specs + [vmem],
        out_specs=pl.BlockSpec((1,) + shape, lambda s: (s, 0, 0, 0, 0, 0)),
        out_shape=jax.ShapeDtypeStruct((windows,) + shape, jnp.bfloat16),
        scratch_shapes=[pltpu.VMEM(shape, jnp.bfloat16)],
        compiler_params=room(16),
        name="column_whiten",
    )(params, *zparts, band)

    def cross(masks, columns, earlier):
        block = pl.BlockSpec((2, SRC_STEP, ch, freq), lambda s: (0, s, 0, 0))
        return pl.pallas_call(
            functools.partial(cross_kernel, masks=masks, added=len(earlier) > 0),
            grid=(sources // SRC_STEP,),
            in_specs=[smem] + [vmem] * (len(columns) + 1) + [block] * len(earlier),
            out_specs=block,
            out_shape=jax.ShapeDtypeStruct((2, sources, ch, freq), jnp.bfloat16),
            scratch_shapes=[pltpu.VMEM((len(masks),) + shape, jnp.float32)],
            compiler_params=room(24),
            cost_estimate=pl.CostEstimate(
                flops=16 * len(masks) * sources * ch * freq, bytes_accessed=16 << 20, transcendentals=0
            ),
            name="cross",
        )(params, *columns, local, *earlier)

    if not in_parts:
        return cross(tuple(range(win)), [column[w : w + 1] for w in range(win)], [])
    far = swap(column, 2, n_chan)
    beside = swap(column, 1, n_chan)
    partial = cross((0, 1), [column, beside], [])
    far, partial = lax.optimization_barrier((far, partial))
    return cross((2, 3), [far, swap(far, 1, n_chan)], [partial])


def solution(mesh):
    in_specs = (
        P(None, "groups", "chan", None),
        P(),
        P(),
        P("groups", "chan"),
        P("groups"),
        P("groups", None),
    )
    out_specs = P(None, "groups", "chan", None)
    return jax.shard_map(body, mesh=mesh, in_specs=in_specs, out_specs=out_specs, check_vma=False)
```

```python
import functools

import jax
import jax.numpy as jnp
from jax import lax
from jax.experimental import pallas as pl
from jax.experimental.pallas import tpu as pltpu
from jax.sharding import PartitionSpec as P

SMOOTH = 17
LANES = 128
WATER = 0.05
SRC_STEP = 16


def room(mib):
    return pltpu.CompilerParams(vmem_limit_bytes=mib * 1024 * 1024)


def split_kernel(spectra_ref, flags_ref, piece_ref):
    _, win, ch, freq = spectra_ref.shape
    tiles = freq // LANES
    extra = piece_ref.shape[1] - 2 * ch
    for w in range(win):
        flags = jnp.broadcast_to(flags_ref[w : w + 1, :], (extra, ch)).astype(jnp.float32)
        for t in range(tiles):
            at = slice(t * LANES, (t + 1) * LANES)
            piece_ref[t * win + w, :ch] = spectra_ref[0, w, :, at]
            piece_ref[t * win + w, ch : 2 * ch] = spectra_ref[1, w, :, at]
            piece_ref[t * win + w, 2 * ch :] = jnp.zeros((extra, LANES), jnp.bfloat16)
            piece_ref[t * win + w, 2 * ch :, :ch] = flags.astype(jnp.bfloat16)


def prep_kernel(bank_ref, bins_ref, flags_ref, weight_ref, band_ref, index_ref, valid_ref, padded_ref):
    _, banks, taps = bank_ref.shape
    half = weight_ref.shape[0] // 2
    ch = half // (2 * banks)
    index_ref[...] = bins_ref[...]
    for w in range(flags_ref.shape[0]):
        column = flag_column(flags_ref[w : w + 1, :])
        valid_ref[w * ch : (w + 1) * ch, :] = jnp.broadcast_to(column, (ch, LANES))
    padded_ref[...] = jnp.zeros(padded_ref.shape, jnp.float32)
    padded_ref[:, :, :taps] = bank_ref[...]

    def skewed(row):
        tile = jnp.broadcast_to(row, (ch, LANES))
        return pltpu.roll(tile, 0, 1, stride=1, stride_axis=0)

    for b in range(banks):
        real = skewed(padded_ref[0, b : b + 1, :])
        imag = skewed(padded_ref[1, b : b + 1, :])
        base = b * 2 * ch
        for row, left, right in ((base, real, -imag), (base + ch, imag, real)):
            for col, val in ((0, left), (LANES, right)):
                high = val.astype(jnp.bfloat16)
                low = (val - high.astype(jnp.float32)).astype(jnp.bfloat16)
                weight_ref[row : row + ch, col : col + LANES] = high
                weight_ref[half + row : half + row + ch, col : col + LANES] = low
    rows = lax.broadcasted_iota(jnp.int32, band_ref.shape, 0)
    cols = lax.broadcasted_iota(jnp.int32, band_ref.shape, 1)
    near = jnp.abs(rows - cols) <= SMOOTH // 2
    band_ref[...] = jnp.where(near, 1.0, 0.0).astype(jnp.bfloat16)


def flag_column(row):
    ch = row.shape[1]
    rows = lax.broadcasted_iota(jnp.int32, (ch, ch), 0)
    cols = lax.broadcasted_iota(jnp.int32, (ch, ch), 1)
    return jnp.sum(jnp.where(rows == cols, row.astype(jnp.float32), 0.0), axis=1, keepdims=True)


def filtered_block(x, weight_ref, index, ch):
    half = weight_ref.shape[0] // 2
    y = jnp.dot(weight_ref[...], x, preferred_element_type=jnp.float32)
    rows = 2 * ch
    pick = y[:rows] + y[half : half + rows]
    for at in range(rows, half, rows):
        here = y[at : at + rows] + y[half + at : half + at + rows]
        pick = jnp.where(index == at // rows, here, pick)
    return pick


def running_scale(real, imag, band_ref):
    count = real.shape[0]
    power = real * real + imag * imag
    high = power.astype(jnp.bfloat16)
    low = (power - high.astype(jnp.float32)).astype(jnp.bfloat16)
    both = jnp.concatenate([high, low], axis=0)
    total = jnp.dot(both, band_ref[...], preferred_element_type=jnp.float32)
    return lax.rsqrt((total[:count] + total[count:]) * (1.0 / SMOOTH) + WATER)


def source_kernel(params_ref, x_ref, weight_ref, index_ref, out_ref, *, win):
    n_chan = x_ref.shape[0]
    _, rounds, _, ch, _ = out_ref.shape
    tile = lax.div(params_ref[0] + pl.program_id(0), win)
    zero = jnp.zeros((), jnp.bfloat16)
    gap = jnp.zeros((LANES - 3 * ch, LANES), jnp.bfloat16)
    columns = []
    for r in range(rounds):
        block = params_ref[2 + r]
        before = jnp.maximum(block - 1, 0)
        after = jnp.minimum(block + 1, n_chan - 1)
        parts = []
        for p in range(2):
            at = slice(p * ch, (p + 1) * ch)
            parts.append(jnp.where(block > 0, x_ref[before, 0, at], zero))
            parts.append(x_ref[block, 0, at])
            parts.append(jnp.where(block < n_chan - 1, x_ref[after, 0, at], zero))
            parts.append(gap)
        columns.append(jnp.concatenate(parts, axis=0))
    x = jnp.concatenate(columns, axis=1)
    index = jnp.concatenate([index_ref[tile]] * rounds, axis=1)
    pick = filtered_block(x, weight_ref, index, ch)
    for r in range(rounds):
        flags = x_ref[params_ref[2 + r], 0, 2 * ch :].astype(jnp.float32)[:1, :ch]
        valid = flag_column(flags)
        for p in range(2):
            part = pick[p * ch : (p + 1) * ch, r * LANES : (r + 1) * LANES] * valid
            out_ref[0, r, p] = part.astype(jnp.bfloat16)


def own_kernel(prev_ref, cur_ref, next_ref, weight_ref, band_ref, index_ref, valid_ref, out_ref, filt_ref):
    _, win, ch, freq = cur_ref.shape
    tiles = freq // LANES
    gap = jnp.zeros((LANES - 3 * ch, freq), jnp.bfloat16)
    index = jnp.concatenate([index_ref[t] for t in range(tiles)], axis=1)

    def one_window(w, _):
        parts = []
        for p in range(2):
            parts += [prev_ref[p, w], cur_ref[p, w], next_ref[p, w], gap]
        x = jnp.concatenate(parts, axis=0)
        pick = filtered_block(x, weight_ref, index, ch)
        at = pl.ds(pl.multiple_of(w * ch, ch), ch)
        filt_ref[0, at, :] = pick[:ch]
        filt_ref[1, at, :] = pick[ch:]
        return 0

    lax.fori_loop(0, win, one_window, 0)
    valid = jnp.concatenate([valid_ref[...]] * tiles, axis=1)
    scale = running_scale(filt_ref[0], filt_ref[1], band_ref) * valid
    for p in range(2):
        white = (filt_ref[p] * scale).astype(jnp.bfloat16)
        for t in range(tiles):
            for w in range(win):
                out_ref[p, t, w] = white[w * ch : (w + 1) * ch, t * LANES : (t + 1) * LANES]


def column_kernel(params_ref, *refs):
    band_ref, out_ref, piece_ref = refs[-3:]
    parts = refs[:-3]
    tiles, rounds, _, ch, _ = piece_ref.shape
    if len(parts) == tiles:
        place = params_ref[1]
        for k, ref in enumerate(parts):
            piece_ref[place ^ k] = ref[0]
    else:
        piece_ref[...] = parts[0][:, 0]
    both = []
    for p in range(2):
        rows = [
            jnp.concatenate([piece_ref[t, r, p] for t in range(tiles)], axis=1) for r in range(rounds)
        ]
        both.append(jnp.concatenate(rows, axis=0).astype(jnp.float32))
    scale = running_scale(both[0], both[1], band_ref)
    for p in range(2):
        white = (both[p] * scale).astype(jnp.bfloat16)
        for t in range(tiles):
            for r in range(rounds):
                out_ref[0, t, r, p] = white[r * ch : (r + 1) * ch, t * LANES : (t + 1) * LANES]


def spread_row(ref, at, row, ch):
    eight = ref[(*at, pl.ds(row, 8, stride=0), slice(None))]
    pair = jnp.concatenate([eight, eight], axis=0).astype(jnp.bfloat16)
    return jnp.concatenate([pair] * (ch // 16), axis=0)


def pairwise(terms):
    while len(terms) > 1:
        half = (len(terms) + 1) // 2
        terms = [terms[i] + terms[i + half] if i + half < len(terms) else terms[i] for i in range(half)]
    return terms[0]


def cross_kernel(params_ref, *refs, masks, added):
    column_refs = refs[: len(masks)]
    local_ref, out_ref, source_ref = refs[len(masks)], refs[-2], refs[-1]
    tiles, win, ch = local_ref.shape[1:4]
    rounds = source_ref.shape[2]
    per_round = ch // SRC_STEP
    step = pl.program_id(0)
    r = step // per_round
    first = 2 + rounds + step * SRC_STEP
    here = lax.rem(params_ref[0], win)

    @pl.when(step == 0)
    def _():
        for i, ref in enumerate(column_refs):
            for t in range(tiles):
                source_ref[i, t] = ref[0, t].astype(jnp.float32) * (1.0 / win)

    whole = out_ref.shape[1] > SRC_STEP

    def one_tile(ft, _):
        at = pl.ds(pl.multiple_of(ft * LANES, LANES), LANES)
        mine = [(local_ref[0, ft, here ^ mask], local_ref[1, ft, here ^ mask]) for mask in masks]
        for j in range(SRC_STEP):
            row = params_ref[first + j]
            re = []
            im = []
            for i in range(len(masks)):
                sr, si = (spread_row(source_ref, (i, ft, r, p), row, ch) for p in range(2))
                lr, li = mine[i]
                re.append(sr * lr + si * li)
                im.append(sr * li - si * lr)
            re = pairwise(re)
            im = pairwise(im)
            if added:
                re = re + refs[-3][0, step * SRC_STEP + j, ft]
                im = im + refs[-3][1, step * SRC_STEP + j, ft]
            if whole:
                out_ref[0, step * SRC_STEP + j, ft] = re
                out_ref[1, step * SRC_STEP + j, ft] = im
            else:
                out_ref[0, j, :, at] = re
                out_ref[1, j, :, at] = im
        return 0

    lax.fori_loop(0, tiles, one_tile, 0)


def swap(x, mask, n_chan):
    return lax.ppermute(x, "chan", [(i, i ^ mask) for i in range(n_chan)])


def body(spectra, filter_bank, band_index, window_mask, owner_order, source_offset):
    n_chan = lax.axis_size("chan")
    me = lax.axis_index("chan").astype(jnp.int32)
    _, win, ch, freq = spectra.shape
    banks, taps = filter_bank.shape[1:]
    rounds = owner_order.shape[0]
    count = win * ch
    tiles = freq // LANES
    pieces = win * tiles
    sources = rounds * ch
    in_parts = n_chan == pieces and win == 4 and tiles & (tiles - 1) == 0
    smem = pl.BlockSpec(memory_space=pltpu.SMEM)
    vmem = pl.BlockSpec(memory_space=pltpu.VMEM)

    split = pl.pallas_call(
        split_kernel,
        out_shape=jax.ShapeDtypeStruct((pieces, 2 * ch + 16, LANES), jnp.bfloat16),
        compiler_params=room(56),
        name="split",
    )(spectra, window_mask)
    if in_parts:
        held = lax.all_to_all(split, "chan", 0, 0)[:, None]
        first = me
    else:
        held = lax.all_gather(split, "chan")
        first = jnp.int32(0)
    params = jnp.concatenate([first[None], lax.div(first, jnp.int32(win))[None], owner_order, source_offset.reshape(-1)])

    ends = n_chan - 1
    before = lax.ppermute(spectra, "chan", [(i, i + 1) for i in range(ends)])
    after = lax.ppermute(spectra, "chan", [(i + 1, i) for i in range(ends)])
    held, before, after = lax.optimization_barrier((held, before, after))

    weight, band, index, valid = pl.pallas_call(
        prep_kernel,
        out_shape=(
            jax.ShapeDtypeStruct((2 * banks * 2 * ch, 2 * LANES), jnp.bfloat16),
            jax.ShapeDtypeStruct((freq, freq), jnp.bfloat16),
            jax.ShapeDtypeStruct((tiles, 1, LANES), jnp.int32),
            jax.ShapeDtypeStruct((count, LANES), jnp.float32),
        ),
        scratch_shapes=[pltpu.VMEM((2, banks, LANES), jnp.float32)],
        compiler_params=room(8),
        name="prep",
    )(filter_bank, band_index.reshape(tiles, 1, LANES), window_mask)

    count_here = held.shape[1]
    filtered = pl.pallas_call(
        functools.partial(source_kernel, win=win),
        grid=(count_here,),
        in_specs=[
            smem,
            pl.BlockSpec((n_chan, 1, 2 * ch + 16, LANES), lambda s: (0, s, 0, 0)),
            vmem,
            vmem,
        ],
        out_specs=pl.BlockSpec((1, rounds, 2, ch, LANES), lambda s: (s, 0, 0, 0, 0)),
        out_shape=jax.ShapeDtypeStruct((count_here, rounds, 2, ch, LANES), jnp.bfloat16),
        compiler_params=room(16),
        name="source_filter",
    )(params, held, weight, index)

    if in_parts:
        zparts = [filtered] + [swap(filtered, win * k, n_chan) for k in range(1, tiles)]

    local = pl.pallas_call(
        own_kernel,
        out_shape=jax.ShapeDtypeStruct((2, tiles, win, ch, LANES), jnp.bfloat16),
        in_specs=[vmem] * 7,
        out_specs=vmem,
        scratch_shapes=[pltpu.VMEM((2, count, freq), jnp.float32)],
        compiler_params=room(16),
        cost_estimate=pl.CostEstimate(
            flops=4 * banks * 2 * ch * 2 * LANES * win * freq, bytes_accessed=3 << 20, transcendentals=0
        ),
        name="own_whiten",
    )(before, spectra, after, weight, band, index, valid)

    shape = (tiles, rounds, 2, ch, LANES)
    if in_parts:
        zparts[-1], local = lax.optimization_barrier((zparts[-1], local))
        windows = 1
        specs = [vmem] * tiles
    else:
        windows = win
        zparts = [filtered.reshape((tiles, win) + shape[1:])]
        specs = [pl.BlockSpec((tiles, 1) + shape[1:], lambda s: (0, s, 0, 0, 0, 0))]
    column = pl.pallas_call(
        column_kernel,
        grid=(windows,),
        in_specs=[smem] + specs + [vmem],
        out_specs=pl.BlockSpec((1,) + shape, lambda s: (s, 0, 0, 0, 0, 0)),
        out_shape=jax.ShapeDtypeStruct((windows,) + shape, jnp.bfloat16),
        scratch_shapes=[pltpu.VMEM(shape, jnp.bfloat16)],
        compiler_params=room(16),
        name="column_whiten",
    )(params, *zparts, band)

    def cross(masks, columns, earlier, final):
        if final:
            spec = pl.BlockSpec((2, SRC_STEP, ch, freq), lambda s: (0, s, 0, 0))
            result = jax.ShapeDtypeStruct((2, sources, ch, freq), jnp.bfloat16)
        else:
            spec = vmem
            result = jax.ShapeDtypeStruct((2, sources, tiles, ch, LANES), jnp.bfloat16)
        return pl.pallas_call(
            functools.partial(cross_kernel, masks=masks, added=len(earlier) > 0),
            grid=(sources // SRC_STEP,),
            in_specs=[smem] + [vmem] * (len(columns) + 1 + len(earlier)),
            out_specs=spec,
            out_shape=result,
            scratch_shapes=[pltpu.VMEM((len(masks),) + shape, jnp.float32)],
            compiler_params=room(32),
            cost_estimate=pl.CostEstimate(
                flops=16 * len(masks) * sources * ch * freq, bytes_accessed=16 << 20, transcendentals=0
            ),
            name="cross",
        )(params, *columns, local, *earlier)

    if not in_parts:
        return cross(tuple(range(win)), [column[w : w + 1] for w in range(win)], [], True)
    far = swap(column, 2, n_chan)
    beside = swap(column, 1, n_chan)
    partial = cross((0, 1), [column, beside], [], False)
    far, partial = lax.optimization_barrier((far, partial))
    return cross((2, 3), [far, swap(far, 1, n_chan)], [partial], True)


def solution(mesh):
    in_specs = (
        P(None, "groups", "chan", None),
        P(),
        P(),
        P("groups", "chan"),
        P("groups"),
        P("groups", None),
    )
    out_specs = P(None, "groups", "chan", None)
    return jax.shard_map(body, mesh=mesh, in_specs=in_specs, out_specs=out_specs, check_vma=False)
```

```python
import functools

import jax
import jax.numpy as jnp
from jax import lax
from jax.experimental import pallas as pl
from jax.experimental.pallas import tpu as pltpu
from jax.sharding import PartitionSpec as P

SMOOTH = 17
LANES = 128
WATER = 0.05
SRC_STEP = 16
OUT_STEP = 8
SLOTS = 4


def room(mib):
    return pltpu.CompilerParams(vmem_limit_bytes=mib * 1024 * 1024)


def split_kernel(spectra_ref, flags_ref, piece_ref):
    _, win, ch, freq = spectra_ref.shape
    tiles = freq // LANES
    extra = piece_ref.shape[1] - 2 * ch
    for w in range(win):
        flags = jnp.broadcast_to(flags_ref[w : w + 1, :], (extra, ch)).astype(jnp.float32)
        for t in range(tiles):
            at = slice(t * LANES, (t + 1) * LANES)
            piece_ref[t * win + w, :ch] = spectra_ref[0, w, :, at]
            piece_ref[t * win + w, ch : 2 * ch] = spectra_ref[1, w, :, at]
            piece_ref[t * win + w, 2 * ch :] = jnp.zeros((extra, LANES), jnp.bfloat16)
            piece_ref[t * win + w, 2 * ch :, :ch] = flags.astype(jnp.bfloat16)


def prep_kernel(bank_ref, bins_ref, flags_ref, weight_ref, band_ref, index_ref, valid_ref, padded_ref):
    _, banks, taps = bank_ref.shape
    half = weight_ref.shape[0] // 2
    ch = half // (2 * banks)
    index_ref[...] = bins_ref[...]
    for w in range(flags_ref.shape[0]):
        column = flag_column(flags_ref[w : w + 1, :])
        valid_ref[w * ch : (w + 1) * ch, :] = jnp.broadcast_to(column, (ch, LANES))
    padded_ref[...] = jnp.zeros(padded_ref.shape, jnp.float32)
    padded_ref[:, :, :taps] = bank_ref[...]

    def skewed(row):
        tile = jnp.broadcast_to(row, (ch, LANES))
        return pltpu.roll(tile, 0, 1, stride=1, stride_axis=0)

    for b in range(banks):
        real = skewed(padded_ref[0, b : b + 1, :])
        imag = skewed(padded_ref[1, b : b + 1, :])
        base = b * 2 * ch
        for row, left, right in ((base, real, -imag), (base + ch, imag, real)):
            for col, val in ((0, left), (LANES, right)):
                high = val.astype(jnp.bfloat16)
                low = (val - high.astype(jnp.float32)).astype(jnp.bfloat16)
                weight_ref[row : row + ch, col : col + LANES] = high
                weight_ref[half + row : half + row + ch, col : col + LANES] = low
    rows = lax.broadcasted_iota(jnp.int32, band_ref.shape, 0)
    cols = lax.broadcasted_iota(jnp.int32, band_ref.shape, 1)
    near = jnp.abs(rows - cols) <= SMOOTH // 2
    band_ref[...] = jnp.where(near, 1.0, 0.0).astype(jnp.bfloat16)


def flag_column(row):
    ch = row.shape[1]
    rows = lax.broadcasted_iota(jnp.int32, (ch, ch), 0)
    cols = lax.broadcasted_iota(jnp.int32, (ch, ch), 1)
    return jnp.sum(jnp.where(rows == cols, row.astype(jnp.float32), 0.0), axis=1, keepdims=True)


def filtered_block(x, weight_ref, index, ch):
    half = weight_ref.shape[0] // 2
    y = jnp.dot(weight_ref[...], x, preferred_element_type=jnp.float32)
    rows = 2 * ch
    pick = y[:rows] + y[half : half + rows]
    for at in range(rows, half, rows):
        here = y[at : at + rows] + y[half + at : half + at + rows]
        pick = jnp.where(index == at // rows, here, pick)
    return pick


def running_scale(real, imag, band_ref):
    count = real.shape[0]
    power = real * real + imag * imag
    high = power.astype(jnp.bfloat16)
    low = (power - high.astype(jnp.float32)).astype(jnp.bfloat16)
    both = jnp.concatenate([high, low], axis=0)
    total = jnp.dot(both, band_ref[...], preferred_element_type=jnp.float32)
    return lax.rsqrt((total[:count] + total[count:]) * (1.0 / SMOOTH) + WATER)


def source_kernel(params_ref, x_ref, weight_ref, index_ref, out_ref, *, win):
    n_chan = x_ref.shape[0]
    _, rounds, _, ch, _ = out_ref.shape
    tile = lax.div(params_ref[0] + pl.program_id(0), win)
    zero = jnp.zeros((), jnp.bfloat16)
    gap = jnp.zeros((LANES - 3 * ch, LANES), jnp.bfloat16)
    columns = []
    for r in range(rounds):
        block = params_ref[2 + r]
        before = jnp.maximum(block - 1, 0)
        after = jnp.minimum(block + 1, n_chan - 1)
        parts = []
        for p in range(2):
            at = slice(p * ch, (p + 1) * ch)
            parts.append(jnp.where(block > 0, x_ref[before, 0, at], zero))
            parts.append(x_ref[block, 0, at])
            parts.append(jnp.where(block < n_chan - 1, x_ref[after, 0, at], zero))
            parts.append(gap)
        columns.append(jnp.concatenate(parts, axis=0))
    x = jnp.concatenate(columns, axis=1)
    index = jnp.concatenate([index_ref[tile]] * rounds, axis=1)
    pick = filtered_block(x, weight_ref, index, ch)
    for r in range(rounds):
        flags = x_ref[params_ref[2 + r], 0, 2 * ch :].astype(jnp.float32)[:1, :ch]
        valid = flag_column(flags)
        for p in range(2):
            part = pick[p * ch : (p + 1) * ch, r * LANES : (r + 1) * LANES] * valid
            out_ref[0, r, p] = part.astype(jnp.bfloat16)


def own_kernel(prev_ref, cur_ref, next_ref, weight_ref, band_ref, index_ref, valid_ref, out_ref, filt_ref):
    _, win, ch, freq = cur_ref.shape
    tiles = freq // LANES
    gap = jnp.zeros((LANES - 3 * ch, freq), jnp.bfloat16)
    index = jnp.concatenate([index_ref[t] for t in range(tiles)], axis=1)

    def one_window(w, _):
        parts = []
        for p in range(2):
            parts += [prev_ref[p, w], cur_ref[p, w], next_ref[p, w], gap]
        x = jnp.concatenate(parts, axis=0)
        pick = filtered_block(x, weight_ref, index, ch)
        at = pl.ds(pl.multiple_of(w * ch, ch), ch)
        filt_ref[0, at, :] = pick[:ch]
        filt_ref[1, at, :] = pick[ch:]
        return 0

    lax.fori_loop(0, win, one_window, 0)
    valid = jnp.concatenate([valid_ref[...]] * tiles, axis=1)
    scale = running_scale(filt_ref[0], filt_ref[1], band_ref) * valid
    for p in range(2):
        white = (filt_ref[p] * scale).astype(jnp.bfloat16)
        for t in range(tiles):
            for w in range(win):
                out_ref[p, t, w] = white[w * ch : (w + 1) * ch, t * LANES : (t + 1) * LANES]


def column_kernel(params_ref, *refs):
    band_ref, out_ref, piece_ref = refs[-3:]
    parts = refs[:-3]
    tiles, rounds, _, ch, _ = piece_ref.shape
    if len(parts) == tiles:
        place = params_ref[1]
        for k, ref in enumerate(parts):
            piece_ref[place ^ k] = ref[0]
    else:
        piece_ref[...] = parts[0][:, 0]
    both = []
    for p in range(2):
        rows = [
            jnp.concatenate([piece_ref[t, r, p] for t in range(tiles)], axis=1) for r in range(rounds)
        ]
        both.append(jnp.concatenate(rows, axis=0).astype(jnp.float32))
    scale = running_scale(both[0], both[1], band_ref)
    for p in range(2):
        white = (both[p] * scale).astype(jnp.bfloat16)
        for t in range(tiles):
            for r in range(rounds):
                out_ref[0, t, r, p] = white[r * ch : (r + 1) * ch, t * LANES : (t + 1) * LANES]


def spread_row(ref, at, row, ch):
    eight = ref[(*at, pl.ds(row, 8, stride=0), slice(None))]
    pair = jnp.concatenate([eight, eight], axis=0).astype(jnp.bfloat16)
    return jnp.concatenate([pair] * (ch // 16), axis=0)


def pairwise(terms):
    while len(terms) > 1:
        half = (len(terms) + 1) // 2
        terms = [terms[i] + terms[i + half] if i + half < len(terms) else terms[i] for i in range(half)]
    return terms[0]


def cross_kernel(params_ref, *refs, masks, added, final):
    column_refs = refs[: len(masks)]
    local_ref = refs[len(masks)]
    partial_ref = refs[len(masks) + 1]
    if final:
        out_ref, source_ref, stage_ref, sems = refs[-4:]
        group = stage_ref.shape[2]
    else:
        out_ref, source_ref = refs[-2:]
        group = SRC_STEP
    tiles, win, ch = local_ref.shape[1:4]
    rounds = source_ref.shape[2]
    per_round = ch // group
    step = pl.program_id(0)
    steps = rounds * per_round
    r = step // per_round
    begin = step * group
    first = 2 + rounds + begin
    here = lax.rem(params_ref[0], win)
    slot = lax.rem(step, SLOTS)

    def copies(at_step):
        at_slot = lax.rem(at_step, SLOTS)
        return [
            pltpu.make_async_copy(
                stage_ref.at[at_slot, p], out_ref.at[p, pl.ds(at_step * group, group)], sems.at[at_slot, p]
            )
            for p in range(2)
        ]

    @pl.when(step == 0)
    def _():
        for i, ref in enumerate(column_refs):
            for t in range(tiles):
                source_ref[i, t] = ref[0, t].astype(jnp.float32) * (1.0 / win)

    if final:

        @pl.when(step >= SLOTS)
        def _():
            for copy in copies(step - SLOTS):
                copy.wait()

    def one_tile(ft, _):
        at = pl.ds(pl.multiple_of(ft * LANES, LANES), LANES)
        mine = [(local_ref[0, ft, here ^ mask], local_ref[1, ft, here ^ mask]) for mask in masks]
        for j in range(group):
            row = params_ref[first + j]
            re = []
            im = []
            for i in range(len(masks)):
                sr, si = (spread_row(source_ref, (i, ft, r, p), row, ch) for p in range(2))
                lr, li = mine[i]
                re.append(sr * lr + si * li)
                im.append(sr * li - si * lr)
            re = pairwise(re)
            im = pairwise(im)
            if added:
                re = re + partial_ref[0, begin + j, ft]
                im = im + partial_ref[1, begin + j, ft]
            if final:
                stage_ref[slot, 0, j, :, at] = re
                stage_ref[slot, 1, j, :, at] = im
            else:
                out_ref[0, begin + j, ft] = re
                out_ref[1, begin + j, ft] = im
        return 0

    lax.fori_loop(0, tiles, one_tile, 0)

    if final:
        for copy in copies(step):
            copy.start()

        @pl.when(step == steps - 1)
        def _():
            for back in range(SLOTS):
                for copy in copies(step - back):
                    copy.wait()


def swap(x, mask, n_chan):
    return lax.ppermute(x, "chan", [(i, i ^ mask) for i in range(n_chan)])


def body(spectra, filter_bank, band_index, window_mask, owner_order, source_offset):
    n_chan = lax.axis_size("chan")
    me = lax.axis_index("chan").astype(jnp.int32)
    _, win, ch, freq = spectra.shape
    banks, taps = filter_bank.shape[1:]
    rounds = owner_order.shape[0]
    count = win * ch
    tiles = freq // LANES
    pieces = win * tiles
    sources = rounds * ch
    in_parts = n_chan == pieces and win == 4 and tiles & (tiles - 1) == 0
    smem = pl.BlockSpec(memory_space=pltpu.SMEM)
    vmem = pl.BlockSpec(memory_space=pltpu.VMEM)

    split = pl.pallas_call(
        split_kernel,
        out_shape=jax.ShapeDtypeStruct((pieces, 2 * ch + 16, LANES), jnp.bfloat16),
        compiler_params=room(56),
        name="split",
    )(spectra, window_mask)
    if in_parts:
        held = lax.all_to_all(split, "chan", 0, 0)[:, None]
        first = me
    else:
        held = lax.all_gather(split, "chan")
        first = jnp.int32(0)
    params = jnp.concatenate([first[None], lax.div(first, jnp.int32(win))[None], owner_order, source_offset.reshape(-1)])

    ends = n_chan - 1
    before = lax.ppermute(spectra, "chan", [(i, i + 1) for i in range(ends)])
    after = lax.ppermute(spectra, "chan", [(i + 1, i) for i in range(ends)])
    held, before, after = lax.optimization_barrier((held, before, after))

    weight, band, index, valid = pl.pallas_call(
        prep_kernel,
        out_shape=(
            jax.ShapeDtypeStruct((2 * banks * 2 * ch, 2 * LANES), jnp.bfloat16),
            jax.ShapeDtypeStruct((freq, freq), jnp.bfloat16),
            jax.ShapeDtypeStruct((tiles, 1, LANES), jnp.int32),
            jax.ShapeDtypeStruct((count, LANES), jnp.float32),
        ),
        scratch_shapes=[pltpu.VMEM((2, banks, LANES), jnp.float32)],
        compiler_params=room(8),
        name="prep",
    )(filter_bank, band_index.reshape(tiles, 1, LANES), window_mask)

    count_here = held.shape[1]
    filtered = pl.pallas_call(
        functools.partial(source_kernel, win=win),
        grid=(count_here,),
        in_specs=[
            smem,
            pl.BlockSpec((n_chan, 1, 2 * ch + 16, LANES), lambda s: (0, s, 0, 0)),
            vmem,
            vmem,
        ],
        out_specs=pl.BlockSpec((1, rounds, 2, ch, LANES), lambda s: (s, 0, 0, 0, 0)),
        out_shape=jax.ShapeDtypeStruct((count_here, rounds, 2, ch, LANES), jnp.bfloat16),
        compiler_params=room(16),
        name="source_filter",
    )(params, held, weight, index)

    if in_parts:
        zparts = [filtered] + [swap(filtered, win * k, n_chan) for k in range(1, tiles)]

    local = pl.pallas_call(
        own_kernel,
        out_shape=jax.ShapeDtypeStruct((2, tiles, win, ch, LANES), jnp.bfloat16),
        in_specs=[vmem] * 7,
        out_specs=vmem,
        scratch_shapes=[pltpu.VMEM((2, count, freq), jnp.float32)],
        compiler_params=room(16),
        cost_estimate=pl.CostEstimate(
            flops=4 * banks * 2 * ch * 2 * LANES * win * freq, bytes_accessed=3 << 20, transcendentals=0
        ),
        name="own_whiten",
    )(before, spectra, after, weight, band, index, valid)

    shape = (tiles, rounds, 2, ch, LANES)
    if in_parts:
        zparts[-1], local = lax.optimization_barrier((zparts[-1], local))
        windows = 1
        specs = [vmem] * tiles
    else:
        windows = win
        zparts = [filtered.reshape((tiles, win) + shape[1:])]
        specs = [pl.BlockSpec((tiles, 1) + shape[1:], lambda s: (0, s, 0, 0, 0, 0))]
    column = pl.pallas_call(
        column_kernel,
        grid=(windows,),
        in_specs=[smem] + specs + [vmem],
        out_specs=pl.BlockSpec((1,) + shape, lambda s: (s, 0, 0, 0, 0, 0)),
        out_shape=jax.ShapeDtypeStruct((windows,) + shape, jnp.bfloat16),
        scratch_shapes=[pltpu.VMEM(shape, jnp.bfloat16)],
        compiler_params=room(16),
        name="column_whiten",
    )(params, *zparts, band)

    def cross(masks, columns, earlier, final):
        scratch = [pltpu.VMEM((len(masks),) + shape, jnp.float32)]
        group = SRC_STEP
        spec = vmem
        result = jax.ShapeDtypeStruct((2, sources, tiles, ch, LANES), jnp.bfloat16)
        if final:
            group = OUT_STEP
            spec = pl.BlockSpec(memory_space=pl.ANY)
            result = jax.ShapeDtypeStruct((2, sources, ch, freq), jnp.bfloat16)
            scratch.append(pltpu.VMEM((SLOTS, 2, group, ch, freq), jnp.bfloat16))
            scratch.append(pltpu.SemaphoreType.DMA((SLOTS, 2)))
        return pl.pallas_call(
            functools.partial(cross_kernel, masks=masks, added=len(earlier) > 0, final=final),
            grid=(sources // group,),
            in_specs=[smem] + [vmem] * (len(columns) + 1 + len(earlier)),
            out_specs=spec,
            out_shape=result,
            scratch_shapes=scratch,
            compiler_params=room(32),
            cost_estimate=pl.CostEstimate(
                flops=16 * len(masks) * sources * ch * freq, bytes_accessed=16 << 20, transcendentals=0
            ),
            name="cross",
        )(params, *columns, local, *earlier)

    if not in_parts:
        return cross(tuple(range(win)), [column[w : w + 1] for w in range(win)], [], True)
    far = swap(column, 2, n_chan)
    beside = swap(column, 1, n_chan)
    partial = cross((0, 1), [column, beside], [], False)
    far, partial = lax.optimization_barrier((far, partial))
    return cross((2, 3), [far, swap(far, 1, n_chan)], [partial], True)


def solution(mesh):
    in_specs = (
        P(None, "groups", "chan", None),
        P(),
        P(),
        P("groups", "chan"),
        P("groups"),
        P("groups", None),
    )
    out_specs = P(None, "groups", "chan", None)
    return jax.shard_map(body, mesh=mesh, in_specs=in_specs, out_specs=out_specs, check_vma=False)
```

```python
import functools

import jax
import jax.numpy as jnp
from jax import lax
from jax.experimental import pallas as pl
from jax.experimental.pallas import tpu as pltpu
from jax.sharding import PartitionSpec as P

SMOOTH = 17
LANES = 128
WATER = 0.05
SRC_STEP = 16
OUT_STEP = 8
SLOTS = 4


def room(mib):
    return pltpu.CompilerParams(vmem_limit_bytes=mib * 1024 * 1024)


def split_kernel(spectra_ref, flags_ref, piece_ref):
    _, win, ch, freq = spectra_ref.shape
    tiles = freq // LANES
    extra = piece_ref.shape[1] - 2 * ch
    for w in range(win):
        flags = jnp.broadcast_to(flags_ref[w : w + 1, :], (extra, ch)).astype(jnp.float32)
        for t in range(tiles):
            at = slice(t * LANES, (t + 1) * LANES)
            piece_ref[t * win + w, :ch] = spectra_ref[0, w, :, at]
            piece_ref[t * win + w, ch : 2 * ch] = spectra_ref[1, w, :, at]
            piece_ref[t * win + w, 2 * ch :] = jnp.zeros((extra, LANES), jnp.bfloat16)
            piece_ref[t * win + w, 2 * ch :, :ch] = flags.astype(jnp.bfloat16)


def prep_kernel(
    bank_ref, bins_ref, flags_ref, offset_ref, weight_ref, band_ref, index_ref, valid_ref, pick_ref, padded_ref
):
    _, banks, taps = bank_ref.shape
    half = weight_ref.shape[0] // 2
    ch = half // (2 * banks)
    index_ref[...] = bins_ref[...]
    channel = lax.broadcasted_iota(jnp.int32, (ch, ch), 0)
    for r in range(offset_ref.shape[0]):
        picked = channel == offset_ref[r : r + 1, :]
        pick_ref[r] = jnp.where(picked, 1.0, 0.0).astype(jnp.bfloat16)
    for w in range(flags_ref.shape[0]):
        column = flag_column(flags_ref[w : w + 1, :])
        valid_ref[w * ch : (w + 1) * ch, :] = jnp.broadcast_to(column, (ch, LANES))
    padded_ref[...] = jnp.zeros(padded_ref.shape, jnp.float32)
    padded_ref[:, :, :taps] = bank_ref[...]

    def skewed(row):
        tile = jnp.broadcast_to(row, (ch, LANES))
        return pltpu.roll(tile, 0, 1, stride=1, stride_axis=0)

    for b in range(banks):
        real = skewed(padded_ref[0, b : b + 1, :])
        imag = skewed(padded_ref[1, b : b + 1, :])
        base = b * 2 * ch
        for row, left, right in ((base, real, -imag), (base + ch, imag, real)):
            for col, val in ((0, left), (LANES, right)):
                high = val.astype(jnp.bfloat16)
                low = (val - high.astype(jnp.float32)).astype(jnp.bfloat16)
                weight_ref[row : row + ch, col : col + LANES] = high
                weight_ref[half + row : half + row + ch, col : col + LANES] = low
    rows = lax.broadcasted_iota(jnp.int32, band_ref.shape, 0)
    cols = lax.broadcasted_iota(jnp.int32, band_ref.shape, 1)
    near = jnp.abs(rows - cols) <= SMOOTH // 2
    band_ref[...] = jnp.where(near, 1.0, 0.0).astype(jnp.bfloat16)


def flag_column(row):
    ch = row.shape[1]
    rows = lax.broadcasted_iota(jnp.int32, (ch, ch), 0)
    cols = lax.broadcasted_iota(jnp.int32, (ch, ch), 1)
    return jnp.sum(jnp.where(rows == cols, row.astype(jnp.float32), 0.0), axis=1, keepdims=True)


def filtered_block(x, weight_ref, index, ch):
    half = weight_ref.shape[0] // 2
    y = jnp.dot(weight_ref[...], x, preferred_element_type=jnp.float32)
    rows = 2 * ch
    pick = y[:rows] + y[half : half + rows]
    for at in range(rows, half, rows):
        here = y[at : at + rows] + y[half + at : half + at + rows]
        pick = jnp.where(index == at // rows, here, pick)
    return pick


def running_scale(real, imag, band_ref):
    count = real.shape[0]
    power = real * real + imag * imag
    high = power.astype(jnp.bfloat16)
    low = (power - high.astype(jnp.float32)).astype(jnp.bfloat16)
    both = jnp.concatenate([high, low], axis=0)
    total = jnp.dot(both, band_ref[...], preferred_element_type=jnp.float32)
    return lax.rsqrt((total[:count] + total[count:]) * (1.0 / SMOOTH) + WATER)


def source_kernel(params_ref, x_ref, weight_ref, index_ref, out_ref, *, win):
    n_chan = x_ref.shape[0]
    _, rounds, _, ch, _ = out_ref.shape
    tile = lax.div(params_ref[0] + pl.program_id(0), win)
    zero = jnp.zeros((), jnp.bfloat16)
    gap = jnp.zeros((LANES - 3 * ch, LANES), jnp.bfloat16)
    columns = []
    for r in range(rounds):
        block = params_ref[2 + r]
        before = jnp.maximum(block - 1, 0)
        after = jnp.minimum(block + 1, n_chan - 1)
        parts = []
        for p in range(2):
            at = slice(p * ch, (p + 1) * ch)
            parts.append(jnp.where(block > 0, x_ref[before, 0, at], zero))
            parts.append(x_ref[block, 0, at])
            parts.append(jnp.where(block < n_chan - 1, x_ref[after, 0, at], zero))
            parts.append(gap)
        columns.append(jnp.concatenate(parts, axis=0))
    x = jnp.concatenate(columns, axis=1)
    index = jnp.concatenate([index_ref[tile]] * rounds, axis=1)
    pick = filtered_block(x, weight_ref, index, ch)
    for r in range(rounds):
        flags = x_ref[params_ref[2 + r], 0, 2 * ch :].astype(jnp.float32)[:1, :ch]
        valid = flag_column(flags)
        for p in range(2):
            part = pick[p * ch : (p + 1) * ch, r * LANES : (r + 1) * LANES] * valid
            out_ref[0, r, p] = part.astype(jnp.bfloat16)


def own_kernel(prev_ref, cur_ref, next_ref, weight_ref, band_ref, index_ref, valid_ref, out_ref, filt_ref):
    _, win, ch, freq = cur_ref.shape
    tiles = freq // LANES
    gap = jnp.zeros((LANES - 3 * ch, freq), jnp.bfloat16)
    index = jnp.concatenate([index_ref[t] for t in range(tiles)], axis=1)

    def one_window(w, _):
        parts = []
        for p in range(2):
            parts += [prev_ref[p, w], cur_ref[p, w], next_ref[p, w], gap]
        x = jnp.concatenate(parts, axis=0)
        pick = filtered_block(x, weight_ref, index, ch)
        at = pl.ds(pl.multiple_of(w * ch, ch), ch)
        filt_ref[0, at, :] = pick[:ch]
        filt_ref[1, at, :] = pick[ch:]
        return 0

    lax.fori_loop(0, win, one_window, 0)
    valid = jnp.concatenate([valid_ref[...]] * tiles, axis=1)
    scale = running_scale(filt_ref[0], filt_ref[1], band_ref) * valid
    for p in range(2):
        white = (filt_ref[p] * scale).astype(jnp.bfloat16)
        for t in range(tiles):
            for w in range(win):
                out_ref[p, t, w] = white[w * ch : (w + 1) * ch, t * LANES : (t + 1) * LANES]


def column_kernel(params_ref, *refs):
    band_ref, pick_ref, out_ref, piece_ref = refs[-4:]
    parts = refs[:-4]
    tiles, rounds, _, ch, _ = piece_ref.shape
    if len(parts) == tiles:
        place = params_ref[1]
        for k, ref in enumerate(parts):
            piece_ref[place ^ k] = ref[0]
    else:
        piece_ref[...] = parts[0][:, 0]
    both = []
    for p in range(2):
        rows = []
        for r in range(rounds):
            row = jnp.concatenate([piece_ref[t, r, p] for t in range(tiles)], axis=1)
            rows.append(
                lax.dot_general(
                    pick_ref[r], row, (((0,), (0,)), ((), ())), preferred_element_type=jnp.float32
                )
            )
        both.append(jnp.concatenate(rows, axis=0))
    scale = running_scale(both[0], both[1], band_ref)
    for p in range(2):
        white = (both[p] * scale).astype(jnp.bfloat16)
        for t in range(tiles):
            for r in range(rounds):
                out_ref[0, t, r, p] = white[r * ch : (r + 1) * ch, t * LANES : (t + 1) * LANES]


def spread_row(ref, at, row, ch):
    eight = ref[(*at, row // 8, pl.ds(row % 8, 8, stride=0), slice(None))]
    pair = jnp.concatenate([eight, eight], axis=0).astype(jnp.bfloat16)
    return jnp.concatenate([pair] * (ch // 16), axis=0)


def pairwise(terms):
    while len(terms) > 1:
        half = (len(terms) + 1) // 2
        terms = [terms[i] + terms[i + half] if i + half < len(terms) else terms[i] for i in range(half)]
    return terms[0]


def cross_kernel(params_ref, *refs, masks, added, final):
    column_refs = refs[: len(masks)]
    local_ref = refs[len(masks)]
    partial_ref = refs[len(masks) + 1]
    if final:
        out_ref, source_ref, stage_ref, sems = refs[-4:]
        group = stage_ref.shape[2]
    else:
        out_ref, source_ref = refs[-2:]
        group = SRC_STEP
    tiles, win, ch = local_ref.shape[1:4]
    steps = source_ref.shape[2]
    rounds = steps * group // ch
    step = pl.program_id(0)
    begin = step * group
    here = lax.rem(params_ref[0], win)
    slot = lax.rem(step, SLOTS)

    def copies(at_step):
        at_slot = lax.rem(at_step, SLOTS)
        return [
            pltpu.make_async_copy(
                stage_ref.at[at_slot, p], out_ref.at[p, pl.ds(at_step * group, group)], sems.at[at_slot, p]
            )
            for p in range(2)
        ]

    @pl.when(step == 0)
    def _():
        for i, ref in enumerate(column_refs):
            for t in range(tiles):
                for rr in range(rounds):
                    for p in range(2):
                        rows = ref[0, t, rr, p].astype(jnp.float32) * (1.0 / win)
                        source_ref[i, t, rr * (ch // group) : (rr + 1) * (ch // group), p] = rows.reshape(
                            ch // group, group // 8, 8, LANES
                        )

    if final:

        @pl.when(step >= SLOTS)
        def _():
            for copy in copies(step - SLOTS):
                copy.wait()

    def one_tile(ft, _):
        at = pl.ds(pl.multiple_of(ft * LANES, LANES), LANES)
        mine = [(local_ref[0, ft, here ^ mask], local_ref[1, ft, here ^ mask]) for mask in masks]
        for j in range(group):
            re = []
            im = []
            for i in range(len(masks)):
                sr, si = (spread_row(source_ref, (i, ft, step, p), j, ch) for p in range(2))
                lr, li = mine[i]
                re.append(sr * lr + si * li)
                im.append(sr * li - si * lr)
            re = pairwise(re)
            im = pairwise(im)
            if added:
                re = re + partial_ref[0, begin + j, ft]
                im = im + partial_ref[1, begin + j, ft]
            if final:
                stage_ref[slot, 0, j, :, at] = re
                stage_ref[slot, 1, j, :, at] = im
            else:
                out_ref[0, begin + j, ft] = re
                out_ref[1, begin + j, ft] = im
        return 0

    lax.fori_loop(0, tiles, one_tile, 0)

    if final:
        for copy in copies(step):
            copy.start()

        @pl.when(step == steps - 1)
        def _():
            for back in range(SLOTS):
                for copy in copies(step - back):
                    copy.wait()


def swap(x, mask, n_chan):
    return lax.ppermute(x, "chan", [(i, i ^ mask) for i in range(n_chan)])


def body(spectra, filter_bank, band_index, window_mask, owner_order, source_offset):
    n_chan = lax.axis_size("chan")
    me = lax.axis_index("chan").astype(jnp.int32)
    _, win, ch, freq = spectra.shape
    banks, taps = filter_bank.shape[1:]
    rounds = owner_order.shape[0]
    count = win * ch
    tiles = freq // LANES
    pieces = win * tiles
    sources = rounds * ch
    in_parts = n_chan == pieces and win == 4 and tiles & (tiles - 1) == 0
    smem = pl.BlockSpec(memory_space=pltpu.SMEM)
    vmem = pl.BlockSpec(memory_space=pltpu.VMEM)

    split = pl.pallas_call(
        split_kernel,
        out_shape=jax.ShapeDtypeStruct((pieces, 2 * ch + 16, LANES), jnp.bfloat16),
        compiler_params=room(56),
        name="split",
    )(spectra, window_mask)
    if in_parts:
        held = lax.all_to_all(split, "chan", 0, 0)[:, None]
        first = me
    else:
        held = lax.all_gather(split, "chan")
        first = jnp.int32(0)
    params = jnp.concatenate([first[None], lax.div(first, jnp.int32(win))[None], owner_order])

    ends = n_chan - 1
    before = lax.ppermute(spectra, "chan", [(i, i + 1) for i in range(ends)])
    after = lax.ppermute(spectra, "chan", [(i + 1, i) for i in range(ends)])
    held, before, after = lax.optimization_barrier((held, before, after))

    weight, band, index, valid, pick = pl.pallas_call(
        prep_kernel,
        out_shape=(
            jax.ShapeDtypeStruct((2 * banks * 2 * ch, 2 * LANES), jnp.bfloat16),
            jax.ShapeDtypeStruct((freq, freq), jnp.bfloat16),
            jax.ShapeDtypeStruct((tiles, 1, LANES), jnp.int32),
            jax.ShapeDtypeStruct((count, LANES), jnp.float32),
            jax.ShapeDtypeStruct((rounds, ch, ch), jnp.bfloat16),
        ),
        scratch_shapes=[pltpu.VMEM((2, banks, LANES), jnp.float32)],
        compiler_params=room(8),
        name="prep",
    )(filter_bank, band_index.reshape(tiles, 1, LANES), window_mask, source_offset)

    count_here = held.shape[1]
    filtered = pl.pallas_call(
        functools.partial(source_kernel, win=win),
        grid=(count_here,),
        in_specs=[
            smem,
            pl.BlockSpec((n_chan, 1, 2 * ch + 16, LANES), lambda s: (0, s, 0, 0)),
            vmem,
            vmem,
        ],
        out_specs=pl.BlockSpec((1, rounds, 2, ch, LANES), lambda s: (s, 0, 0, 0, 0)),
        out_shape=jax.ShapeDtypeStruct((count_here, rounds, 2, ch, LANES), jnp.bfloat16),
        compiler_params=room(16),
        name="source_filter",
    )(params, held, weight, index)

    if in_parts:
        zparts = [filtered] + [swap(filtered, win * k, n_chan) for k in range(1, tiles)]

    local = pl.pallas_call(
        own_kernel,
        out_shape=jax.ShapeDtypeStruct((2, tiles, win, ch, LANES), jnp.bfloat16),
        in_specs=[vmem] * 7,
        out_specs=vmem,
        scratch_shapes=[pltpu.VMEM((2, count, freq), jnp.float32)],
        compiler_params=room(16),
        cost_estimate=pl.CostEstimate(
            flops=4 * banks * 2 * ch * 2 * LANES * win * freq, bytes_accessed=3 << 20, transcendentals=0
        ),
        name="own_whiten",
    )(before, spectra, after, weight, band, index, valid)

    shape = (tiles, rounds, 2, ch, LANES)
    if in_parts:
        zparts[-1], local = lax.optimization_barrier((zparts[-1], local))
        windows = 1
        specs = [vmem] * tiles
    else:
        windows = win
        zparts = [filtered.reshape((tiles, win) + shape[1:])]
        specs = [pl.BlockSpec((tiles, 1) + shape[1:], lambda s: (0, s, 0, 0, 0, 0))]
    column = pl.pallas_call(
        column_kernel,
        grid=(windows,),
        in_specs=[smem] + specs + [vmem, vmem],
        out_specs=pl.BlockSpec((1,) + shape, lambda s: (s, 0, 0, 0, 0, 0)),
        out_shape=jax.ShapeDtypeStruct((windows,) + shape, jnp.bfloat16),
        scratch_shapes=[pltpu.VMEM(shape, jnp.bfloat16)],
        compiler_params=room(16),
        name="column_whiten",
    )(params, *zparts, band, pick)

    def cross(masks, columns, earlier, final):
        group = OUT_STEP if final else SRC_STEP
        rows = (len(masks), tiles, sources // group, 2, group // 8, 8, LANES)
        scratch = [pltpu.VMEM(rows, jnp.float32)]
        spec = vmem
        result = jax.ShapeDtypeStruct((2, sources, tiles, ch, LANES), jnp.bfloat16)
        if final:
            spec = pl.BlockSpec(memory_space=pl.ANY)
            result = jax.ShapeDtypeStruct((2, sources, ch, freq), jnp.bfloat16)
            scratch.append(pltpu.VMEM((SLOTS, 2, group, ch, freq), jnp.bfloat16))
            scratch.append(pltpu.SemaphoreType.DMA((SLOTS, 2)))
        return pl.pallas_call(
            functools.partial(cross_kernel, masks=masks, added=len(earlier) > 0, final=final),
            grid=(sources // group,),
            in_specs=[smem] + [vmem] * (len(columns) + 1 + len(earlier)),
            out_specs=spec,
            out_shape=result,
            scratch_shapes=scratch,
            compiler_params=room(32),
            cost_estimate=pl.CostEstimate(
                flops=16 * len(masks) * sources * ch * freq, bytes_accessed=16 << 20, transcendentals=0
            ),
            name="cross",
        )(params, *columns, local, *earlier)

    if not in_parts:
        return cross(tuple(range(win)), [column[w : w + 1] for w in range(win)], [], True)
    far = swap(column, 2, n_chan)
    beside = swap(column, 1, n_chan)
    partial = cross((0, 1), [column, beside], [], False)
    far, partial = lax.optimization_barrier((far, partial))
    return cross((2, 3), [far, swap(far, 1, n_chan)], [partial], True)


def solution(mesh):
    in_specs = (
        P(None, "groups", "chan", None),
        P(),
        P(),
        P("groups", "chan"),
        P("groups"),
        P("groups", None),
    )
    out_specs = P(None, "groups", "chan", None)
    return jax.shard_map(body, mesh=mesh, in_specs=in_specs, out_specs=out_specs, check_vma=False)
```

```python
import functools

import jax
import jax.numpy as jnp
from jax import lax
from jax.experimental import pallas as pl
from jax.experimental.pallas import tpu as pltpu
from jax.sharding import PartitionSpec as P

SMOOTH = 17
LANES = 128
WATER = 0.05
OUT_STEP = 8
SLOTS = 4


def room(mib):
    return pltpu.CompilerParams(vmem_limit_bytes=mib * 1024 * 1024)


def split_kernel(spectra_ref, flags_ref, piece_ref):
    _, win, ch, freq = spectra_ref.shape
    tiles = freq // LANES
    extra = piece_ref.shape[1] - 2 * ch
    for w in range(win):
        flags = jnp.broadcast_to(flags_ref[w : w + 1, :], (extra, ch)).astype(jnp.float32)
        for t in range(tiles):
            at = slice(t * LANES, (t + 1) * LANES)
            piece_ref[t * win + w, :ch] = spectra_ref[0, w, :, at]
            piece_ref[t * win + w, ch : 2 * ch] = spectra_ref[1, w, :, at]
            piece_ref[t * win + w, 2 * ch :] = jnp.zeros((extra, LANES), jnp.bfloat16)
            piece_ref[t * win + w, 2 * ch :, :ch] = flags.astype(jnp.bfloat16)


def prep_kernel(
    bank_ref, bins_ref, flags_ref, offset_ref, weight_ref, band_ref, index_ref, valid_ref, pick_ref, padded_ref
):
    _, banks, taps = bank_ref.shape
    half = weight_ref.shape[0] // 2
    ch = half // (2 * banks)
    index_ref[...] = bins_ref[...]
    channel = lax.broadcasted_iota(jnp.int32, (ch, ch), 0)
    for r in range(offset_ref.shape[0]):
        picked = channel == offset_ref[r : r + 1, :]
        pick_ref[r] = jnp.where(picked, 1.0, 0.0).astype(jnp.bfloat16)
    for w in range(flags_ref.shape[0]):
        column = flag_column(flags_ref[w : w + 1, :])
        valid_ref[w * ch : (w + 1) * ch, :] = jnp.broadcast_to(column, (ch, LANES))
    padded_ref[...] = jnp.zeros(padded_ref.shape, jnp.float32)
    padded_ref[:, :, :taps] = bank_ref[...]

    def skewed(row):
        tile = jnp.broadcast_to(row, (ch, LANES))
        return pltpu.roll(tile, 0, 1, stride=1, stride_axis=0)

    for b in range(banks):
        real = skewed(padded_ref[0, b : b + 1, :])
        imag = skewed(padded_ref[1, b : b + 1, :])
        base = b * 2 * ch
        for row, left, right in ((base, real, -imag), (base + ch, imag, real)):
            for col, val in ((0, left), (LANES, right)):
                high = val.astype(jnp.bfloat16)
                low = (val - high.astype(jnp.float32)).astype(jnp.bfloat16)
                weight_ref[row : row + ch, col : col + LANES] = high
                weight_ref[half + row : half + row + ch, col : col + LANES] = low
    rows = lax.broadcasted_iota(jnp.int32, band_ref.shape, 0)
    cols = lax.broadcasted_iota(jnp.int32, band_ref.shape, 1)
    near = jnp.abs(rows - cols) <= SMOOTH // 2
    band_ref[...] = jnp.where(near, 1.0, 0.0).astype(jnp.bfloat16)


def flag_column(row):
    ch = row.shape[1]
    rows = lax.broadcasted_iota(jnp.int32, (ch, ch), 0)
    cols = lax.broadcasted_iota(jnp.int32, (ch, ch), 1)
    return jnp.sum(jnp.where(rows == cols, row.astype(jnp.float32), 0.0), axis=1, keepdims=True)


def filtered_block(x, weight_ref, index, ch):
    half = weight_ref.shape[0] // 2
    y = jnp.dot(weight_ref[...], x, preferred_element_type=jnp.float32)
    rows = 2 * ch
    pick = y[:rows] + y[half : half + rows]
    for at in range(rows, half, rows):
        here = y[at : at + rows] + y[half + at : half + at + rows]
        pick = jnp.where(index == at // rows, here, pick)
    return pick


def running_scale(real, imag, band_ref):
    count = real.shape[0]
    power = real * real + imag * imag
    high = power.astype(jnp.bfloat16)
    low = (power - high.astype(jnp.float32)).astype(jnp.bfloat16)
    both = jnp.concatenate([high, low], axis=0)
    total = jnp.dot(both, band_ref[...], preferred_element_type=jnp.float32)
    return lax.rsqrt((total[:count] + total[count:]) * (1.0 / SMOOTH) + WATER)


def source_kernel(params_ref, x_ref, weight_ref, index_ref, *out_refs, win):
    n_chan = x_ref.shape[0]
    _, some, _, ch, _ = out_refs[0].shape
    rounds = some * len(out_refs)
    tile = lax.div(params_ref[0] + pl.program_id(0), win)
    zero = jnp.zeros((), jnp.bfloat16)
    gap = jnp.zeros((LANES - 3 * ch, LANES), jnp.bfloat16)
    columns = []
    for r in range(rounds):
        block = params_ref[2 + r]
        before = jnp.maximum(block - 1, 0)
        after = jnp.minimum(block + 1, n_chan - 1)
        parts = []
        for p in range(2):
            at = slice(p * ch, (p + 1) * ch)
            parts.append(jnp.where(block > 0, x_ref[before, 0, at], zero))
            parts.append(x_ref[block, 0, at])
            parts.append(jnp.where(block < n_chan - 1, x_ref[after, 0, at], zero))
            parts.append(gap)
        columns.append(jnp.concatenate(parts, axis=0))
    x = jnp.concatenate(columns, axis=1)
    index = jnp.concatenate([index_ref[tile]] * rounds, axis=1)
    pick = filtered_block(x, weight_ref, index, ch)
    for r in range(rounds):
        flags = x_ref[params_ref[2 + r], 0, 2 * ch :].astype(jnp.float32)[:1, :ch]
        valid = flag_column(flags)
        for p in range(2):
            part = pick[p * ch : (p + 1) * ch, r * LANES : (r + 1) * LANES] * valid
            out_refs[r // some][0, r % some, p] = part.astype(jnp.bfloat16)


def own_kernel(prev_ref, cur_ref, next_ref, weight_ref, band_ref, index_ref, valid_ref, out_ref, filt_ref):
    _, win, ch, freq = cur_ref.shape
    tiles = freq // LANES
    gap = jnp.zeros((LANES - 3 * ch, freq), jnp.bfloat16)
    index = jnp.concatenate([index_ref[t] for t in range(tiles)], axis=1)

    def one_window(w, _):
        parts = []
        for p in range(2):
            parts += [prev_ref[p, w], cur_ref[p, w], next_ref[p, w], gap]
        x = jnp.concatenate(parts, axis=0)
        pick = filtered_block(x, weight_ref, index, ch)
        at = pl.ds(pl.multiple_of(w * ch, ch), ch)
        filt_ref[0, at, :] = pick[:ch]
        filt_ref[1, at, :] = pick[ch:]
        return 0

    lax.fori_loop(0, win, one_window, 0)
    valid = jnp.concatenate([valid_ref[...]] * tiles, axis=1)
    scale = running_scale(filt_ref[0], filt_ref[1], band_ref) * valid
    for p in range(2):
        white = (filt_ref[p] * scale).astype(jnp.bfloat16)
        for t in range(tiles):
            for w in range(win):
                out_ref[p, t, w] = white[w * ch : (w + 1) * ch, t * LANES : (t + 1) * LANES]


def column_kernel(params_ref, *refs, start):
    band_ref, pick_ref, out_ref, piece_ref = refs[-4:]
    parts = refs[:-4]
    tiles, rounds, _, ch, _ = piece_ref.shape
    if len(parts) == tiles:
        place = params_ref[1]
        for k, ref in enumerate(parts):
            piece_ref[place ^ k] = ref[0]
    else:
        piece_ref[...] = parts[0][:, 0]
    both = []
    for p in range(2):
        rows = []
        for r in range(rounds):
            row = jnp.concatenate([piece_ref[t, r, p] for t in range(tiles)], axis=1)
            rows.append(
                lax.dot_general(
                    pick_ref[start + r], row, (((0,), (0,)), ((), ())), preferred_element_type=jnp.float32
                )
            )
        both.append(jnp.concatenate(rows, axis=0))
    scale = running_scale(both[0], both[1], band_ref)
    for p in range(2):
        white = (both[p] * scale).astype(jnp.bfloat16)
        for t in range(tiles):
            for r in range(rounds):
                out_ref[0, t, r, p] = white[r * ch : (r + 1) * ch, t * LANES : (t + 1) * LANES]


def spread_row(ref, at, row, ch):
    eight = ref[(*at, row // 8, pl.ds(row % 8, 8, stride=0), slice(None))]
    pair = jnp.concatenate([eight, eight], axis=0).astype(jnp.bfloat16)
    return jnp.concatenate([pair] * (ch // 16), axis=0)


def pairwise(terms):
    while len(terms) > 1:
        half = (len(terms) + 1) // 2
        terms = [terms[i] + terms[i + half] if i + half < len(terms) else terms[i] for i in range(half)]
    return terms[0]


def cross_kernel(params_ref, *refs, masks, start):
    column_refs = refs[: len(masks)]
    local_ref = refs[len(masks)]
    out_ref, source_ref, stage_ref, sems = refs[-4:]
    tiles, win, ch = local_ref.shape[1:4]
    steps = source_ref.shape[2]
    group = stage_ref.shape[2]
    per_round = ch // group
    step = pl.program_id(0)
    here = lax.rem(params_ref[0], win)
    slot = lax.rem(step, SLOTS)

    def copies(at_step):
        at_slot = lax.rem(at_step, SLOTS)
        rows = pl.ds(start * ch + at_step * group, group)
        return [
            pltpu.make_async_copy(stage_ref.at[at_slot, p], out_ref.at[p, rows], sems.at[at_slot, p])
            for p in range(2)
        ]

    @pl.when(step == 0)
    def _():
        for i, ref in enumerate(column_refs):
            for t in range(tiles):
                for r in range(steps // per_round):
                    for p in range(2):
                        rows = ref[0, t, r, p].astype(jnp.float32) * (1.0 / win)
                        source_ref[i, t, r * per_round : (r + 1) * per_round, p] = rows.reshape(
                            per_round, group // 8, 8, LANES
                        )

    @pl.when(step >= SLOTS)
    def _():
        for copy in copies(step - SLOTS):
            copy.wait()

    def one_tile(ft, _):
        at = pl.ds(pl.multiple_of(ft * LANES, LANES), LANES)
        mine = [(local_ref[0, ft, here ^ mask], local_ref[1, ft, here ^ mask]) for mask in masks]
        for j in range(group):
            re = []
            im = []
            for i in range(len(masks)):
                sr, si = (spread_row(source_ref, (i, ft, step, p), j, ch) for p in range(2))
                lr, li = mine[i]
                re.append(sr * lr + si * li)
                im.append(sr * li - si * lr)
            stage_ref[slot, 0, j, :, at] = pairwise(re)
            stage_ref[slot, 1, j, :, at] = pairwise(im)
        return 0

    lax.fori_loop(0, tiles, one_tile, 0)
    for copy in copies(step):
        copy.start()

    @pl.when(step == steps - 1)
    def _():
        for back in range(SLOTS):
            for copy in copies(step - back):
                copy.wait()


def swap(x, mask, n_chan):
    return lax.ppermute(x, "chan", [(i, i ^ mask) for i in range(n_chan)])


def body(spectra, filter_bank, band_index, window_mask, owner_order, source_offset):
    n_chan = lax.axis_size("chan")
    me = lax.axis_index("chan").astype(jnp.int32)
    _, win, ch, freq = spectra.shape
    banks, taps = filter_bank.shape[1:]
    rounds = owner_order.shape[0]
    count = win * ch
    tiles = freq // LANES
    pieces = win * tiles
    sources = rounds * ch
    in_parts = n_chan == pieces and win == 4 and tiles & (tiles - 1) == 0
    smem = pl.BlockSpec(memory_space=pltpu.SMEM)
    vmem = pl.BlockSpec(memory_space=pltpu.VMEM)

    split = pl.pallas_call(
        split_kernel,
        out_shape=jax.ShapeDtypeStruct((pieces, 2 * ch + 16, LANES), jnp.bfloat16),
        compiler_params=room(56),
        name="split",
    )(spectra, window_mask)
    if in_parts:
        held = lax.all_to_all(split, "chan", 0, 0)[:, None]
        first = me
    else:
        held = lax.all_gather(split, "chan")
        first = jnp.int32(0)
    params = jnp.concatenate([first[None], lax.div(first, jnp.int32(win))[None], owner_order])

    ends = n_chan - 1
    before = lax.ppermute(spectra, "chan", [(i, i + 1) for i in range(ends)])
    after = lax.ppermute(spectra, "chan", [(i + 1, i) for i in range(ends)])
    held, before, after = lax.optimization_barrier((held, before, after))

    weight, band, index, valid, pick = pl.pallas_call(
        prep_kernel,
        out_shape=(
            jax.ShapeDtypeStruct((2 * banks * 2 * ch, 2 * LANES), jnp.bfloat16),
            jax.ShapeDtypeStruct((freq, freq), jnp.bfloat16),
            jax.ShapeDtypeStruct((tiles, 1, LANES), jnp.int32),
            jax.ShapeDtypeStruct((count, LANES), jnp.float32),
            jax.ShapeDtypeStruct((rounds, ch, ch), jnp.bfloat16),
        ),
        scratch_shapes=[pltpu.VMEM((2, banks, LANES), jnp.float32)],
        compiler_params=room(8),
        name="prep",
    )(filter_bank, band_index.reshape(tiles, 1, LANES), window_mask, source_offset)

    count_here = held.shape[1]
    chunks = 2 if in_parts and rounds % 2 == 0 else 1
    some = rounds // chunks
    filtered = pl.pallas_call(
        functools.partial(source_kernel, win=win),
        grid=(count_here,),
        in_specs=[
            smem,
            pl.BlockSpec((n_chan, 1, 2 * ch + 16, LANES), lambda s: (0, s, 0, 0)),
            vmem,
            vmem,
        ],
        out_specs=[pl.BlockSpec((1, some, 2, ch, LANES), lambda s: (s, 0, 0, 0, 0))] * chunks,
        out_shape=[jax.ShapeDtypeStruct((count_here, some, 2, ch, LANES), jnp.bfloat16)] * chunks,
        compiler_params=room(16),
        name="source_filter",
    )(params, held, weight, index)

    local = pl.pallas_call(
        own_kernel,
        out_shape=jax.ShapeDtypeStruct((2, tiles, win, ch, LANES), jnp.bfloat16),
        in_specs=[vmem] * 7,
        out_specs=vmem,
        scratch_shapes=[pltpu.VMEM((2, count, freq), jnp.float32)],
        compiler_params=room(16),
        cost_estimate=pl.CostEstimate(
            flops=4 * banks * 2 * ch * 2 * LANES * win * freq, bytes_accessed=3 << 20, transcendentals=0
        ),
        name="own_whiten",
    )(before, spectra, after, weight, band, index, valid)

    shape = (tiles, some, 2, ch, LANES)
    if in_parts:
        windows = 1
        specs = [vmem] * tiles
        filtered = list(filtered)
        filtered[-1], local = lax.optimization_barrier((filtered[-1], local))
        zparts = [[f] + [swap(f, win * k, n_chan) for k in range(1, tiles)] for f in filtered]
    else:
        windows = win
        zparts = [[f.reshape((tiles, win) + shape[1:])] for f in filtered]
        specs = [pl.BlockSpec((tiles, 1) + shape[1:], lambda s: (0, s, 0, 0, 0, 0))]

    def whiten(c):
        return pl.pallas_call(
            functools.partial(column_kernel, start=c * some),
            grid=(windows,),
            in_specs=[smem] + specs + [vmem, vmem],
            out_specs=pl.BlockSpec((1,) + shape, lambda s: (s, 0, 0, 0, 0, 0)),
            out_shape=jax.ShapeDtypeStruct((windows,) + shape, jnp.bfloat16),
            scratch_shapes=[pltpu.VMEM(shape, jnp.bfloat16)],
            compiler_params=room(16),
            name="column_whiten",
        )(params, *zparts[c], band, pick)

    def cross(c, masks, columns, earlier):
        steps = some * ch // OUT_STEP
        anywhere = pl.BlockSpec(memory_space=pl.ANY)
        return pl.pallas_call(
            functools.partial(cross_kernel, masks=masks, start=c * some),
            grid=(steps,),
            in_specs=[smem] + [vmem] * (len(columns) + 1) + [anywhere] * len(earlier),
            out_specs=anywhere,
            out_shape=jax.ShapeDtypeStruct((2, sources, ch, freq), jnp.bfloat16),
            input_output_aliases={len(columns) + 2: 0} if earlier else {},
            scratch_shapes=[
                pltpu.VMEM((len(masks), tiles, steps, 2, OUT_STEP // 8, 8, LANES), jnp.float32),
                pltpu.VMEM((SLOTS, 2, OUT_STEP, ch, freq), jnp.bfloat16),
                pltpu.SemaphoreType.DMA((SLOTS, 2)),
            ],
            compiler_params=room(24),
            cost_estimate=pl.CostEstimate(
                flops=16 * win * sources * ch * freq // chunks, bytes_accessed=12 << 20, transcendentals=0
            ),
            name="cross",
        )(params, *columns, local, *earlier)

    out = []
    for c in range(chunks):
        column = whiten(c)
        if in_parts:
            far = swap(column, 2, n_chan)
            masks = (0, 1, 2, 3)
            columns = [column, swap(column, 1, n_chan), far, swap(far, 1, n_chan)]
        else:
            masks = tuple(range(win))
            columns = [column[w : w + 1] for w in range(win)]
        out = [cross(c, masks, columns, out)]
    return out[0]


def solution(mesh):
    in_specs = (
        P(None, "groups", "chan", None),
        P(),
        P(),
        P("groups", "chan"),
        P("groups"),
        P("groups", None),
    )
    out_specs = P(None, "groups", "chan", None)
    return jax.shard_map(body, mesh=mesh, in_specs=in_specs, out_specs=out_specs, check_vma=False)
```

```python
import functools

import jax
import jax.numpy as jnp
from jax import lax
from jax.experimental import pallas as pl
from jax.experimental.pallas import tpu as pltpu
from jax.sharding import PartitionSpec as P

SMOOTH = 17
LANES = 128
WATER = 0.05
SRC_STEP = 16
SLOTS = 3


def room(mib):
    return pltpu.CompilerParams(vmem_limit_bytes=mib * 1024 * 1024)


def split_kernel(spectra_ref, flags_ref, piece_ref):
    _, win, ch, freq = spectra_ref.shape
    tiles = freq // LANES
    extra = piece_ref.shape[1] - 2 * ch
    for w in range(win):
        flags = jnp.broadcast_to(flags_ref[w : w + 1, :], (extra, ch)).astype(jnp.float32)
        for t in range(tiles):
            at = slice(t * LANES, (t + 1) * LANES)
            piece_ref[t * win + w, :ch] = spectra_ref[0, w, :, at]
            piece_ref[t * win + w, ch : 2 * ch] = spectra_ref[1, w, :, at]
            piece_ref[t * win + w, 2 * ch :] = jnp.zeros((extra, LANES), jnp.bfloat16)
            piece_ref[t * win + w, 2 * ch :, :ch] = flags.astype(jnp.bfloat16)


def prep_kernel(
    bank_ref, bins_ref, flags_ref, offset_ref, weight_ref, band_ref, index_ref, valid_ref, pick_ref, padded_ref
):
    _, banks, taps = bank_ref.shape
    half = weight_ref.shape[0] // 2
    ch = half // (2 * banks)
    index_ref[...] = bins_ref[...]
    channel = lax.broadcasted_iota(jnp.int32, (ch, ch), 0)
    for r in range(offset_ref.shape[0]):
        picked = channel == offset_ref[r : r + 1, :]
        pick_ref[r] = jnp.where(picked, 1.0, 0.0).astype(jnp.bfloat16)
    for w in range(flags_ref.shape[0]):
        column = flag_column(flags_ref[w : w + 1, :])
        valid_ref[w * ch : (w + 1) * ch, :] = jnp.broadcast_to(column, (ch, LANES))
    padded_ref[...] = jnp.zeros(padded_ref.shape, jnp.float32)
    padded_ref[:, :, :taps] = bank_ref[...]

    def skewed(row):
        tile = jnp.broadcast_to(row, (ch, LANES))
        return pltpu.roll(tile, 0, 1, stride=1, stride_axis=0)

    for b in range(banks):
        real = skewed(padded_ref[0, b : b + 1, :])
        imag = skewed(padded_ref[1, b : b + 1, :])
        base = b * 2 * ch
        for row, left, right in ((base, real, -imag), (base + ch, imag, real)):
            for col, val in ((0, left), (LANES, right)):
                high = val.astype(jnp.bfloat16)
                low = (val - high.astype(jnp.float32)).astype(jnp.bfloat16)
                weight_ref[row : row + ch, col : col + LANES] = high
                weight_ref[half + row : half + row + ch, col : col + LANES] = low
    rows = lax.broadcasted_iota(jnp.int32, band_ref.shape, 0)
    cols = lax.broadcasted_iota(jnp.int32, band_ref.shape, 1)
    near = jnp.abs(rows - cols) <= SMOOTH // 2
    band_ref[...] = jnp.where(near, 1.0, 0.0).astype(jnp.bfloat16)


def flag_column(row):
    ch = row.shape[1]
    rows = lax.broadcasted_iota(jnp.int32, (ch, ch), 0)
    cols = lax.broadcasted_iota(jnp.int32, (ch, ch), 1)
    return jnp.sum(jnp.where(rows == cols, row.astype(jnp.float32), 0.0), axis=1, keepdims=True)


def filtered_block(x, weight_ref, index, ch):
    half = weight_ref.shape[0] // 2
    y = jnp.dot(weight_ref[...], x, preferred_element_type=jnp.float32)
    rows = 2 * ch
    pick = y[:rows] + y[half : half + rows]
    for at in range(rows, half, rows):
        here = y[at : at + rows] + y[half + at : half + at + rows]
        pick = jnp.where(index == at // rows, here, pick)
    return pick


def running_scale(real, imag, band_ref):
    count = real.shape[0]
    power = real * real + imag * imag
    high = power.astype(jnp.bfloat16)
    low = (power - high.astype(jnp.float32)).astype(jnp.bfloat16)
    both = jnp.concatenate([high, low], axis=0)
    total = jnp.dot(both, band_ref[...], preferred_element_type=jnp.float32)
    return lax.rsqrt((total[:count] + total[count:]) * (1.0 / SMOOTH) + WATER)


def source_kernel(params_ref, x_ref, weight_ref, index_ref, out_ref, *, win):
    n_chan = x_ref.shape[0]
    _, rounds, _, ch, _ = out_ref.shape
    tile = lax.div(params_ref[0] + pl.program_id(0), win)
    zero = jnp.zeros((), jnp.bfloat16)
    gap = jnp.zeros((LANES - 3 * ch, LANES), jnp.bfloat16)
    columns = []
    for r in range(rounds):
        block = params_ref[2 + r]
        before = jnp.maximum(block - 1, 0)
        after = jnp.minimum(block + 1, n_chan - 1)
        parts = []
        for p in range(2):
            at = slice(p * ch, (p + 1) * ch)
            parts.append(jnp.where(block > 0, x_ref[before, 0, at], zero))
            parts.append(x_ref[block, 0, at])
            parts.append(jnp.where(block < n_chan - 1, x_ref[after, 0, at], zero))
            parts.append(gap)
        columns.append(jnp.concatenate(parts, axis=0))
    x = jnp.concatenate(columns, axis=1)
    index = jnp.concatenate([index_ref[tile]] * rounds, axis=1)
    pick = filtered_block(x, weight_ref, index, ch)
    for r in range(rounds):
        flags = x_ref[params_ref[2 + r], 0, 2 * ch :].astype(jnp.float32)[:1, :ch]
        valid = flag_column(flags)
        for p in range(2):
            part = pick[p * ch : (p + 1) * ch, r * LANES : (r + 1) * LANES] * valid
            out_ref[0, r, p] = part.astype(jnp.bfloat16)


def own_kernel(prev_ref, cur_ref, next_ref, weight_ref, band_ref, index_ref, valid_ref, out_ref, filt_ref):
    _, win, ch, freq = cur_ref.shape
    tiles = freq // LANES
    gap = jnp.zeros((LANES - 3 * ch, freq), jnp.bfloat16)
    index = jnp.concatenate([index_ref[t] for t in range(tiles)], axis=1)

    def one_window(w, _):
        parts = []
        for p in range(2):
            parts += [prev_ref[p, w], cur_ref[p, w], next_ref[p, w], gap]
        x = jnp.concatenate(parts, axis=0)
        pick = filtered_block(x, weight_ref, index, ch)
        at = pl.ds(pl.multiple_of(w * ch, ch), ch)
        filt_ref[0, at, :] = pick[:ch]
        filt_ref[1, at, :] = pick[ch:]
        return 0

    lax.fori_loop(0, win, one_window, 0)
    valid = jnp.concatenate([valid_ref[...]] * tiles, axis=1)
    scale = running_scale(filt_ref[0], filt_ref[1], band_ref) * valid
    for p in range(2):
        white = (filt_ref[p] * scale).astype(jnp.bfloat16)
        for t in range(tiles):
            for w in range(win):
                out_ref[p, t, w] = white[w * ch : (w + 1) * ch, t * LANES : (t + 1) * LANES]


def column_kernel(params_ref, *refs, win):
    band_ref, pick_ref, out_ref, piece_ref = refs[-4:]
    parts = refs[:-4]
    tiles, rounds, _, ch, _ = piece_ref.shape
    if len(parts) == tiles:
        place = params_ref[1]
        for k, ref in enumerate(parts):
            piece_ref[place ^ k] = ref[0]
    else:
        piece_ref[...] = parts[0][:, 0]
    both = []
    for p in range(2):
        rows = []
        for r in range(rounds):
            row = jnp.concatenate([piece_ref[t, r, p] for t in range(tiles)], axis=1)
            rows.append(
                lax.dot_general(
                    pick_ref[r], row, (((0,), (0,)), ((), ())), preferred_element_type=jnp.float32
                )
            )
        both.append(jnp.concatenate(rows, axis=0))
    scale = running_scale(both[0], both[1], band_ref)
    for p in range(2):
        white = (both[p] * scale).astype(jnp.bfloat16) * jnp.bfloat16(1.0 / win)
        for t in range(tiles):
            for r in range(rounds):
                out_ref[0, t, r, p] = white[r * ch : (r + 1) * ch, t * LANES : (t + 1) * LANES]


def spread_row(block, j, ch):
    return jnp.broadcast_to(block[j : j + 1, :], (ch, block.shape[1]))


def pairwise(terms):
    while len(terms) > 1:
        half = (len(terms) + 1) // 2
        terms = [terms[i] + terms[i + half] if i + half < len(terms) else terms[i] for i in range(half)]
    return terms[0]


def cross_kernel(params_ref, *refs, masks, added, final):
    column_refs = refs[: len(masks)]
    local_ref = refs[len(masks)]
    partial_ref = refs[len(masks) + 1]
    if final:
        out_ref, stage_ref, sems = refs[-3:]
    else:
        out_ref = refs[-1]
    tiles, win, ch = local_ref.shape[1:4]
    rounds = column_refs[0].shape[2]
    group = SRC_STEP
    per_round = ch // group
    steps = rounds * per_round
    step = pl.program_id(0)
    r = step // per_round
    begin = step * group
    rows = pl.ds(pl.multiple_of(lax.rem(step, per_round) * group, group), group)
    here = lax.rem(params_ref[0], win)
    slot = lax.rem(step, SLOTS)

    def copies(at_step):
        at_slot = lax.rem(at_step, SLOTS)
        return [
            pltpu.make_async_copy(
                stage_ref.at[at_slot, p], out_ref.at[p, pl.ds(at_step * group, group)], sems.at[at_slot, p]
            )
            for p in range(2)
        ]

    if final:

        @pl.when(step >= SLOTS)
        def _():
            for copy in copies(step - SLOTS):
                copy.wait()

    def one_tile(ft, _):
        at = pl.ds(pl.multiple_of(ft * LANES, LANES), LANES)
        mine = [(local_ref[0, ft, here ^ mask], local_ref[1, ft, here ^ mask]) for mask in masks]
        theirs = [(ref[0, ft, r, 0, rows, :], ref[0, ft, r, 1, rows, :]) for ref in column_refs]
        for j in range(group):
            re = []
            im = []
            for (lr, li), block in zip(mine, theirs):
                sr, si = (spread_row(part, j, ch) for part in block)
                re.append(sr * lr + si * li)
                im.append(sr * li - si * lr)
            re = pairwise(re)
            im = pairwise(im)
            if added:
                re = re + partial_ref[0, begin + j, ft]
                im = im + partial_ref[1, begin + j, ft]
            if final:
                stage_ref[slot, 0, j, :, at] = re
                stage_ref[slot, 1, j, :, at] = im
            else:
                out_ref[0, begin + j, ft] = re
                out_ref[1, begin + j, ft] = im
        return 0

    lax.fori_loop(0, tiles, one_tile, 0)

    if final:
        for copy in copies(step):
            copy.start()

        @pl.when(step == steps - 1)
        def _():
            for back in range(SLOTS):
                for copy in copies(step - back):
                    copy.wait()


def swap(x, mask, n_chan):
    return lax.ppermute(x, "chan", [(i, i ^ mask) for i in range(n_chan)])


def body(spectra, filter_bank, band_index, window_mask, owner_order, source_offset):
    n_chan = lax.axis_size("chan")
    me = lax.axis_index("chan").astype(jnp.int32)
    _, win, ch, freq = spectra.shape
    banks, taps = filter_bank.shape[1:]
    rounds = owner_order.shape[0]
    count = win * ch
    tiles = freq // LANES
    pieces = win * tiles
    sources = rounds * ch
    in_parts = n_chan == pieces and win == 4 and tiles & (tiles - 1) == 0
    smem = pl.BlockSpec(memory_space=pltpu.SMEM)
    vmem = pl.BlockSpec(memory_space=pltpu.VMEM)

    split = pl.pallas_call(
        split_kernel,
        out_shape=jax.ShapeDtypeStruct((pieces, 2 * ch + 16, LANES), jnp.bfloat16),
        compiler_params=room(56),
        name="split",
    )(spectra, window_mask)
    if in_parts:
        held = lax.all_to_all(split, "chan", 0, 0)[:, None]
        first = me
    else:
        held = lax.all_gather(split, "chan")
        first = jnp.int32(0)
    params = jnp.concatenate([first[None], lax.div(first, jnp.int32(win))[None], owner_order])

    ends = n_chan - 1
    before = lax.ppermute(spectra, "chan", [(i, i + 1) for i in range(ends)])
    after = lax.ppermute(spectra, "chan", [(i + 1, i) for i in range(ends)])
    held, before, after = lax.optimization_barrier((held, before, after))

    weight, band, index, valid, pick = pl.pallas_call(
        prep_kernel,
        out_shape=(
            jax.ShapeDtypeStruct((2 * banks * 2 * ch, 2 * LANES), jnp.bfloat16),
            jax.ShapeDtypeStruct((freq, freq), jnp.bfloat16),
            jax.ShapeDtypeStruct((tiles, 1, LANES), jnp.int32),
            jax.ShapeDtypeStruct((count, LANES), jnp.float32),
            jax.ShapeDtypeStruct((rounds, ch, ch), jnp.bfloat16),
        ),
        scratch_shapes=[pltpu.VMEM((2, banks, LANES), jnp.float32)],
        compiler_params=room(8),
        name="prep",
    )(filter_bank, band_index.reshape(tiles, 1, LANES), window_mask, source_offset)

    count_here = held.shape[1]
    filtered = pl.pallas_call(
        functools.partial(source_kernel, win=win),
        grid=(count_here,),
        in_specs=[
            smem,
            pl.BlockSpec((n_chan, 1, 2 * ch + 16, LANES), lambda s: (0, s, 0, 0)),
            vmem,
            vmem,
        ],
        out_specs=pl.BlockSpec((1, rounds, 2, ch, LANES), lambda s: (s, 0, 0, 0, 0)),
        out_shape=jax.ShapeDtypeStruct((count_here, rounds, 2, ch, LANES), jnp.bfloat16),
        compiler_params=room(16),
        name="source_filter",
    )(params, held, weight, index)

    if in_parts:
        zparts = [filtered] + [swap(filtered, win * k, n_chan) for k in range(1, tiles)]

    local = pl.pallas_call(
        own_kernel,
        out_shape=jax.ShapeDtypeStruct((2, tiles, win, ch, LANES), jnp.bfloat16),
        in_specs=[vmem] * 7,
        out_specs=vmem,
        scratch_shapes=[pltpu.VMEM((2, count, freq), jnp.float32)],
        compiler_params=room(16),
        cost_estimate=pl.CostEstimate(
            flops=4 * banks * 2 * ch * 2 * LANES * win * freq, bytes_accessed=3 << 20, transcendentals=0
        ),
        name="own_whiten",
    )(before, spectra, after, weight, band, index, valid)

    shape = (tiles, rounds, 2, ch, LANES)
    if in_parts:
        zparts[-1], local = lax.optimization_barrier((zparts[-1], local))
        windows = 1
        specs = [vmem] * tiles
    else:
        windows = win
        zparts = [filtered.reshape((tiles, win) + shape[1:])]
        specs = [pl.BlockSpec((tiles, 1) + shape[1:], lambda s: (0, s, 0, 0, 0, 0))]
    column = pl.pallas_call(
        functools.partial(column_kernel, win=win),
        grid=(windows,),
        in_specs=[smem] + specs + [vmem, vmem],
        out_specs=pl.BlockSpec((1,) + shape, lambda s: (s, 0, 0, 0, 0, 0)),
        out_shape=jax.ShapeDtypeStruct((windows,) + shape, jnp.bfloat16),
        scratch_shapes=[pltpu.VMEM(shape, jnp.bfloat16)],
        compiler_params=room(16),
        name="column_whiten",
    )(params, *zparts, band, pick)

    def cross(masks, columns, earlier, final):
        group = SRC_STEP
        scratch = []
        spec = vmem
        result = jax.ShapeDtypeStruct((2, sources, tiles, ch, LANES), jnp.bfloat16)
        if final:
            spec = pl.BlockSpec(memory_space=pl.ANY)
            result = jax.ShapeDtypeStruct((2, sources, ch, freq), jnp.bfloat16)
            scratch.append(pltpu.VMEM((SLOTS, 2, group, ch, freq), jnp.bfloat16))
            scratch.append(pltpu.SemaphoreType.DMA((SLOTS, 2)))
        return pl.pallas_call(
            functools.partial(cross_kernel, masks=masks, added=len(earlier) > 0, final=final),
            grid=(sources // group,),
            in_specs=[smem] + [vmem] * (len(columns) + 1 + len(earlier)),
            out_specs=spec,
            out_shape=result,
            scratch_shapes=scratch,
            compiler_params=room(32),
            cost_estimate=pl.CostEstimate(
                flops=16 * len(masks) * sources * ch * freq, bytes_accessed=16 << 20, transcendentals=0
            ),
            name="cross",
        )(params, *columns, local, *earlier)

    if not in_parts:
        return cross(tuple(range(win)), [column[w : w + 1] for w in range(win)], [], True)
    far = swap(column, 2, n_chan)
    beside = swap(column, 1, n_chan)
    partial = cross((0, 1), [column, beside], [], False)
    far, partial = lax.optimization_barrier((far, partial))
    return cross((2, 3), [far, swap(far, 1, n_chan)], [partial], True)


def solution(mesh):
    in_specs = (
        P(None, "groups", "chan", None),
        P(),
        P(),
        P("groups", "chan"),
        P("groups"),
        P("groups", None),
    )
    out_specs = P(None, "groups", "chan", None)
    return jax.shard_map(body, mesh=mesh, in_specs=in_specs, out_specs=out_specs, check_vma=False)
```

```python
import functools

import jax
import jax.numpy as jnp
from jax import lax
from jax.experimental import pallas as pl
from jax.experimental.pallas import tpu as pltpu
from jax.sharding import PartitionSpec as P

SMOOTH = 17
LANES = 128
WATER = 0.05
SRC_STEP = 16
SLOTS = 3


def room(mib):
    return pltpu.CompilerParams(vmem_limit_bytes=mib * 1024 * 1024)


def split_kernel(spectra_ref, flags_ref, piece_ref):
    _, win, ch, freq = spectra_ref.shape
    tiles = freq // LANES
    extra = piece_ref.shape[1] - 2 * ch
    for w in range(win):
        flags = jnp.broadcast_to(flags_ref[w : w + 1, :], (extra, ch)).astype(jnp.float32)
        for t in range(tiles):
            at = slice(t * LANES, (t + 1) * LANES)
            piece_ref[t * win + w, :ch] = spectra_ref[0, w, :, at]
            piece_ref[t * win + w, ch : 2 * ch] = spectra_ref[1, w, :, at]
            piece_ref[t * win + w, 2 * ch :] = jnp.zeros((extra, LANES), jnp.bfloat16)
            piece_ref[t * win + w, 2 * ch :, :ch] = flags.astype(jnp.bfloat16)


def prep_kernel(
    bank_ref, bins_ref, flags_ref, offset_ref, weight_ref, band_ref, index_ref, valid_ref, pick_ref, padded_ref
):
    _, banks, taps = bank_ref.shape
    half = weight_ref.shape[0] // 2
    ch = half // (2 * banks)
    index_ref[...] = bins_ref[...]
    channel = lax.broadcasted_iota(jnp.int32, (ch, ch), 0)
    for r in range(offset_ref.shape[0]):
        picked = channel == offset_ref[r : r + 1, :]
        pick_ref[r] = jnp.where(picked, 1.0, 0.0).astype(jnp.bfloat16)
    for w in range(flags_ref.shape[0]):
        column = flag_column(flags_ref[w : w + 1, :])
        valid_ref[w * ch : (w + 1) * ch, :] = jnp.broadcast_to(column, (ch, LANES))
    padded_ref[...] = jnp.zeros(padded_ref.shape, jnp.float32)
    padded_ref[:, :, :taps] = bank_ref[...]

    def skewed(row):
        tile = jnp.broadcast_to(row, (ch, LANES))
        return pltpu.roll(tile, 0, 1, stride=1, stride_axis=0)

    for b in range(banks):
        real = skewed(padded_ref[0, b : b + 1, :])
        imag = skewed(padded_ref[1, b : b + 1, :])
        base = b * 2 * ch
        for row, left, right in ((base, real, -imag), (base + ch, imag, real)):
            for col, val in ((0, left), (LANES, right)):
                high = val.astype(jnp.bfloat16)
                low = (val - high.astype(jnp.float32)).astype(jnp.bfloat16)
                weight_ref[row : row + ch, col : col + LANES] = high
                weight_ref[half + row : half + row + ch, col : col + LANES] = low
    rows = lax.broadcasted_iota(jnp.int32, band_ref.shape, 0)
    cols = lax.broadcasted_iota(jnp.int32, band_ref.shape, 1)
    near = jnp.abs(rows - cols) <= SMOOTH // 2
    band_ref[...] = jnp.where(near, 1.0, 0.0).astype(jnp.bfloat16)


def flag_column(row):
    ch = row.shape[1]
    rows = lax.broadcasted_iota(jnp.int32, (ch, ch), 0)
    cols = lax.broadcasted_iota(jnp.int32, (ch, ch), 1)
    return jnp.sum(jnp.where(rows == cols, row.astype(jnp.float32), 0.0), axis=1, keepdims=True)


def filtered_block(x, weight_ref, index, ch):
    half = weight_ref.shape[0] // 2
    y = jnp.dot(weight_ref[...], x, preferred_element_type=jnp.float32)
    rows = 2 * ch
    pick = y[:rows] + y[half : half + rows]
    for at in range(rows, half, rows):
        here = y[at : at + rows] + y[half + at : half + at + rows]
        pick = jnp.where(index == at // rows, here, pick)
    return pick


def running_scale(real, imag, band_ref):
    count = real.shape[0]
    power = real * real + imag * imag
    high = power.astype(jnp.bfloat16)
    low = (power - high.astype(jnp.float32)).astype(jnp.bfloat16)
    both = jnp.concatenate([high, low], axis=0)
    total = jnp.dot(both, band_ref[...], preferred_element_type=jnp.float32)
    return lax.rsqrt((total[:count] + total[count:]) * (1.0 / SMOOTH) + WATER)


def source_kernel(params_ref, x_ref, weight_ref, index_ref, out_ref, *, win):
    n_chan = x_ref.shape[0]
    _, rounds, _, ch, _ = out_ref.shape
    tile = lax.div(params_ref[0] + pl.program_id(0), win)
    zero = jnp.zeros((), jnp.bfloat16)
    gap = jnp.zeros((LANES - 3 * ch, LANES), jnp.bfloat16)
    columns = []
    for r in range(rounds):
        block = params_ref[2 + r]
        before = jnp.maximum(block - 1, 0)
        after = jnp.minimum(block + 1, n_chan - 1)
        parts = []
        for p in range(2):
            at = slice(p * ch, (p + 1) * ch)
            parts.append(jnp.where(block > 0, x_ref[before, 0, at], zero))
            parts.append(x_ref[block, 0, at])
            parts.append(jnp.where(block < n_chan - 1, x_ref[after, 0, at], zero))
            parts.append(gap)
        columns.append(jnp.concatenate(parts, axis=0))
    x = jnp.concatenate(columns, axis=1)
    index = jnp.concatenate([index_ref[tile]] * rounds, axis=1)
    pick = filtered_block(x, weight_ref, index, ch)
    for r in range(rounds):
        flags = x_ref[params_ref[2 + r], 0, 2 * ch :].astype(jnp.float32)[:1, :ch]
        valid = flag_column(flags)
        for p in range(2):
            part = pick[p * ch : (p + 1) * ch, r * LANES : (r + 1) * LANES] * valid
            out_ref[0, r, p] = part.astype(jnp.bfloat16)


def own_kernel(prev_ref, cur_ref, next_ref, weight_ref, band_ref, index_ref, valid_ref, out_ref, filt_ref):
    _, win, ch, freq = cur_ref.shape
    tiles = freq // LANES
    gap = jnp.zeros((LANES - 3 * ch, freq), jnp.bfloat16)
    index = jnp.concatenate([index_ref[t] for t in range(tiles)], axis=1)

    def one_window(w, _):
        parts = []
        for p in range(2):
            parts += [prev_ref[p, w], cur_ref[p, w], next_ref[p, w], gap]
        x = jnp.concatenate(parts, axis=0)
        pick = filtered_block(x, weight_ref, index, ch)
        at = pl.ds(pl.multiple_of(w * ch, ch), ch)
        filt_ref[0, at, :] = pick[:ch]
        filt_ref[1, at, :] = pick[ch:]
        return 0

    lax.fori_loop(0, win, one_window, 0)
    valid = jnp.concatenate([valid_ref[...]] * tiles, axis=1)
    scale = running_scale(filt_ref[0], filt_ref[1], band_ref) * valid
    for p in range(2):
        white = (filt_ref[p] * scale).astype(jnp.bfloat16)
        for t in range(tiles):
            for w in range(win):
                out_ref[p, t, w] = white[w * ch : (w + 1) * ch, t * LANES : (t + 1) * LANES]


def column_kernel(params_ref, *refs, win):
    band_ref, pick_ref, out_ref, piece_ref = refs[-4:]
    parts = refs[:-4]
    tiles, rounds, _, ch, _ = piece_ref.shape
    if len(parts) == tiles:
        place = params_ref[1]
        for k, ref in enumerate(parts):
            piece_ref[place ^ k] = ref[0]
    else:
        piece_ref[...] = parts[0][:, 0]
    both = []
    for p in range(2):
        rows = []
        for r in range(rounds):
            row = jnp.concatenate([piece_ref[t, r, p] for t in range(tiles)], axis=1)
            rows.append(
                lax.dot_general(
                    pick_ref[r], row, (((0,), (0,)), ((), ())), preferred_element_type=jnp.float32
                )
            )
        both.append(jnp.concatenate(rows, axis=0))
    scale = running_scale(both[0], both[1], band_ref)
    for p in range(2):
        white = (both[p] * scale).astype(jnp.bfloat16) * jnp.bfloat16(1.0 / win)
        for t in range(tiles):
            for r in range(rounds):
                out_ref[0, t, r, p] = white[r * ch : (r + 1) * ch, t * LANES : (t + 1) * LANES]


def spread_row(block, j, ch):
    return jnp.broadcast_to(block[j : j + 1, :], (ch, block.shape[1]))


def pairwise(terms):
    while len(terms) > 1:
        half = (len(terms) + 1) // 2
        terms = [terms[i] + terms[i + half] if i + half < len(terms) else terms[i] for i in range(half)]
    return terms[0]


def cross_kernel(params_ref, *refs, masks, added, final):
    column_refs = refs[: len(masks)]
    local_ref = refs[len(masks)]
    partial_ref = refs[len(masks) + 1]
    if final:
        out_ref, stage_ref, sems = refs[-3:]
    else:
        out_ref = refs[-1]
    tiles, win, ch = local_ref.shape[1:4]
    rounds = column_refs[0].shape[2]
    group = SRC_STEP
    per_round = ch // group
    steps = rounds * per_round
    step = pl.program_id(0)
    r = step // per_round
    begin = step * group
    rows = pl.ds(pl.multiple_of(lax.rem(step, per_round) * group, group), group)
    here = lax.rem(params_ref[0], win)
    slot = lax.rem(step, SLOTS)

    def copies(at_step):
        at_slot = lax.rem(at_step, SLOTS)
        return [
            pltpu.make_async_copy(
                stage_ref.at[at_slot, p], out_ref.at[p, pl.ds(at_step * group, group)], sems.at[at_slot, p]
            )
            for p in range(2)
        ]

    if final:

        @pl.when(step >= SLOTS)
        def _():
            for copy in copies(step - SLOTS):
                copy.wait()

    def one_tile(ft, _):
        at = pl.ds(pl.multiple_of(ft * LANES, LANES), LANES)
        mine = [(local_ref[0, ft, here ^ mask], local_ref[1, ft, here ^ mask]) for mask in masks]
        theirs = [(ref[0, ft, r, 0, rows, :], ref[0, ft, r, 1, rows, :]) for ref in column_refs]
        for j in range(group):
            re = []
            im = []
            for (lr, li), block in zip(mine, theirs):
                sr, si = (spread_row(part, j, ch) for part in block)
                re.append(sr * lr + si * li)
                im.append(sr * li - si * lr)
            re = pairwise(re)
            im = pairwise(im)
            if added:
                re = re + partial_ref[0, begin + j, ft]
                im = im + partial_ref[1, begin + j, ft]
            if final:
                stage_ref[slot, 0, j, :, at] = re
                stage_ref[slot, 1, j, :, at] = im
            else:
                out_ref[0, begin + j, ft] = re
                out_ref[1, begin + j, ft] = im
        return 0

    lax.fori_loop(0, tiles, one_tile, 0)

    if final:
        for copy in copies(step):
            copy.start()

        @pl.when(step == steps - 1)
        def _():
            for back in range(SLOTS):
                for copy in copies(step - back):
                    copy.wait()


def swap(x, mask, n_chan):
    return lax.ppermute(x, "chan", [(i, i ^ mask) for i in range(n_chan)])


def body(spectra, filter_bank, band_index, window_mask, owner_order, source_offset):
    n_chan = lax.axis_size("chan")
    me = lax.axis_index("chan").astype(jnp.int32)
    _, win, ch, freq = spectra.shape
    banks, taps = filter_bank.shape[1:]
    rounds = owner_order.shape[0]
    count = win * ch
    tiles = freq // LANES
    pieces = win * tiles
    sources = rounds * ch
    in_parts = n_chan == pieces and win == 4 and tiles & (tiles - 1) == 0
    smem = pl.BlockSpec(memory_space=pltpu.SMEM)
    vmem = pl.BlockSpec(memory_space=pltpu.VMEM)

    split = pl.pallas_call(
        split_kernel,
        out_shape=jax.ShapeDtypeStruct((pieces, 2 * ch + 16, LANES), jnp.bfloat16),
        compiler_params=room(56),
        name="split",
    )(spectra, window_mask)
    if in_parts:
        held = lax.all_to_all(split, "chan", 0, 0)[:, None]
        first = me
    else:
        held = lax.all_gather(split, "chan")
        first = jnp.int32(0)
    params = jnp.concatenate([first[None], lax.div(first, jnp.int32(win))[None], owner_order])

    ends = n_chan - 1
    before = lax.ppermute(spectra, "chan", [(i, i + 1) for i in range(ends)])
    after = lax.ppermute(spectra, "chan", [(i + 1, i) for i in range(ends)])
    held, before = lax.optimization_barrier((held, before))

    weight, band, index, valid, pick = pl.pallas_call(
        prep_kernel,
        out_shape=(
            jax.ShapeDtypeStruct((2 * banks * 2 * ch, 2 * LANES), jnp.bfloat16),
            jax.ShapeDtypeStruct((freq, freq), jnp.bfloat16),
            jax.ShapeDtypeStruct((tiles, 1, LANES), jnp.int32),
            jax.ShapeDtypeStruct((count, LANES), jnp.float32),
            jax.ShapeDtypeStruct((rounds, ch, ch), jnp.bfloat16),
        ),
        scratch_shapes=[pltpu.VMEM((2, banks, LANES), jnp.float32)],
        compiler_params=room(8),
        name="prep",
    )(filter_bank, band_index.reshape(tiles, 1, LANES), window_mask, source_offset)

    count_here = held.shape[1]
    filtered = pl.pallas_call(
        functools.partial(source_kernel, win=win),
        grid=(count_here,),
        in_specs=[
            smem,
            pl.BlockSpec((n_chan, 1, 2 * ch + 16, LANES), lambda s: (0, s, 0, 0)),
            vmem,
            vmem,
        ],
        out_specs=pl.BlockSpec((1, rounds, 2, ch, LANES), lambda s: (s, 0, 0, 0, 0)),
        out_shape=jax.ShapeDtypeStruct((count_here, rounds, 2, ch, LANES), jnp.bfloat16),
        compiler_params=room(16),
        name="source_filter",
    )(params, held, weight, index)

    if in_parts:
        zparts = [filtered] + [swap(filtered, win * k, n_chan) for k in range(1, tiles)]

    local = pl.pallas_call(
        own_kernel,
        out_shape=jax.ShapeDtypeStruct((2, tiles, win, ch, LANES), jnp.bfloat16),
        in_specs=[vmem] * 7,
        out_specs=vmem,
        scratch_shapes=[pltpu.VMEM((2, count, freq), jnp.float32)],
        compiler_params=room(16),
        cost_estimate=pl.CostEstimate(
            flops=4 * banks * 2 * ch * 2 * LANES * win * freq, bytes_accessed=3 << 20, transcendentals=0
        ),
        name="own_whiten",
    )(before, spectra, after, weight, band, index, valid)

    shape = (tiles, rounds, 2, ch, LANES)
    if in_parts:
        zparts[-1], local = lax.optimization_barrier((zparts[-1], local))
        windows = 1
        specs = [vmem] * tiles
    else:
        windows = win
        zparts = [filtered.reshape((tiles, win) + shape[1:])]
        specs = [pl.BlockSpec((tiles, 1) + shape[1:], lambda s: (0, s, 0, 0, 0, 0))]
    column = pl.pallas_call(
        functools.partial(column_kernel, win=win),
        grid=(windows,),
        in_specs=[smem] + specs + [vmem, vmem],
        out_specs=pl.BlockSpec((1,) + shape, lambda s: (s, 0, 0, 0, 0, 0)),
        out_shape=jax.ShapeDtypeStruct((windows,) + shape, jnp.bfloat16),
        scratch_shapes=[pltpu.VMEM(shape, jnp.bfloat16)],
        compiler_params=room(16),
        name="column_whiten",
    )(params, *zparts, band, pick)

    def cross(masks, columns, earlier, final):
        group = SRC_STEP
        scratch = []
        spec = vmem
        result = jax.ShapeDtypeStruct((2, sources, tiles, ch, LANES), jnp.bfloat16)
        if final:
            spec = pl.BlockSpec(memory_space=pl.ANY)
            result = jax.ShapeDtypeStruct((2, sources, ch, freq), jnp.bfloat16)
            scratch.append(pltpu.VMEM((SLOTS, 2, group, ch, freq), jnp.bfloat16))
            scratch.append(pltpu.SemaphoreType.DMA((SLOTS, 2)))
        return pl.pallas_call(
            functools.partial(cross_kernel, masks=masks, added=len(earlier) > 0, final=final),
            grid=(sources // group,),
            in_specs=[smem] + [vmem] * (len(columns) + 1 + len(earlier)),
            out_specs=spec,
            out_shape=result,
            scratch_shapes=scratch,
            compiler_params=room(32),
            cost_estimate=pl.CostEstimate(
                flops=16 * len(masks) * sources * ch * freq, bytes_accessed=16 << 20, transcendentals=0
            ),
            name="cross",
        )(params, *columns, local, *earlier)

    if not in_parts:
        return cross(tuple(range(win)), [column[w : w + 1] for w in range(win)], [], True)
    far = swap(column, 2, n_chan)
    beside = swap(column, 1, n_chan)
    partial = cross((0, 1), [column, beside], [], False)
    far, partial = lax.optimization_barrier((far, partial))
    return cross((2, 3), [far, swap(far, 1, n_chan)], [partial], True)


def solution(mesh):
    in_specs = (
        P(None, "groups", "chan", None),
        P(),
        P(),
        P("groups", "chan"),
        P("groups"),
        P("groups", None),
    )
    out_specs = P(None, "groups", "chan", None)
    return jax.shard_map(body, mesh=mesh, in_specs=in_specs, out_specs=out_specs, check_vma=False)
```

```python
import functools

import jax
import jax.numpy as jnp
from jax import lax
from jax.experimental import pallas as pl
from jax.experimental.pallas import tpu as pltpu
from jax.sharding import PartitionSpec as P

SMOOTH = 17
LANES = 128
WATER = 0.05
SRC_STEP = 16
SLOTS = 3


def room(mib):
    return pltpu.CompilerParams(vmem_limit_bytes=mib * 1024 * 1024)


def split_kernel(spectra_ref, flags_ref, piece_ref):
    _, win, ch, freq = spectra_ref.shape
    tiles = freq // LANES
    extra = piece_ref.shape[1] - 2 * ch
    for w in range(win):
        flags = jnp.broadcast_to(flags_ref[w : w + 1, :], (extra, ch)).astype(jnp.float32)
        for t in range(tiles):
            at = slice(t * LANES, (t + 1) * LANES)
            piece_ref[t * win + w, :ch] = spectra_ref[0, w, :, at]
            piece_ref[t * win + w, ch : 2 * ch] = spectra_ref[1, w, :, at]
            piece_ref[t * win + w, 2 * ch :] = jnp.zeros((extra, LANES), jnp.bfloat16)
            piece_ref[t * win + w, 2 * ch :, :ch] = flags.astype(jnp.bfloat16)


def prep_kernel(
    bank_ref, bins_ref, flags_ref, offset_ref, weight_ref, band_ref, index_ref, valid_ref, pick_ref, padded_ref
):
    _, banks, taps = bank_ref.shape
    half = weight_ref.shape[0] // 2
    ch = half // (2 * banks)
    index_ref[...] = bins_ref[...]
    channel = lax.broadcasted_iota(jnp.int32, (ch, ch), 0)
    for r in range(offset_ref.shape[0]):
        picked = channel == offset_ref[r : r + 1, :]
        pick_ref[r] = jnp.where(picked, 1.0, 0.0).astype(jnp.bfloat16)
    for w in range(flags_ref.shape[0]):
        column = flag_column(flags_ref[w : w + 1, :])
        valid_ref[w * ch : (w + 1) * ch, :] = jnp.broadcast_to(column, (ch, LANES))
    padded_ref[...] = jnp.zeros(padded_ref.shape, jnp.float32)
    padded_ref[:, :, :taps] = bank_ref[...]

    def skewed(row):
        tile = jnp.broadcast_to(row, (ch, LANES))
        return pltpu.roll(tile, 0, 1, stride=1, stride_axis=0)

    for b in range(banks):
        real = skewed(padded_ref[0, b : b + 1, :])
        imag = skewed(padded_ref[1, b : b + 1, :])
        base = b * 2 * ch
        for row, left, right in ((base, real, -imag), (base + ch, imag, real)):
            for col, val in ((0, left), (LANES, right)):
                high = val.astype(jnp.bfloat16)
                low = (val - high.astype(jnp.float32)).astype(jnp.bfloat16)
                weight_ref[row : row + ch, col : col + LANES] = high
                weight_ref[half + row : half + row + ch, col : col + LANES] = low
    rows = lax.broadcasted_iota(jnp.int32, band_ref.shape, 0)
    cols = lax.broadcasted_iota(jnp.int32, band_ref.shape, 1)
    near = jnp.abs(rows - cols) <= SMOOTH // 2
    band_ref[...] = jnp.where(near, 1.0, 0.0).astype(jnp.bfloat16)


def flag_column(row):
    ch = row.shape[1]
    rows = lax.broadcasted_iota(jnp.int32, (ch, ch), 0)
    cols = lax.broadcasted_iota(jnp.int32, (ch, ch), 1)
    return jnp.sum(jnp.where(rows == cols, row.astype(jnp.float32), 0.0), axis=1, keepdims=True)


def filtered_block(x, weight_ref, index, ch):
    half = weight_ref.shape[0] // 2
    y = jnp.dot(weight_ref[...], x, preferred_element_type=jnp.float32)
    rows = 2 * ch
    pick = y[:rows] + y[half : half + rows]
    for at in range(rows, half, rows):
        here = y[at : at + rows] + y[half + at : half + at + rows]
        pick = jnp.where(index == at // rows, here, pick)
    return pick


def running_scale(real, imag, band_ref):
    count = real.shape[0]
    power = real * real + imag * imag
    high = power.astype(jnp.bfloat16)
    low = (power - high.astype(jnp.float32)).astype(jnp.bfloat16)
    both = jnp.concatenate([high, low], axis=0)
    total = jnp.dot(both, band_ref[...], preferred_element_type=jnp.float32)
    return lax.rsqrt((total[:count] + total[count:]) * (1.0 / SMOOTH) + WATER)


def source_kernel(params_ref, x_ref, weight_ref, index_ref, out_ref, *, win):
    n_chan = x_ref.shape[0]
    _, rounds, _, ch, _ = out_ref.shape
    tile = lax.div(params_ref[0] + pl.program_id(0), win)
    zero = jnp.zeros((), jnp.bfloat16)
    gap = jnp.zeros((LANES - 3 * ch, LANES), jnp.bfloat16)
    columns = []
    for r in range(rounds):
        block = params_ref[2 + r]
        before = jnp.maximum(block - 1, 0)
        after = jnp.minimum(block + 1, n_chan - 1)
        parts = []
        for p in range(2):
            at = slice(p * ch, (p + 1) * ch)
            parts.append(jnp.where(block > 0, x_ref[before, 0, at], zero))
            parts.append(x_ref[block, 0, at])
            parts.append(jnp.where(block < n_chan - 1, x_ref[after, 0, at], zero))
            parts.append(gap)
        columns.append(jnp.concatenate(parts, axis=0))
    x = jnp.concatenate(columns, axis=1)
    index = jnp.concatenate([index_ref[tile]] * rounds, axis=1)
    pick = filtered_block(x, weight_ref, index, ch)
    for r in range(rounds):
        flags = x_ref[params_ref[2 + r], 0, 2 * ch :].astype(jnp.float32)[:1, :ch]
        valid = flag_column(flags)
        for p in range(2):
            part = pick[p * ch : (p + 1) * ch, r * LANES : (r + 1) * LANES] * valid
            out_ref[0, r, p] = part.astype(jnp.bfloat16)


def own_kernel(prev_ref, cur_ref, next_ref, weight_ref, band_ref, index_ref, valid_ref, out_ref, filt_ref):
    _, win, ch, freq = cur_ref.shape
    tiles = freq // LANES
    gap = jnp.zeros((LANES - 3 * ch, freq), jnp.bfloat16)
    index = jnp.concatenate([index_ref[t] for t in range(tiles)], axis=1)

    def one_window(w, _):
        parts = []
        for p in range(2):
            parts += [prev_ref[p, w], cur_ref[p, w], next_ref[p, w], gap]
        x = jnp.concatenate(parts, axis=0)
        pick = filtered_block(x, weight_ref, index, ch)
        at = pl.ds(pl.multiple_of(w * ch, ch), ch)
        filt_ref[0, at, :] = pick[:ch]
        filt_ref[1, at, :] = pick[ch:]
        return 0

    lax.fori_loop(0, win, one_window, 0)
    valid = jnp.concatenate([valid_ref[...]] * tiles, axis=1)
    scale = running_scale(filt_ref[0], filt_ref[1], band_ref) * valid
    for p in range(2):
        white = (filt_ref[p] * scale).astype(jnp.bfloat16)
        for t in range(tiles):
            for w in range(win):
                out_ref[p, t, w] = white[w * ch : (w + 1) * ch, t * LANES : (t + 1) * LANES]


def column_kernel(params_ref, *refs, win):
    band_ref, pick_ref, out_ref, piece_ref = refs[-4:]
    parts = refs[:-4]
    tiles, rounds, _, ch, _ = piece_ref.shape
    if len(parts) == tiles:
        place = params_ref[1]
        for k, ref in enumerate(parts):
            piece_ref[place ^ k] = ref[0]
    else:
        piece_ref[...] = parts[0][:, 0]
    both = []
    for p in range(2):
        rows = []
        for r in range(rounds):
            row = jnp.concatenate([piece_ref[t, r, p] for t in range(tiles)], axis=1)
            rows.append(
                lax.dot_general(
                    pick_ref[r], row, (((0,), (0,)), ((), ())), preferred_element_type=jnp.float32
                )
            )
        both.append(jnp.concatenate(rows, axis=0))
    scale = running_scale(both[0], both[1], band_ref)
    for p in range(2):
        white = (both[p] * scale).astype(jnp.bfloat16) * jnp.bfloat16(1.0 / win)
        for t in range(tiles):
            for r in range(rounds):
                out_ref[0, t, r, p] = white[r * ch : (r + 1) * ch, t * LANES : (t + 1) * LANES]


def spread_row(block, j, ch):
    return jnp.broadcast_to(block[j : j + 1, :], (ch, block.shape[1]))


def pairwise(terms):
    while len(terms) > 1:
        half = (len(terms) + 1) // 2
        terms = [terms[i] + terms[i + half] if i + half < len(terms) else terms[i] for i in range(half)]
    return terms[0]


def cross_kernel(params_ref, *refs, masks, added, final):
    column_refs = refs[: len(masks)]
    local_ref = refs[len(masks)]
    partial_ref = refs[len(masks) + 1]
    if final:
        out_ref, stage_ref, sems = refs[-3:]
    else:
        out_ref = refs[-1]
    tiles, win, ch = local_ref.shape[1:4]
    rounds = column_refs[0].shape[2]
    group = SRC_STEP
    per_round = ch // group
    steps = rounds * per_round
    step = pl.program_id(0)
    r = step // per_round
    begin = step * group
    rows = pl.ds(pl.multiple_of(lax.rem(step, per_round) * group, group), group)
    here = lax.rem(params_ref[0], win)
    slot = lax.rem(step, SLOTS)

    def copies(at_step):
        at_slot = lax.rem(at_step, SLOTS)
        return [
            pltpu.make_async_copy(
                stage_ref.at[at_slot, p], out_ref.at[p, pl.ds(at_step * group, group)], sems.at[at_slot, p]
            )
            for p in range(2)
        ]

    if final:

        @pl.when(step >= SLOTS)
        def _():
            for copy in copies(step - SLOTS):
                copy.wait()

    def one_tile(ft, _):
        at = pl.ds(pl.multiple_of(ft * LANES, LANES), LANES)
        mine = [(local_ref[0, ft, here ^ mask], local_ref[1, ft, here ^ mask]) for mask in masks]
        theirs = [(ref[0, ft, r, 0, rows, :], ref[0, ft, r, 1, rows, :]) for ref in column_refs]
        for j in range(group):
            re = []
            im = []
            for (lr, li), block in zip(mine, theirs):
                sr, si = (spread_row(part, j, ch) for part in block)
                re.append(sr * lr + si * li)
                im.append(sr * li - si * lr)
            re = pairwise(re)
            im = pairwise(im)
            if added:
                re = re + partial_ref[0, begin + j, ft]
                im = im + partial_ref[1, begin + j, ft]
            if final:
                stage_ref[slot, 0, j, :, at] = re
                stage_ref[slot, 1, j, :, at] = im
            else:
                out_ref[0, begin + j, ft] = re
                out_ref[1, begin + j, ft] = im
        return 0

    lax.fori_loop(0, tiles, one_tile, 0)

    if final:
        for copy in copies(step):
            copy.start()

        @pl.when(step == steps - 1)
        def _():
            for back in range(SLOTS):
                for copy in copies(step - back):
                    copy.wait()


def swap(x, mask, n_chan):
    return lax.ppermute(x, "chan", [(i, i ^ mask) for i in range(n_chan)])


def body(spectra, filter_bank, band_index, window_mask, owner_order, source_offset):
    n_chan = lax.axis_size("chan")
    me = lax.axis_index("chan").astype(jnp.int32)
    _, win, ch, freq = spectra.shape
    banks, taps = filter_bank.shape[1:]
    rounds = owner_order.shape[0]
    count = win * ch
    tiles = freq // LANES
    pieces = win * tiles
    sources = rounds * ch
    in_parts = n_chan == pieces and win == 4 and tiles & (tiles - 1) == 0
    smem = pl.BlockSpec(memory_space=pltpu.SMEM)
    vmem = pl.BlockSpec(memory_space=pltpu.VMEM)

    split = pl.pallas_call(
        split_kernel,
        out_shape=jax.ShapeDtypeStruct((pieces, 2 * ch + 16, LANES), jnp.bfloat16),
        compiler_params=room(56),
        name="split",
    )(spectra, window_mask)
    if in_parts:
        held = lax.all_to_all(split, "chan", 0, 0)[:, None]
        first = me
    else:
        held = lax.all_gather(split, "chan")
        first = jnp.int32(0)
    params = jnp.concatenate([first[None], lax.div(first, jnp.int32(win))[None], owner_order])

    ends = n_chan - 1
    before = lax.ppermute(spectra, "chan", [(i, i + 1) for i in range(ends)])
    after = lax.ppermute(spectra, "chan", [(i + 1, i) for i in range(ends)])

    weight, band, index, valid, pick = pl.pallas_call(
        prep_kernel,
        out_shape=(
            jax.ShapeDtypeStruct((2 * banks * 2 * ch, 2 * LANES), jnp.bfloat16),
            jax.ShapeDtypeStruct((freq, freq), jnp.bfloat16),
            jax.ShapeDtypeStruct((tiles, 1, LANES), jnp.int32),
            jax.ShapeDtypeStruct((count, LANES), jnp.float32),
            jax.ShapeDtypeStruct((rounds, ch, ch), jnp.bfloat16),
        ),
        scratch_shapes=[pltpu.VMEM((2, banks, LANES), jnp.float32)],
        compiler_params=room(8),
        name="prep",
    )(filter_bank, band_index.reshape(tiles, 1, LANES), window_mask, source_offset)

    count_here = held.shape[1]
    filtered = pl.pallas_call(
        functools.partial(source_kernel, win=win),
        grid=(count_here,),
        in_specs=[
            smem,
            pl.BlockSpec((n_chan, 1, 2 * ch + 16, LANES), lambda s: (0, s, 0, 0)),
            vmem,
            vmem,
        ],
        out_specs=pl.BlockSpec((1, rounds, 2, ch, LANES), lambda s: (s, 0, 0, 0, 0)),
        out_shape=jax.ShapeDtypeStruct((count_here, rounds, 2, ch, LANES), jnp.bfloat16),
        compiler_params=room(16),
        name="source_filter",
    )(params, held, weight, index)

    if in_parts:
        zparts = [filtered] + [swap(filtered, win * k, n_chan) for k in range(1, tiles)]

    local = pl.pallas_call(
        own_kernel,
        out_shape=jax.ShapeDtypeStruct((2, tiles, win, ch, LANES), jnp.bfloat16),
        in_specs=[vmem] * 7,
        out_specs=vmem,
        scratch_shapes=[pltpu.VMEM((2, count, freq), jnp.float32)],
        compiler_params=room(16),
        cost_estimate=pl.CostEstimate(
            flops=4 * banks * 2 * ch * 2 * LANES * win * freq, bytes_accessed=3 << 20, transcendentals=0
        ),
        name="own_whiten",
    )(before, spectra, after, weight, band, index, valid)

    shape = (tiles, rounds, 2, ch, LANES)
    if in_parts:
        zparts[-1], local = lax.optimization_barrier((zparts[-1], local))
        windows = 1
        specs = [vmem] * tiles
    else:
        windows = win
        zparts = [filtered.reshape((tiles, win) + shape[1:])]
        specs = [pl.BlockSpec((tiles, 1) + shape[1:], lambda s: (0, s, 0, 0, 0, 0))]
    column = pl.pallas_call(
        functools.partial(column_kernel, win=win),
        grid=(windows,),
        in_specs=[smem] + specs + [vmem, vmem],
        out_specs=pl.BlockSpec((1,) + shape, lambda s: (s, 0, 0, 0, 0, 0)),
        out_shape=jax.ShapeDtypeStruct((windows,) + shape, jnp.bfloat16),
        scratch_shapes=[pltpu.VMEM(shape, jnp.bfloat16)],
        compiler_params=room(16),
        name="column_whiten",
    )(params, *zparts, band, pick)

    def cross(masks, columns, earlier, final):
        group = SRC_STEP
        scratch = []
        spec = vmem
        result = jax.ShapeDtypeStruct((2, sources, tiles, ch, LANES), jnp.bfloat16)
        if final:
            spec = pl.BlockSpec(memory_space=pl.ANY)
            result = jax.ShapeDtypeStruct((2, sources, ch, freq), jnp.bfloat16)
            scratch.append(pltpu.VMEM((SLOTS, 2, group, ch, freq), jnp.bfloat16))
            scratch.append(pltpu.SemaphoreType.DMA((SLOTS, 2)))
        return pl.pallas_call(
            functools.partial(cross_kernel, masks=masks, added=len(earlier) > 0, final=final),
            grid=(sources // group,),
            in_specs=[smem] + [vmem] * (len(columns) + 1 + len(earlier)),
            out_specs=spec,
            out_shape=result,
            scratch_shapes=scratch,
            compiler_params=room(32),
            cost_estimate=pl.CostEstimate(
                flops=16 * len(masks) * sources * ch * freq, bytes_accessed=16 << 20, transcendentals=0
            ),
            name="cross",
        )(params, *columns, local, *earlier)

    if not in_parts:
        return cross(tuple(range(win)), [column[w : w + 1] for w in range(win)], [], True)
    far = swap(column, 2, n_chan)
    beside = swap(column, 1, n_chan)
    partial = cross((0, 1), [column, beside], [], False)
    far, partial = lax.optimization_barrier((far, partial))
    return cross((2, 3), [far, swap(far, 1, n_chan)], [partial], True)


def solution(mesh):
    in_specs = (
        P(None, "groups", "chan", None),
        P(),
        P(),
        P("groups", "chan"),
        P("groups"),
        P("groups", None),
    )
    out_specs = P(None, "groups", "chan", None)
    return jax.shard_map(body, mesh=mesh, in_specs=in_specs, out_specs=out_specs, check_vma=False)
```

```python
import functools

import jax
import jax.numpy as jnp
from jax import lax
from jax.experimental import pallas as pl
from jax.experimental.pallas import tpu as pltpu
from jax.sharding import PartitionSpec as P

SMOOTH = 17
LANES = 128
WATER = 0.05
SRC_STEP = 16
SLOTS = 3


def room(mib):
    return pltpu.CompilerParams(vmem_limit_bytes=mib * 1024 * 1024)


def fetch(pairs, sems):
    copies = [pltpu.make_async_copy(src, dst, sems.at[i]) for i, (src, dst) in enumerate(pairs)]
    for copy in copies:
        copy.start()
    return copies


def split_kernel(whole_ref, valid_ref, piece_ref, flags_ref, spectra_ref, sems):
    _, win, ch, freq = whole_ref.shape
    tiles = freq // LANES
    extra = piece_ref.shape[1] - 2 * ch
    copies = fetch(
        [(valid_ref, flags_ref)] + [(whole_ref.at[:, w], spectra_ref.at[:, w]) for w in range(win)], sems
    )
    copies[0].wait()
    for w in range(win):
        copies[1 + w].wait()
        flags = jnp.broadcast_to(flags_ref[w : w + 1, :], (extra, ch)).astype(jnp.float32)
        for t in range(tiles):
            at = slice(t * LANES, (t + 1) * LANES)
            piece_ref[t * win + w, :ch] = spectra_ref[0, w, :, at]
            piece_ref[t * win + w, ch : 2 * ch] = spectra_ref[1, w, :, at]
            piece_ref[t * win + w, 2 * ch :] = jnp.zeros((extra, LANES), jnp.bfloat16)
            piece_ref[t * win + w, 2 * ch :, :ch] = flags.astype(jnp.bfloat16)


def prep_kernel(*refs):
    sources, (weight_ref, band_ref, index_ref, valid_ref, pick_ref) = refs[:4], refs[4:9]
    (bank_ref, bins_ref, flags_ref, offset_ref), padded_ref, sems = refs[9:13], refs[13], refs[14]
    for copy in fetch(list(zip(sources, (bank_ref, bins_ref, flags_ref, offset_ref))), sems):
        copy.wait()
    _, banks, taps = bank_ref.shape
    half = weight_ref.shape[0] // 2
    ch = half // (2 * banks)
    index_ref[...] = bins_ref[...]
    channel = lax.broadcasted_iota(jnp.int32, (ch, ch), 0)
    for r in range(offset_ref.shape[0]):
        picked = channel == offset_ref[r : r + 1, :]
        pick_ref[r] = jnp.where(picked, 1.0, 0.0).astype(jnp.bfloat16)
    for w in range(flags_ref.shape[0]):
        column = flag_column(flags_ref[w : w + 1, :])
        valid_ref[w * ch : (w + 1) * ch, :] = jnp.broadcast_to(column, (ch, LANES))
    padded_ref[...] = jnp.zeros(padded_ref.shape, jnp.float32)
    padded_ref[:, :, :taps] = bank_ref[...]

    def skewed(row):
        tile = jnp.broadcast_to(row, (ch, LANES))
        return pltpu.roll(tile, 0, 1, stride=1, stride_axis=0)

    for b in range(banks):
        real = skewed(padded_ref[0, b : b + 1, :])
        imag = skewed(padded_ref[1, b : b + 1, :])
        base = b * 2 * ch
        for row, left, right in ((base, real, -imag), (base + ch, imag, real)):
            for col, val in ((0, left), (LANES, right)):
                high = val.astype(jnp.bfloat16)
                low = (val - high.astype(jnp.float32)).astype(jnp.bfloat16)
                weight_ref[row : row + ch, col : col + LANES] = high
                weight_ref[half + row : half + row + ch, col : col + LANES] = low
    rows = lax.broadcasted_iota(jnp.int32, band_ref.shape, 0)
    cols = lax.broadcasted_iota(jnp.int32, band_ref.shape, 1)
    near = jnp.abs(rows - cols) <= SMOOTH // 2
    band_ref[...] = jnp.where(near, 1.0, 0.0).astype(jnp.bfloat16)


def flag_column(row):
    ch = row.shape[1]
    rows = lax.broadcasted_iota(jnp.int32, (ch, ch), 0)
    cols = lax.broadcasted_iota(jnp.int32, (ch, ch), 1)
    return jnp.sum(jnp.where(rows == cols, row.astype(jnp.float32), 0.0), axis=1, keepdims=True)


def filtered_block(x, weight_ref, index, ch):
    half = weight_ref.shape[0] // 2
    y = jnp.dot(weight_ref[...], x, preferred_element_type=jnp.float32)
    rows = 2 * ch
    pick = y[:rows] + y[half : half + rows]
    for at in range(rows, half, rows):
        here = y[at : at + rows] + y[half + at : half + at + rows]
        pick = jnp.where(index == at // rows, here, pick)
    return pick


def running_scale(real, imag, band_ref):
    count = real.shape[0]
    power = real * real + imag * imag
    high = power.astype(jnp.bfloat16)
    low = (power - high.astype(jnp.float32)).astype(jnp.bfloat16)
    both = jnp.concatenate([high, low], axis=0)
    total = jnp.dot(both, band_ref[...], preferred_element_type=jnp.float32)
    return lax.rsqrt((total[:count] + total[count:]) * (1.0 / SMOOTH) + WATER)


def source_kernel(params_ref, x_ref, weight_ref, index_ref, out_ref, *, win):
    n_chan = x_ref.shape[0]
    _, rounds, _, ch, _ = out_ref.shape
    tile = lax.div(params_ref[0] + pl.program_id(0), win)
    zero = jnp.zeros((), jnp.bfloat16)
    gap = jnp.zeros((LANES - 3 * ch, LANES), jnp.bfloat16)
    columns = []
    for r in range(rounds):
        block = params_ref[2 + r]
        before = jnp.maximum(block - 1, 0)
        after = jnp.minimum(block + 1, n_chan - 1)
        parts = []
        for p in range(2):
            at = slice(p * ch, (p + 1) * ch)
            parts.append(jnp.where(block > 0, x_ref[before, 0, at], zero))
            parts.append(x_ref[block, 0, at])
            parts.append(jnp.where(block < n_chan - 1, x_ref[after, 0, at], zero))
            parts.append(gap)
        columns.append(jnp.concatenate(parts, axis=0))
    x = jnp.concatenate(columns, axis=1)
    index = jnp.concatenate([index_ref[tile]] * rounds, axis=1)
    pick = filtered_block(x, weight_ref, index, ch)
    for r in range(rounds):
        flags = x_ref[params_ref[2 + r], 0, 2 * ch :].astype(jnp.float32)[:1, :ch]
        valid = flag_column(flags)
        for p in range(2):
            part = pick[p * ch : (p + 1) * ch, r * LANES : (r + 1) * LANES] * valid
            out_ref[0, r, p] = part.astype(jnp.bfloat16)


def own_kernel(prev_ref, piece_ref, next_ref, weight_ref, band_ref, index_ref, valid_ref, out_ref, filt_ref):
    _, win, ch, freq = prev_ref.shape
    tiles = freq // LANES
    gap = jnp.zeros((LANES - 3 * ch, freq), jnp.bfloat16)
    index = jnp.concatenate([index_ref[t] for t in range(tiles)], axis=1)

    def one_window(w, _):
        parts = []
        for p in range(2):
            at = slice(p * ch, (p + 1) * ch)
            here = jnp.concatenate([piece_ref[t * win + w, at] for t in range(tiles)], axis=1)
            parts += [prev_ref[p, w], here, next_ref[p, w], gap]
        x = jnp.concatenate(parts, axis=0)
        pick = filtered_block(x, weight_ref, index, ch)
        at = pl.ds(pl.multiple_of(w * ch, ch), ch)
        filt_ref[0, at, :] = pick[:ch]
        filt_ref[1, at, :] = pick[ch:]
        return 0

    lax.fori_loop(0, win, one_window, 0)
    valid = jnp.concatenate([valid_ref[...]] * tiles, axis=1)
    scale = running_scale(filt_ref[0], filt_ref[1], band_ref) * valid
    for p in range(2):
        white = (filt_ref[p] * scale).astype(jnp.bfloat16)
        for t in range(tiles):
            for w in range(win):
                out_ref[p, t, w] = white[w * ch : (w + 1) * ch, t * LANES : (t + 1) * LANES]


def column_kernel(params_ref, *refs, win):
    band_ref, pick_ref, out_ref, piece_ref = refs[-4:]
    parts = refs[:-4]
    tiles, rounds, _, ch, _ = piece_ref.shape
    if len(parts) == tiles:
        place = params_ref[1]
        for k, ref in enumerate(parts):
            piece_ref[place ^ k] = ref[0]
    else:
        piece_ref[...] = parts[0][:, 0]
    both = []
    for p in range(2):
        rows = []
        for r in range(rounds):
            row = jnp.concatenate([piece_ref[t, r, p] for t in range(tiles)], axis=1)
            rows.append(
                lax.dot_general(
                    pick_ref[r], row, (((0,), (0,)), ((), ())), preferred_element_type=jnp.float32
                )
            )
        both.append(jnp.concatenate(rows, axis=0))
    scale = running_scale(both[0], both[1], band_ref)
    for p in range(2):
        white = (both[p] * scale).astype(jnp.bfloat16) * jnp.bfloat16(1.0 / win)
        for t in range(tiles):
            for r in range(rounds):
                out_ref[0, t, r, p] = white[r * ch : (r + 1) * ch, t * LANES : (t + 1) * LANES]


def spread_row(block, j, ch):
    return jnp.broadcast_to(block[j : j + 1, :], (ch, block.shape[1]))


def pairwise(terms):
    while len(terms) > 1:
        half = (len(terms) + 1) // 2
        terms = [terms[i] + terms[i + half] if i + half < len(terms) else terms[i] for i in range(half)]
    return terms[0]


def cross_kernel(params_ref, *refs, masks, added, final):
    column_refs = refs[: len(masks)]
    local_ref = refs[len(masks)]
    partial_ref = refs[len(masks) + 1]
    if final:
        out_ref, stage_ref, sems = refs[-3:]
    else:
        out_ref = refs[-1]
    tiles, win, ch = local_ref.shape[1:4]
    rounds = column_refs[0].shape[2]
    group = SRC_STEP
    per_round = ch // group
    steps = rounds * per_round
    step = pl.program_id(0)
    r = step // per_round
    begin = step * group
    rows = pl.ds(pl.multiple_of(lax.rem(step, per_round) * group, group), group)
    here = lax.rem(params_ref[0], win)
    slot = lax.rem(step, SLOTS)

    def copies(at_step):
        at_slot = lax.rem(at_step, SLOTS)
        return [
            pltpu.make_async_copy(
                stage_ref.at[at_slot, p], out_ref.at[p, pl.ds(at_step * group, group)], sems.at[at_slot, p]
            )
            for p in range(2)
        ]

    if final:

        @pl.when(step >= SLOTS)
        def _():
            for copy in copies(step - SLOTS):
                copy.wait()

    def one_tile(ft, _):
        at = pl.ds(pl.multiple_of(ft * LANES, LANES), LANES)
        mine = [(local_ref[0, ft, here ^ mask], local_ref[1, ft, here ^ mask]) for mask in masks]
        theirs = [(ref[0, ft, r, 0, rows, :], ref[0, ft, r, 1, rows, :]) for ref in column_refs]
        for j in range(group):
            re = []
            im = []
            for (lr, li), block in zip(mine, theirs):
                sr, si = (spread_row(part, j, ch) for part in block)
                re.append(sr * lr + si * li)
                im.append(sr * li - si * lr)
            re = pairwise(re)
            im = pairwise(im)
            if added:
                re = re + partial_ref[0, begin + j, ft]
                im = im + partial_ref[1, begin + j, ft]
            if final:
                stage_ref[slot, 0, j, :, at] = re
                stage_ref[slot, 1, j, :, at] = im
            else:
                out_ref[0, begin + j, ft] = re
                out_ref[1, begin + j, ft] = im
        return 0

    lax.fori_loop(0, tiles, one_tile, 0)

    if final:
        for copy in copies(step):
            copy.start()

        @pl.when(step == steps - 1)
        def _():
            for back in range(SLOTS):
                for copy in copies(step - back):
                    copy.wait()


def swap(x, mask, n_chan):
    return lax.ppermute(x, "chan", [(i, i ^ mask) for i in range(n_chan)])


def body(spectra, filter_bank, band_index, window_mask, owner_order, source_offset):
    n_chan = lax.axis_size("chan")
    me = lax.axis_index("chan").astype(jnp.int32)
    _, win, ch, freq = spectra.shape
    banks, taps = filter_bank.shape[1:]
    rounds = owner_order.shape[0]
    count = win * ch
    tiles = freq // LANES
    pieces = win * tiles
    sources = rounds * ch
    in_parts = n_chan == pieces and win == 4 and tiles & (tiles - 1) == 0
    smem = pl.BlockSpec(memory_space=pltpu.SMEM)
    vmem = pl.BlockSpec(memory_space=pltpu.VMEM)
    hbm = pl.BlockSpec(memory_space=pltpu.HBM)

    split = pl.pallas_call(
        split_kernel,
        out_shape=jax.ShapeDtypeStruct((pieces, 2 * ch + 16, LANES), jnp.bfloat16),
        in_specs=[hbm, hbm],
        out_specs=vmem,
        scratch_shapes=[
            pltpu.VMEM(window_mask.shape, jnp.int32),
            pltpu.VMEM(spectra.shape, jnp.bfloat16),
            pltpu.SemaphoreType.DMA((1 + win,)),
        ],
        compiler_params=room(6),
        name="split",
    )(spectra, window_mask)
    if in_parts:
        held = lax.all_to_all(split, "chan", 0, 0)[:, None]
        first = me
    else:
        held = lax.all_gather(split, "chan")
        first = jnp.int32(0)
    params = jnp.concatenate([first[None], lax.div(first, jnp.int32(win))[None], owner_order])

    ends = n_chan - 1
    before = lax.ppermute(spectra, "chan", [(i, i + 1) for i in range(ends)])
    after = lax.ppermute(spectra, "chan", [(i + 1, i) for i in range(ends)])

    weight, band, index, valid, pick = pl.pallas_call(
        prep_kernel,
        out_shape=(
            jax.ShapeDtypeStruct((2 * banks * 2 * ch, 2 * LANES), jnp.bfloat16),
            jax.ShapeDtypeStruct((freq, freq), jnp.bfloat16),
            jax.ShapeDtypeStruct((tiles, 1, LANES), jnp.int32),
            jax.ShapeDtypeStruct((count, LANES), jnp.float32),
            jax.ShapeDtypeStruct((rounds, ch, ch), jnp.bfloat16),
        ),
        in_specs=[hbm] * 4,
        out_specs=[vmem] * 5,
        scratch_shapes=[
            pltpu.VMEM(filter_bank.shape, jnp.float32),
            pltpu.VMEM((tiles, 1, LANES), jnp.int32),
            pltpu.VMEM(window_mask.shape, jnp.int32),
            pltpu.VMEM(source_offset.shape, jnp.int32),
            pltpu.VMEM((2, banks, LANES), jnp.float32),
            pltpu.SemaphoreType.DMA((4,)),
        ],
        compiler_params=room(8),
        name="prep",
    )(filter_bank, band_index.reshape(tiles, 1, LANES), window_mask, source_offset)

    count_here = held.shape[1]
    filtered = pl.pallas_call(
        functools.partial(source_kernel, win=win),
        grid=(count_here,),
        in_specs=[
            smem,
            pl.BlockSpec((n_chan, 1, 2 * ch + 16, LANES), lambda s: (0, s, 0, 0)),
            vmem,
            vmem,
        ],
        out_specs=pl.BlockSpec((1, rounds, 2, ch, LANES), lambda s: (s, 0, 0, 0, 0)),
        out_shape=jax.ShapeDtypeStruct((count_here, rounds, 2, ch, LANES), jnp.bfloat16),
        compiler_params=room(16),
        name="source_filter",
    )(params, held, weight, index)

    if in_parts:
        zparts = [filtered] + [swap(filtered, win * k, n_chan) for k in range(1, tiles)]

    local = pl.pallas_call(
        own_kernel,
        out_shape=jax.ShapeDtypeStruct((2, tiles, win, ch, LANES), jnp.bfloat16),
        in_specs=[vmem] * 7,
        out_specs=vmem,
        scratch_shapes=[pltpu.VMEM((2, count, freq), jnp.float32)],
        compiler_params=room(16),
        cost_estimate=pl.CostEstimate(
            flops=4 * banks * 2 * ch * 2 * LANES * win * freq, bytes_accessed=3 << 20, transcendentals=0
        ),
        name="own_whiten",
    )(before, split, after, weight, band, index, valid)

    shape = (tiles, rounds, 2, ch, LANES)
    if in_parts:
        zparts[-1], local = lax.optimization_barrier((zparts[-1], local))
        windows = 1
        specs = [vmem] * tiles
    else:
        windows = win
        zparts = [filtered.reshape((tiles, win) + shape[1:])]
        specs = [pl.BlockSpec((tiles, 1) + shape[1:], lambda s: (0, s, 0, 0, 0, 0))]
    column = pl.pallas_call(
        functools.partial(column_kernel, win=win),
        grid=(windows,),
        in_specs=[smem] + specs + [vmem, vmem],
        out_specs=pl.BlockSpec((1,) + shape, lambda s: (s, 0, 0, 0, 0, 0)),
        out_shape=jax.ShapeDtypeStruct((windows,) + shape, jnp.bfloat16),
        scratch_shapes=[pltpu.VMEM(shape, jnp.bfloat16)],
        compiler_params=room(16),
        name="column_whiten",
    )(params, *zparts, band, pick)

    def cross(masks, columns, earlier, final):
        group = SRC_STEP
        scratch = []
        spec = vmem
        result = jax.ShapeDtypeStruct((2, sources, tiles, ch, LANES), jnp.bfloat16)
        if final:
            spec = pl.BlockSpec(memory_space=pl.ANY)
            result = jax.ShapeDtypeStruct((2, sources, ch, freq), jnp.bfloat16)
            scratch.append(pltpu.VMEM((SLOTS, 2, group, ch, freq), jnp.bfloat16))
            scratch.append(pltpu.SemaphoreType.DMA((SLOTS, 2)))
        return pl.pallas_call(
            functools.partial(cross_kernel, masks=masks, added=len(earlier) > 0, final=final),
            grid=(sources // group,),
            in_specs=[smem] + [vmem] * (len(columns) + 1 + len(earlier)),
            out_specs=spec,
            out_shape=result,
            scratch_shapes=scratch,
            compiler_params=room(32),
            cost_estimate=pl.CostEstimate(
                flops=16 * len(masks) * sources * ch * freq, bytes_accessed=16 << 20, transcendentals=0
            ),
            name="cross",
        )(params, *columns, local, *earlier)

    if not in_parts:
        return cross(tuple(range(win)), [column[w : w + 1] for w in range(win)], [], True)
    far = swap(column, 2, n_chan)
    beside = swap(column, 1, n_chan)
    partial = cross((0, 1), [column, beside], [], False)
    far, partial = lax.optimization_barrier((far, partial))
    return cross((2, 3), [far, swap(far, 1, n_chan)], [partial], True)


def solution(mesh):
    in_specs = (
        P(None, "groups", "chan", None),
        P(),
        P(),
        P("groups", "chan"),
        P("groups"),
        P("groups", None),
    )
    out_specs = P(None, "groups", "chan", None)
    return jax.shard_map(body, mesh=mesh, in_specs=in_specs, out_specs=out_specs, check_vma=False)
```

```python
import functools

import jax
import jax.numpy as jnp
from jax import lax
from jax.experimental import pallas as pl
from jax.experimental.pallas import tpu as pltpu
from jax.sharding import PartitionSpec as P

SMOOTH = 17
LANES = 128
WATER = 0.05
SRC_STEP = 16
SLOTS = 3


def room(mib):
    return pltpu.CompilerParams(vmem_limit_bytes=mib * 1024 * 1024)


def split_kernel(spectra_ref, flags_ref, piece_ref):
    _, win, ch, freq = spectra_ref.shape
    tiles = freq // LANES
    extra = piece_ref.shape[1] - 2 * ch
    for w in range(win):
        flags = jnp.broadcast_to(flags_ref[w : w + 1, :], (extra, ch)).astype(jnp.float32)
        for t in range(tiles):
            at = slice(t * LANES, (t + 1) * LANES)
            piece_ref[t * win + w, :ch] = spectra_ref[0, w, :, at]
            piece_ref[t * win + w, ch : 2 * ch] = spectra_ref[1, w, :, at]
            piece_ref[t * win + w, 2 * ch :] = jnp.zeros((extra, LANES), jnp.bfloat16)
            piece_ref[t * win + w, 2 * ch :, :ch] = flags.astype(jnp.bfloat16)


def prep_kernel(
    bank_ref, bins_ref, flags_ref, offset_ref, weight_ref, band_ref, index_ref, valid_ref, pick_ref, padded_ref
):
    _, banks, taps = bank_ref.shape
    half = weight_ref.shape[0] // 2
    ch = half // (2 * banks)
    index_ref[...] = bins_ref[...]
    channel = lax.broadcasted_iota(jnp.int32, (ch, ch), 0)
    for r in range(offset_ref.shape[0]):
        picked = channel == offset_ref[r : r + 1, :]
        pick_ref[r] = jnp.where(picked, 1.0, 0.0).astype(jnp.bfloat16)
    for w in range(flags_ref.shape[0]):
        column = flag_column(flags_ref[w : w + 1, :])
        valid_ref[w * ch : (w + 1) * ch, :] = jnp.broadcast_to(column, (ch, LANES))
    padded_ref[...] = jnp.zeros(padded_ref.shape, jnp.float32)
    padded_ref[:, :, :taps] = bank_ref[...]

    def skewed(row):
        tile = jnp.broadcast_to(row, (ch, LANES))
        return pltpu.roll(tile, 0, 1, stride=1, stride_axis=0)

    for b in range(banks):
        real = skewed(padded_ref[0, b : b + 1, :])
        imag = skewed(padded_ref[1, b : b + 1, :])
        base = b * 2 * ch
        for row, left, right in ((base, real, -imag), (base + ch, imag, real)):
            for col, val in ((0, left), (LANES, right)):
                high = val.astype(jnp.bfloat16)
                low = (val - high.astype(jnp.float32)).astype(jnp.bfloat16)
                weight_ref[row : row + ch, col : col + LANES] = high
                weight_ref[half + row : half + row + ch, col : col + LANES] = low
    rows = lax.broadcasted_iota(jnp.int32, band_ref.shape, 0)
    cols = lax.broadcasted_iota(jnp.int32, band_ref.shape, 1)
    near = jnp.abs(rows - cols) <= SMOOTH // 2
    band_ref[...] = jnp.where(near, 1.0, 0.0).astype(jnp.bfloat16)


def flag_column(row):
    ch = row.shape[1]
    rows = lax.broadcasted_iota(jnp.int32, (ch, ch), 0)
    cols = lax.broadcasted_iota(jnp.int32, (ch, ch), 1)
    return jnp.sum(jnp.where(rows == cols, row.astype(jnp.float32), 0.0), axis=1, keepdims=True)


def filtered_block(x, weight_ref, index, ch):
    half = weight_ref.shape[0] // 2
    y = jnp.dot(weight_ref[...], x, preferred_element_type=jnp.float32)
    rows = 2 * ch
    pick = y[:rows] + y[half : half + rows]
    for at in range(rows, half, rows):
        here = y[at : at + rows] + y[half + at : half + at + rows]
        pick = jnp.where(index == at // rows, here, pick)
    return pick


def running_scale(real, imag, band_ref):
    count = real.shape[0]
    power = real * real + imag * imag
    high = power.astype(jnp.bfloat16)
    low = (power - high.astype(jnp.float32)).astype(jnp.bfloat16)
    both = jnp.concatenate([high, low], axis=0)
    total = jnp.dot(both, band_ref[...], preferred_element_type=jnp.float32)
    return lax.rsqrt((total[:count] + total[count:]) * (1.0 / SMOOTH) + WATER)


def source_kernel(params_ref, x_ref, weight_ref, index_ref, out_ref, *, win):
    n_chan = x_ref.shape[0]
    _, rounds, _, ch, _ = out_ref.shape
    tile = lax.div(params_ref[0] + pl.program_id(0), win)
    zero = jnp.zeros((), jnp.bfloat16)
    gap = jnp.zeros((LANES - 3 * ch, LANES), jnp.bfloat16)
    columns = []
    for r in range(rounds):
        block = params_ref[2 + r]
        before = jnp.maximum(block - 1, 0)
        after = jnp.minimum(block + 1, n_chan - 1)
        parts = []
        for p in range(2):
            at = slice(p * ch, (p + 1) * ch)
            parts.append(jnp.where(block > 0, x_ref[before, 0, at], zero))
            parts.append(x_ref[block, 0, at])
            parts.append(jnp.where(block < n_chan - 1, x_ref[after, 0, at], zero))
            parts.append(gap)
        columns.append(jnp.concatenate(parts, axis=0))
    x = jnp.concatenate(columns, axis=1)
    index = jnp.concatenate([index_ref[tile]] * rounds, axis=1)
    pick = filtered_block(x, weight_ref, index, ch)
    for r in range(rounds):
        flags = x_ref[params_ref[2 + r], 0, 2 * ch :].astype(jnp.float32)[:1, :ch]
        valid = flag_column(flags)
        for p in range(2):
            part = pick[p * ch : (p + 1) * ch, r * LANES : (r + 1) * LANES] * valid
            out_ref[0, r, p] = part.astype(jnp.bfloat16)


def own_kernel(prev_ref, cur_ref, next_ref, weight_ref, band_ref, index_ref, valid_ref, out_ref, filt_ref):
    _, win, ch, freq = cur_ref.shape
    tiles = freq // LANES
    gap = jnp.zeros((LANES - 3 * ch, freq), jnp.bfloat16)
    index = jnp.concatenate([index_ref[t] for t in range(tiles)], axis=1)

    def one_window(w, _):
        parts = []
        for p in range(2):
            parts += [prev_ref[p, w], cur_ref[p, w], next_ref[p, w], gap]
        x = jnp.concatenate(parts, axis=0)
        pick = filtered_block(x, weight_ref, index, ch)
        at = pl.ds(pl.multiple_of(w * ch, ch), ch)
        filt_ref[0, at, :] = pick[:ch]
        filt_ref[1, at, :] = pick[ch:]
        return 0

    lax.fori_loop(0, win, one_window, 0)
    valid = jnp.concatenate([valid_ref[...]] * tiles, axis=1)
    scale = running_scale(filt_ref[0], filt_ref[1], band_ref) * valid
    for p in range(2):
        white = (filt_ref[p] * scale).astype(jnp.bfloat16)
        for t in range(tiles):
            for w in range(win):
                out_ref[p, t, w] = white[w * ch : (w + 1) * ch, t * LANES : (t + 1) * LANES]


def column_kernel(params_ref, *refs, win):
    band_ref, pick_ref, out_ref, piece_ref = refs[-4:]
    parts = refs[:-4]
    tiles, rounds, _, ch, _ = piece_ref.shape
    if len(parts) == tiles:
        place = params_ref[1]
        for k, ref in enumerate(parts):
            piece_ref[place ^ k] = ref[0]
    else:
        piece_ref[...] = parts[0][:, 0]
    both = []
    for p in range(2):
        rows = []
        for r in range(rounds):
            row = jnp.concatenate([piece_ref[t, r, p] for t in range(tiles)], axis=1)
            rows.append(
                lax.dot_general(
                    pick_ref[r], row, (((0,), (0,)), ((), ())), preferred_element_type=jnp.float32
                )
            )
        both.append(jnp.concatenate(rows, axis=0))
    scale = running_scale(both[0], both[1], band_ref)
    for p in range(2):
        white = (both[p] * scale).astype(jnp.bfloat16) * jnp.bfloat16(1.0 / win)
        for t in range(tiles):
            for r in range(rounds):
                out_ref[0, t, r, p] = white[r * ch : (r + 1) * ch, t * LANES : (t + 1) * LANES]


def spread_row(block, j, ch):
    return jnp.broadcast_to(block[j : j + 1, :], (ch, block.shape[1]))


def pairwise(terms):
    while len(terms) > 1:
        half = (len(terms) + 1) // 2
        terms = [terms[i] + terms[i + half] if i + half < len(terms) else terms[i] for i in range(half)]
    return terms[0]


def cross_kernel(params_ref, *refs, masks, added, final):
    column_refs = refs[: len(masks)]
    local_ref = refs[len(masks)]
    partial_ref = refs[len(masks) + 1]
    if final:
        out_ref, stage_ref, sems = refs[-3:]
    else:
        out_ref = refs[-1]
    tiles, win, ch = local_ref.shape[1:4]
    rounds = column_refs[0].shape[2]
    group = SRC_STEP
    per_round = ch // group
    steps = rounds * per_round
    step = pl.program_id(0)
    r = step // per_round
    begin = step * group
    rows = pl.ds(pl.multiple_of(lax.rem(step, per_round) * group, group), group)
    here = lax.rem(params_ref[0], win)
    slot = lax.rem(step, SLOTS)

    def copies(at_step, ft):
        at_slot = lax.rem(at_step, SLOTS)
        bins = pl.ds(pl.multiple_of(ft * LANES, LANES), LANES)
        return [
            pltpu.make_async_copy(
                stage_ref.at[at_slot, p, ft],
                out_ref.at[p, pl.ds(at_step * group, group), :, bins],
                sems.at[at_slot, p, ft],
            )
            for p in range(2)
        ]

    def one_tile(ft, _):
        if final:

            @pl.when(step >= SLOTS)
            def _():
                for copy in copies(step - SLOTS, ft):
                    copy.wait()

        mine = [(local_ref[0, ft, here ^ mask], local_ref[1, ft, here ^ mask]) for mask in masks]
        theirs = [(ref[0, ft, r, 0, rows, :], ref[0, ft, r, 1, rows, :]) for ref in column_refs]
        for j in range(group):
            re = []
            im = []
            for (lr, li), block in zip(mine, theirs):
                sr, si = (spread_row(part, j, ch) for part in block)
                re.append(sr * lr + si * li)
                im.append(sr * li - si * lr)
            re = pairwise(re)
            im = pairwise(im)
            if added:
                re = re + partial_ref[0, begin + j, ft]
                im = im + partial_ref[1, begin + j, ft]
            if final:
                stage_ref[slot, 0, ft, j] = re
                stage_ref[slot, 1, ft, j] = im
            else:
                out_ref[0, begin + j, ft] = re
                out_ref[1, begin + j, ft] = im
        if final:
            for copy in copies(step, ft):
                copy.start()
        return 0

    lax.fori_loop(0, tiles, one_tile, 0)

    if final:

        @pl.when(step == steps - 1)
        def _():
            for back in reversed(range(SLOTS)):
                for ft in range(tiles):
                    for copy in copies(step - back, ft):
                        copy.wait()


def swap(x, mask, n_chan):
    return lax.ppermute(x, "chan", [(i, i ^ mask) for i in range(n_chan)])


def body(spectra, filter_bank, band_index, window_mask, owner_order, source_offset):
    n_chan = lax.axis_size("chan")
    me = lax.axis_index("chan").astype(jnp.int32)
    _, win, ch, freq = spectra.shape
    banks, taps = filter_bank.shape[1:]
    rounds = owner_order.shape[0]
    count = win * ch
    tiles = freq // LANES
    pieces = win * tiles
    sources = rounds * ch
    in_parts = n_chan == pieces and win == 4 and tiles & (tiles - 1) == 0
    smem = pl.BlockSpec(memory_space=pltpu.SMEM)
    vmem = pl.BlockSpec(memory_space=pltpu.VMEM)

    split = pl.pallas_call(
        split_kernel,
        out_shape=jax.ShapeDtypeStruct((pieces, 2 * ch + 16, LANES), jnp.bfloat16),
        compiler_params=room(56),
        name="split",
    )(spectra, window_mask)
    if in_parts:
        held = lax.all_to_all(split, "chan", 0, 0)[:, None]
        first = me
    else:
        held = lax.all_gather(split, "chan")
        first = jnp.int32(0)
    params = jnp.concatenate([first[None], lax.div(first, jnp.int32(win))[None], owner_order])

    ends = n_chan - 1
    before = lax.ppermute(spectra, "chan", [(i, i + 1) for i in range(ends)])
    after = lax.ppermute(spectra, "chan", [(i + 1, i) for i in range(ends)])

    weight, band, index, valid, pick = pl.pallas_call(
        prep_kernel,
        out_shape=(
            jax.ShapeDtypeStruct((2 * banks * 2 * ch, 2 * LANES), jnp.bfloat16),
            jax.ShapeDtypeStruct((freq, freq), jnp.bfloat16),
            jax.ShapeDtypeStruct((tiles, 1, LANES), jnp.int32),
            jax.ShapeDtypeStruct((count, LANES), jnp.float32),
            jax.ShapeDtypeStruct((rounds, ch, ch), jnp.bfloat16),
        ),
        scratch_shapes=[pltpu.VMEM((2, banks, LANES), jnp.float32)],
        compiler_params=room(8),
        name="prep",
    )(filter_bank, band_index.reshape(tiles, 1, LANES), window_mask, source_offset)

    count_here = held.shape[1]
    filtered = pl.pallas_call(
        functools.partial(source_kernel, win=win),
        grid=(count_here,),
        in_specs=[
            smem,
            pl.BlockSpec((n_chan, 1, 2 * ch + 16, LANES), lambda s: (0, s, 0, 0)),
            vmem,
            vmem,
        ],
        out_specs=pl.BlockSpec((1, rounds, 2, ch, LANES), lambda s: (s, 0, 0, 0, 0)),
        out_shape=jax.ShapeDtypeStruct((count_here, rounds, 2, ch, LANES), jnp.bfloat16),
        compiler_params=room(16),
        name="source_filter",
    )(params, held, weight, index)

    if in_parts:
        zparts = [filtered] + [swap(filtered, win * k, n_chan) for k in range(1, tiles)]

    local = pl.pallas_call(
        own_kernel,
        out_shape=jax.ShapeDtypeStruct((2, tiles, win, ch, LANES), jnp.bfloat16),
        in_specs=[vmem] * 7,
        out_specs=vmem,
        scratch_shapes=[pltpu.VMEM((2, count, freq), jnp.float32)],
        compiler_params=room(16),
        cost_estimate=pl.CostEstimate(
            flops=4 * banks * 2 * ch * 2 * LANES * win * freq, bytes_accessed=3 << 20, transcendentals=0
        ),
        name="own_whiten",
    )(before, spectra, after, weight, band, index, valid)

    shape = (tiles, rounds, 2, ch, LANES)
    if in_parts:
        zparts[-1], local = lax.optimization_barrier((zparts[-1], local))
        windows = 1
        specs = [vmem] * tiles
    else:
        windows = win
        zparts = [filtered.reshape((tiles, win) + shape[1:])]
        specs = [pl.BlockSpec((tiles, 1) + shape[1:], lambda s: (0, s, 0, 0, 0, 0))]
    column = pl.pallas_call(
        functools.partial(column_kernel, win=win),
        grid=(windows,),
        in_specs=[smem] + specs + [vmem, vmem],
        out_specs=pl.BlockSpec((1,) + shape, lambda s: (s, 0, 0, 0, 0, 0)),
        out_shape=jax.ShapeDtypeStruct((windows,) + shape, jnp.bfloat16),
        scratch_shapes=[pltpu.VMEM(shape, jnp.bfloat16)],
        compiler_params=room(16),
        name="column_whiten",
    )(params, *zparts, band, pick)

    def cross(masks, columns, earlier, final):
        group = SRC_STEP
        scratch = []
        spec = vmem
        result = jax.ShapeDtypeStruct((2, sources, tiles, ch, LANES), jnp.bfloat16)
        if final:
            spec = pl.BlockSpec(memory_space=pl.ANY)
            result = jax.ShapeDtypeStruct((2, sources, ch, freq), jnp.bfloat16)
            scratch.append(pltpu.VMEM((SLOTS, 2, tiles, group, ch, LANES), jnp.bfloat16))
            scratch.append(pltpu.SemaphoreType.DMA((SLOTS, 2, tiles)))
        return pl.pallas_call(
            functools.partial(cross_kernel, masks=masks, added=len(earlier) > 0, final=final),
            grid=(sources // group,),
            in_specs=[smem] + [vmem] * (len(columns) + 1 + len(earlier)),
            out_specs=spec,
            out_shape=result,
            scratch_shapes=scratch,
            compiler_params=room(32),
            cost_estimate=pl.CostEstimate(
                flops=16 * len(masks) * sources * ch * freq, bytes_accessed=16 << 20, transcendentals=0
            ),
            name="cross",
        )(params, *columns, local, *earlier)

    if not in_parts:
        return cross(tuple(range(win)), [column[w : w + 1] for w in range(win)], [], True)
    far = swap(column, 2, n_chan)
    beside = swap(column, 1, n_chan)
    partial = cross((0, 1), [column, beside], [], False)
    far, partial = lax.optimization_barrier((far, partial))
    return cross((2, 3), [far, swap(far, 1, n_chan)], [partial], True)


def solution(mesh):
    in_specs = (
        P(None, "groups", "chan", None),
        P(),
        P(),
        P("groups", "chan"),
        P("groups"),
        P("groups", None),
    )
    out_specs = P(None, "groups", "chan", None)
    return jax.shard_map(body, mesh=mesh, in_specs=in_specs, out_specs=out_specs, check_vma=False)
```

```python
import functools

import jax
import jax.numpy as jnp
from jax import lax
from jax.experimental import pallas as pl
from jax.experimental.pallas import tpu as pltpu
from jax.sharding import PartitionSpec as P

SMOOTH = 17
LANES = 128
WATER = 0.05
SRC_STEP = 16
SLOTS = 3


def room(mib):
    return pltpu.CompilerParams(vmem_limit_bytes=mib * 1024 * 1024)


def split_kernel(whole_ref, flags_ref, piece_ref, spectra_ref, sems):
    _, win, ch, freq = whole_ref.shape
    tiles = freq // LANES
    extra = piece_ref.shape[1] - 2 * ch
    copies = [
        pltpu.make_async_copy(whole_ref.at[:, w], spectra_ref.at[:, w], sems.at[w]) for w in range(win)
    ]
    for copy in copies:
        copy.start()
    for w in range(win):
        copies[w].wait()
        flags = jnp.broadcast_to(flags_ref[w : w + 1, :], (extra, ch)).astype(jnp.float32)
        for t in range(tiles):
            at = slice(t * LANES, (t + 1) * LANES)
            piece_ref[t * win + w, :ch] = spectra_ref[0, w, :, at]
            piece_ref[t * win + w, ch : 2 * ch] = spectra_ref[1, w, :, at]
            piece_ref[t * win + w, 2 * ch :] = jnp.zeros((extra, LANES), jnp.bfloat16)
            piece_ref[t * win + w, 2 * ch :, :ch] = flags.astype(jnp.bfloat16)


def prep_kernel(
    bank_ref, bins_ref, flags_ref, offset_ref, weight_ref, band_ref, index_ref, valid_ref, pick_ref, padded_ref
):
    _, banks, taps = bank_ref.shape
    half = weight_ref.shape[0] // 2
    ch = half // (2 * banks)
    index_ref[...] = bins_ref[...]
    channel = lax.broadcasted_iota(jnp.int32, (ch, ch), 0)
    for r in range(offset_ref.shape[0]):
        picked = channel == offset_ref[r : r + 1, :]
        pick_ref[r] = jnp.where(picked, 1.0, 0.0).astype(jnp.bfloat16)
    for w in range(flags_ref.shape[0]):
        column = flag_column(flags_ref[w : w + 1, :])
        valid_ref[w * ch : (w + 1) * ch, :] = jnp.broadcast_to(column, (ch, LANES))
    padded_ref[...] = jnp.zeros(padded_ref.shape, jnp.float32)
    padded_ref[:, :, :taps] = bank_ref[...]

    def skewed(row):
        tile = jnp.broadcast_to(row, (ch, LANES))
        return pltpu.roll(tile, 0, 1, stride=1, stride_axis=0)

    for b in range(banks):
        real = skewed(padded_ref[0, b : b + 1, :])
        imag = skewed(padded_ref[1, b : b + 1, :])
        base = b * 2 * ch
        for row, left, right in ((base, real, -imag), (base + ch, imag, real)):
            for col, val in ((0, left), (LANES, right)):
                high = val.astype(jnp.bfloat16)
                low = (val - high.astype(jnp.float32)).astype(jnp.bfloat16)
                weight_ref[row : row + ch, col : col + LANES] = high
                weight_ref[half + row : half + row + ch, col : col + LANES] = low
    rows = lax.broadcasted_iota(jnp.int32, band_ref.shape, 0)
    cols = lax.broadcasted_iota(jnp.int32, band_ref.shape, 1)
    near = jnp.abs(rows - cols) <= SMOOTH // 2
    band_ref[...] = jnp.where(near, 1.0, 0.0).astype(jnp.bfloat16)


def flag_column(row):
    ch = row.shape[1]
    rows = lax.broadcasted_iota(jnp.int32, (ch, ch), 0)
    cols = lax.broadcasted_iota(jnp.int32, (ch, ch), 1)
    return jnp.sum(jnp.where(rows == cols, row.astype(jnp.float32), 0.0), axis=1, keepdims=True)


def filtered_block(x, weight_ref, index, ch):
    half = weight_ref.shape[0] // 2
    y = jnp.dot(weight_ref[...], x, preferred_element_type=jnp.float32)
    rows = 2 * ch
    pick = y[:rows] + y[half : half + rows]
    for at in range(rows, half, rows):
        here = y[at : at + rows] + y[half + at : half + at + rows]
        pick = jnp.where(index == at // rows, here, pick)
    return pick


def running_scale(real, imag, band_ref):
    count = real.shape[0]
    power = real * real + imag * imag
    high = power.astype(jnp.bfloat16)
    low = (power - high.astype(jnp.float32)).astype(jnp.bfloat16)
    both = jnp.concatenate([high, low], axis=0)
    total = jnp.dot(both, band_ref[...], preferred_element_type=jnp.float32)
    return lax.rsqrt((total[:count] + total[count:]) * (1.0 / SMOOTH) + WATER)


def source_kernel(params_ref, x_ref, weight_ref, index_ref, out_ref, *, win):
    n_chan = x_ref.shape[0]
    _, rounds, _, ch, _ = out_ref.shape
    tile = lax.div(params_ref[0] + pl.program_id(0), win)
    zero = jnp.zeros((), jnp.bfloat16)
    gap = jnp.zeros((LANES - 3 * ch, LANES), jnp.bfloat16)
    columns = []
    for r in range(rounds):
        block = params_ref[2 + r]
        before = jnp.maximum(block - 1, 0)
        after = jnp.minimum(block + 1, n_chan - 1)
        parts = []
        for p in range(2):
            at = slice(p * ch, (p + 1) * ch)
            parts.append(jnp.where(block > 0, x_ref[before, 0, at], zero))
            parts.append(x_ref[block, 0, at])
            parts.append(jnp.where(block < n_chan - 1, x_ref[after, 0, at], zero))
            parts.append(gap)
        columns.append(jnp.concatenate(parts, axis=0))
    x = jnp.concatenate(columns, axis=1)
    index = jnp.concatenate([index_ref[tile]] * rounds, axis=1)
    pick = filtered_block(x, weight_ref, index, ch)
    for r in range(rounds):
        flags = x_ref[params_ref[2 + r], 0, 2 * ch :].astype(jnp.float32)[:1, :ch]
        valid = flag_column(flags)
        for p in range(2):
            part = pick[p * ch : (p + 1) * ch, r * LANES : (r + 1) * LANES] * valid
            out_ref[0, r, p] = part.astype(jnp.bfloat16)


def own_kernel(prev_ref, cur_ref, next_ref, weight_ref, band_ref, index_ref, valid_ref, out_ref, filt_ref):
    _, win, ch, freq = cur_ref.shape
    tiles = freq // LANES
    gap = jnp.zeros((LANES - 3 * ch, freq), jnp.bfloat16)
    index = jnp.concatenate([index_ref[t] for t in range(tiles)], axis=1)

    def one_window(w, _):
        parts = []
        for p in range(2):
            parts += [prev_ref[p, w], cur_ref[p, w], next_ref[p, w], gap]
        x = jnp.concatenate(parts, axis=0)
        pick = filtered_block(x, weight_ref, index, ch)
        at = pl.ds(pl.multiple_of(w * ch, ch), ch)
        filt_ref[0, at, :] = pick[:ch]
        filt_ref[1, at, :] = pick[ch:]
        return 0

    lax.fori_loop(0, win, one_window, 0)
    valid = jnp.concatenate([valid_ref[...]] * tiles, axis=1)
    scale = running_scale(filt_ref[0], filt_ref[1], band_ref) * valid
    for p in range(2):
        white = (filt_ref[p] * scale).astype(jnp.bfloat16)
        for t in range(tiles):
            for w in range(win):
                out_ref[p, t, w] = white[w * ch : (w + 1) * ch, t * LANES : (t + 1) * LANES]


def column_kernel(params_ref, *refs, win):
    band_ref, pick_ref, out_ref, piece_ref = refs[-4:]
    parts = refs[:-4]
    tiles, rounds, _, ch, _ = piece_ref.shape
    if len(parts) == tiles:
        place = params_ref[1]
        for k, ref in enumerate(parts):
            piece_ref[place ^ k] = ref[0]
    else:
        piece_ref[...] = parts[0][:, 0]
    both = []
    for p in range(2):
        rows = []
        for r in range(rounds):
            row = jnp.concatenate([piece_ref[t, r, p] for t in range(tiles)], axis=1)
            rows.append(
                lax.dot_general(
                    pick_ref[r], row, (((0,), (0,)), ((), ())), preferred_element_type=jnp.float32
                )
            )
        both.append(jnp.concatenate(rows, axis=0))
    scale = running_scale(both[0], both[1], band_ref)
    for p in range(2):
        white = (both[p] * scale).astype(jnp.bfloat16) * jnp.bfloat16(1.0 / win)
        for t in range(tiles):
            for r in range(rounds):
                out_ref[0, t, r, p] = white[r * ch : (r + 1) * ch, t * LANES : (t + 1) * LANES]


def spread_row(block, j, ch):
    return jnp.broadcast_to(block[j : j + 1, :], (ch, block.shape[1]))


def pairwise(terms):
    while len(terms) > 1:
        half = (len(terms) + 1) // 2
        terms = [terms[i] + terms[i + half] if i + half < len(terms) else terms[i] for i in range(half)]
    return terms[0]


def cross_kernel(params_ref, *refs, masks, added, final):
    column_refs = refs[: len(masks)]
    local_ref = refs[len(masks)]
    partial_ref = refs[len(masks) + 1]
    if final:
        out_ref, stage_ref, sems = refs[-3:]
    else:
        out_ref = refs[-1]
    tiles, win, ch = local_ref.shape[1:4]
    rounds = column_refs[0].shape[2]
    group = SRC_STEP
    per_round = ch // group
    steps = rounds * per_round
    step = pl.program_id(0)
    r = step // per_round
    begin = step * group
    rows = pl.ds(pl.multiple_of(lax.rem(step, per_round) * group, group), group)
    here = lax.rem(params_ref[0], win)
    slot = lax.rem(step, SLOTS)

    half = group // 2

    def copies(at_step, h):
        at_slot = lax.rem(at_step, SLOTS)
        return [
            pltpu.make_async_copy(
                stage_ref.at[at_slot, p, pl.ds(h * half, half)],
                out_ref.at[p, pl.ds(at_step * group + h * half, half)],
                sems.at[at_slot, p, h],
            )
            for p in range(2)
        ]

    if final:

        @pl.when(step >= SLOTS)
        def _():
            for copy in copies(step - SLOTS, 0) + copies(step - SLOTS, 1):
                copy.wait()

    def one_tile(h, ft, _):
        at = pl.ds(pl.multiple_of(ft * LANES, LANES), LANES)
        mine = [(local_ref[0, ft, here ^ mask], local_ref[1, ft, here ^ mask]) for mask in masks]
        theirs = [(ref[0, ft, r, 0, rows, :], ref[0, ft, r, 1, rows, :]) for ref in column_refs]
        for j in range(h * half, (h + 1) * half):
            re = []
            im = []
            for (lr, li), block in zip(mine, theirs):
                sr, si = (spread_row(part, j, ch) for part in block)
                re.append(sr * lr + si * li)
                im.append(sr * li - si * lr)
            re = pairwise(re)
            im = pairwise(im)
            if added:
                re = re + partial_ref[0, begin + j, ft]
                im = im + partial_ref[1, begin + j, ft]
            if final:
                stage_ref[slot, 0, j, :, at] = re
                stage_ref[slot, 1, j, :, at] = im
            else:
                out_ref[0, begin + j, ft] = re
                out_ref[1, begin + j, ft] = im
        return 0

    for h in range(2):
        lax.fori_loop(0, tiles, functools.partial(one_tile, h), 0)
        if final:
            for copy in copies(step, h):
                copy.start()

    if final:

        @pl.when(step == steps - 1)
        def _():
            for back in reversed(range(SLOTS)):
                for copy in copies(step - back, 0) + copies(step - back, 1):
                    copy.wait()


def swap(x, mask, n_chan):
    return lax.ppermute(x, "chan", [(i, i ^ mask) for i in range(n_chan)])


def body(spectra, filter_bank, band_index, window_mask, owner_order, source_offset):
    n_chan = lax.axis_size("chan")
    me = lax.axis_index("chan").astype(jnp.int32)
    _, win, ch, freq = spectra.shape
    banks, taps = filter_bank.shape[1:]
    rounds = owner_order.shape[0]
    count = win * ch
    tiles = freq // LANES
    pieces = win * tiles
    sources = rounds * ch
    in_parts = n_chan == pieces and win == 4 and tiles & (tiles - 1) == 0
    smem = pl.BlockSpec(memory_space=pltpu.SMEM)
    vmem = pl.BlockSpec(memory_space=pltpu.VMEM)

    split = pl.pallas_call(
        split_kernel,
        out_shape=jax.ShapeDtypeStruct((pieces, 2 * ch + 16, LANES), jnp.bfloat16),
        in_specs=[pl.BlockSpec(memory_space=pl.ANY), vmem],
        out_specs=vmem,
        scratch_shapes=[pltpu.VMEM(spectra.shape, jnp.bfloat16), pltpu.SemaphoreType.DMA((win,))],
        compiler_params=room(56),
        name="split",
    )(spectra, window_mask)
    if in_parts:
        held = lax.all_to_all(split, "chan", 0, 0)[:, None]
        first = me
    else:
        held = lax.all_gather(split, "chan")
        first = jnp.int32(0)
    params = jnp.concatenate([first[None], lax.div(first, jnp.int32(win))[None], owner_order])

    ends = n_chan - 1
    before = lax.ppermute(spectra, "chan", [(i, i + 1) for i in range(ends)])
    after = lax.ppermute(spectra, "chan", [(i + 1, i) for i in range(ends)])

    weight, band, index, valid, pick = pl.pallas_call(
        prep_kernel,
        out_shape=(
            jax.ShapeDtypeStruct((2 * banks * 2 * ch, 2 * LANES), jnp.bfloat16),
            jax.ShapeDtypeStruct((freq, freq), jnp.bfloat16),
            jax.ShapeDtypeStruct((tiles, 1, LANES), jnp.int32),
            jax.ShapeDtypeStruct((count, LANES), jnp.float32),
            jax.ShapeDtypeStruct((rounds, ch, ch), jnp.bfloat16),
        ),
        scratch_shapes=[pltpu.VMEM((2, banks, LANES), jnp.float32)],
        compiler_params=room(8),
        name="prep",
    )(filter_bank, band_index.reshape(tiles, 1, LANES), window_mask, source_offset)

    count_here = held.shape[1]
    filtered = pl.pallas_call(
        functools.partial(source_kernel, win=win),
        grid=(count_here,),
        in_specs=[
            smem,
            pl.BlockSpec((n_chan, 1, 2 * ch + 16, LANES), lambda s: (0, s, 0, 0)),
            vmem,
            vmem,
        ],
        out_specs=pl.BlockSpec((1, rounds, 2, ch, LANES), lambda s: (s, 0, 0, 0, 0)),
        out_shape=jax.ShapeDtypeStruct((count_here, rounds, 2, ch, LANES), jnp.bfloat16),
        compiler_params=room(16),
        name="source_filter",
    )(params, held, weight, index)

    if in_parts:
        zparts = [filtered] + [swap(filtered, win * k, n_chan) for k in range(1, tiles)]

    local = pl.pallas_call(
        own_kernel,
        out_shape=jax.ShapeDtypeStruct((2, tiles, win, ch, LANES), jnp.bfloat16),
        in_specs=[vmem] * 7,
        out_specs=vmem,
        scratch_shapes=[pltpu.VMEM((2, count, freq), jnp.float32)],
        compiler_params=room(16),
        cost_estimate=pl.CostEstimate(
            flops=4 * banks * 2 * ch * 2 * LANES * win * freq, bytes_accessed=3 << 20, transcendentals=0
        ),
        name="own_whiten",
    )(before, spectra, after, weight, band, index, valid)

    shape = (tiles, rounds, 2, ch, LANES)
    if in_parts:
        zparts[-1], local = lax.optimization_barrier((zparts[-1], local))
        windows = 1
        specs = [vmem] * tiles
    else:
        windows = win
        zparts = [filtered.reshape((tiles, win) + shape[1:])]
        specs = [pl.BlockSpec((tiles, 1) + shape[1:], lambda s: (0, s, 0, 0, 0, 0))]
    column = pl.pallas_call(
        functools.partial(column_kernel, win=win),
        grid=(windows,),
        in_specs=[smem] + specs + [vmem, vmem],
        out_specs=pl.BlockSpec((1,) + shape, lambda s: (s, 0, 0, 0, 0, 0)),
        out_shape=jax.ShapeDtypeStruct((windows,) + shape, jnp.bfloat16),
        scratch_shapes=[pltpu.VMEM(shape, jnp.bfloat16)],
        compiler_params=room(16),
        name="column_whiten",
    )(params, *zparts, band, pick)

    def cross(masks, columns, earlier, final):
        group = SRC_STEP
        scratch = []
        spec = vmem
        result = jax.ShapeDtypeStruct((2, sources, tiles, ch, LANES), jnp.bfloat16)
        if final:
            spec = pl.BlockSpec(memory_space=pl.ANY)
            result = jax.ShapeDtypeStruct((2, sources, ch, freq), jnp.bfloat16)
            scratch.append(pltpu.VMEM((SLOTS, 2, group, ch, freq), jnp.bfloat16))
            scratch.append(pltpu.SemaphoreType.DMA((SLOTS, 2, 2)))
        return pl.pallas_call(
            functools.partial(cross_kernel, masks=masks, added=len(earlier) > 0, final=final),
            grid=(sources // group,),
            in_specs=[smem] + [vmem] * (len(columns) + 1 + len(earlier)),
            out_specs=spec,
            out_shape=result,
            scratch_shapes=scratch,
            compiler_params=room(32),
            cost_estimate=pl.CostEstimate(
                flops=16 * len(masks) * sources * ch * freq, bytes_accessed=16 << 20, transcendentals=0
            ),
            name="cross",
        )(params, *columns, local, *earlier)

    if not in_parts:
        return cross(tuple(range(win)), [column[w : w + 1] for w in range(win)], [], True)
    far = swap(column, 2, n_chan)
    beside = swap(column, 1, n_chan)
    partial = cross((0, 1), [column, beside], [], False)
    far, partial = lax.optimization_barrier((far, partial))
    return cross((2, 3), [far, swap(far, 1, n_chan)], [partial], True)


def solution(mesh):
    in_specs = (
        P(None, "groups", "chan", None),
        P(),
        P(),
        P("groups", "chan"),
        P("groups"),
        P("groups", None),
    )
    out_specs = P(None, "groups", "chan", None)
    return jax.shard_map(body, mesh=mesh, in_specs=in_specs, out_specs=out_specs, check_vma=False)
```

```python
import functools

import jax
import jax.numpy as jnp
from jax import lax
from jax.experimental import pallas as pl
from jax.experimental.pallas import tpu as pltpu
from jax.sharding import PartitionSpec as P

SMOOTH = 17
LANES = 128
WATER = 0.05
SRC_STEP = 16
SLOTS = 6


def room(mib):
    return pltpu.CompilerParams(vmem_limit_bytes=mib * 1024 * 1024)


def split_kernel(spectra_ref, flags_ref, piece_ref):
    _, win, ch, freq = spectra_ref.shape
    tiles = freq // LANES
    extra = piece_ref.shape[1] - 2 * ch
    for w in range(win):
        flags = jnp.broadcast_to(flags_ref[w : w + 1, :], (extra, ch)).astype(jnp.float32)
        for t in range(tiles):
            at = slice(t * LANES, (t + 1) * LANES)
            piece_ref[t * win + w, :ch] = spectra_ref[0, w, :, at]
            piece_ref[t * win + w, ch : 2 * ch] = spectra_ref[1, w, :, at]
            piece_ref[t * win + w, 2 * ch :] = jnp.zeros((extra, LANES), jnp.bfloat16)
            piece_ref[t * win + w, 2 * ch :, :ch] = flags.astype(jnp.bfloat16)


def prep_kernel(
    bank_ref, bins_ref, flags_ref, offset_ref, weight_ref, band_ref, index_ref, valid_ref, pick_ref, padded_ref
):
    _, banks, taps = bank_ref.shape
    half = weight_ref.shape[0] // 2
    ch = half // (2 * banks)
    index_ref[...] = bins_ref[...]
    channel = lax.broadcasted_iota(jnp.int32, (ch, ch), 0)
    for r in range(offset_ref.shape[0]):
        picked = channel == offset_ref[r : r + 1, :]
        pick_ref[r] = jnp.where(picked, 1.0, 0.0).astype(jnp.bfloat16)
    for w in range(flags_ref.shape[0]):
        column = flag_column(flags_ref[w : w + 1, :])
        valid_ref[w * ch : (w + 1) * ch, :] = jnp.broadcast_to(column, (ch, LANES))
    padded_ref[...] = jnp.zeros(padded_ref.shape, jnp.float32)
    padded_ref[:, :, :taps] = bank_ref[...]

    def skewed(row):
        tile = jnp.broadcast_to(row, (ch, LANES))
        return pltpu.roll(tile, 0, 1, stride=1, stride_axis=0)

    for b in range(banks):
        real = skewed(padded_ref[0, b : b + 1, :])
        imag = skewed(padded_ref[1, b : b + 1, :])
        base = b * 2 * ch
        for row, left, right in ((base, real, -imag), (base + ch, imag, real)):
            for col, val in ((0, left), (LANES, right)):
                high = val.astype(jnp.bfloat16)
                low = (val - high.astype(jnp.float32)).astype(jnp.bfloat16)
                weight_ref[row : row + ch, col : col + LANES] = high
                weight_ref[half + row : half + row + ch, col : col + LANES] = low
    rows = lax.broadcasted_iota(jnp.int32, band_ref.shape, 0)
    cols = lax.broadcasted_iota(jnp.int32, band_ref.shape, 1)
    near = jnp.abs(rows - cols) <= SMOOTH // 2
    band_ref[...] = jnp.where(near, 1.0, 0.0).astype(jnp.bfloat16)


def flag_column(row):
    ch = row.shape[1]
    rows = lax.broadcasted_iota(jnp.int32, (ch, ch), 0)
    cols = lax.broadcasted_iota(jnp.int32, (ch, ch), 1)
    return jnp.sum(jnp.where(rows == cols, row.astype(jnp.float32), 0.0), axis=1, keepdims=True)


def filtered_block(x, weight_ref, index, ch):
    half = weight_ref.shape[0] // 2
    y = jnp.dot(weight_ref[...], x, preferred_element_type=jnp.float32)
    rows = 2 * ch
    pick = y[:rows] + y[half : half + rows]
    for at in range(rows, half, rows):
        here = y[at : at + rows] + y[half + at : half + at + rows]
        pick = jnp.where(index == at // rows, here, pick)
    return pick


def running_scale(real, imag, band_ref):
    count = real.shape[0]
    power = real * real + imag * imag
    high = power.astype(jnp.bfloat16)
    low = (power - high.astype(jnp.float32)).astype(jnp.bfloat16)
    both = jnp.concatenate([high, low], axis=0)
    total = jnp.dot(both, band_ref[...], preferred_element_type=jnp.float32)
    return lax.rsqrt((total[:count] + total[count:]) * (1.0 / SMOOTH) + WATER)


def source_kernel(params_ref, x_ref, weight_ref, index_ref, out_ref, *, win):
    n_chan = x_ref.shape[0]
    _, rounds, _, ch, _ = out_ref.shape
    tile = lax.div(params_ref[0] + pl.program_id(0), win)
    zero = jnp.zeros((), jnp.bfloat16)
    gap = jnp.zeros((LANES - 3 * ch, LANES), jnp.bfloat16)
    columns = []
    for r in range(rounds):
        block = params_ref[2 + r]
        before = jnp.maximum(block - 1, 0)
        after = jnp.minimum(block + 1, n_chan - 1)
        parts = []
        for p in range(2):
            at = slice(p * ch, (p + 1) * ch)
            parts.append(jnp.where(block > 0, x_ref[before, 0, at], zero))
            parts.append(x_ref[block, 0, at])
            parts.append(jnp.where(block < n_chan - 1, x_ref[after, 0, at], zero))
            parts.append(gap)
        columns.append(jnp.concatenate(parts, axis=0))
    x = jnp.concatenate(columns, axis=1)
    index = jnp.concatenate([index_ref[tile]] * rounds, axis=1)
    pick = filtered_block(x, weight_ref, index, ch)
    for r in range(rounds):
        flags = x_ref[params_ref[2 + r], 0, 2 * ch :].astype(jnp.float32)[:1, :ch]
        valid = flag_column(flags)
        for p in range(2):
            part = pick[p * ch : (p + 1) * ch, r * LANES : (r + 1) * LANES] * valid
            out_ref[0, r, p] = part.astype(jnp.bfloat16)


def own_kernel(prev_ref, cur_ref, next_ref, weight_ref, band_ref, index_ref, valid_ref, out_ref, filt_ref):
    _, win, ch, freq = cur_ref.shape
    tiles = freq // LANES
    gap = jnp.zeros((LANES - 3 * ch, freq), jnp.bfloat16)
    index = jnp.concatenate([index_ref[t] for t in range(tiles)], axis=1)

    def one_window(w, _):
        parts = []
        for p in range(2):
            parts += [prev_ref[p, w], cur_ref[p, w], next_ref[p, w], gap]
        x = jnp.concatenate(parts, axis=0)
        pick = filtered_block(x, weight_ref, index, ch)
        at = pl.ds(pl.multiple_of(w * ch, ch), ch)
        filt_ref[0, at, :] = pick[:ch]
        filt_ref[1, at, :] = pick[ch:]
        return 0

    lax.fori_loop(0, win, one_window, 0)
    valid = jnp.concatenate([valid_ref[...]] * tiles, axis=1)
    scale = running_scale(filt_ref[0], filt_ref[1], band_ref) * valid
    for p in range(2):
        white = (filt_ref[p] * scale).astype(jnp.bfloat16)
        for t in range(tiles):
            for w in range(win):
                out_ref[p, t, w] = white[w * ch : (w + 1) * ch, t * LANES : (t + 1) * LANES]


def column_kernel(params_ref, *refs, win):
    band_ref, pick_ref, out_ref, piece_ref = refs[-4:]
    parts = refs[:-4]
    tiles, rounds, _, ch, _ = piece_ref.shape
    if len(parts) == tiles:
        place = params_ref[1]
        for k, ref in enumerate(parts):
            piece_ref[place ^ k] = ref[0]
    else:
        piece_ref[...] = parts[0][:, 0]
    both = []
    for p in range(2):
        rows = []
        for r in range(rounds):
            row = jnp.concatenate([piece_ref[t, r, p] for t in range(tiles)], axis=1)
            rows.append(
                lax.dot_general(
                    pick_ref[r], row, (((0,), (0,)), ((), ())), preferred_element_type=jnp.float32
                )
            )
        both.append(jnp.concatenate(rows, axis=0))
    scale = running_scale(both[0], both[1], band_ref)
    for p in range(2):
        white = (both[p] * scale).astype(jnp.bfloat16) * jnp.bfloat16(1.0 / win)
        for t in range(tiles):
            for r in range(rounds):
                out_ref[0, t, r, p] = white[r * ch : (r + 1) * ch, t * LANES : (t + 1) * LANES]


def spread_row(block, j, ch):
    return jnp.broadcast_to(block[j : j + 1, :], (ch, block.shape[1]))


def pairwise(terms):
    while len(terms) > 1:
        half = (len(terms) + 1) // 2
        terms = [terms[i] + terms[i + half] if i + half < len(terms) else terms[i] for i in range(half)]
    return terms[0]


def cross_kernel(params_ref, *refs, masks, added, final):
    column_refs = refs[: len(masks)]
    local_ref = refs[len(masks)]
    partial_ref = refs[len(masks) + 1]
    if final:
        out_ref, stage_ref, sems = refs[-3:]
    else:
        out_ref = refs[-1]
    tiles, win, ch = local_ref.shape[1:4]
    rounds = column_refs[0].shape[2]
    group = SRC_STEP
    per_round = ch // group
    steps = rounds * per_round
    step = pl.program_id(0)
    r = step // per_round
    begin = step * group
    rows = pl.ds(pl.multiple_of(lax.rem(step, per_round) * group, group), group)
    here = lax.rem(params_ref[0], win)
    slot = lax.rem(step, SLOTS)

    def copies(at_step):
        at_slot = lax.rem(at_step, SLOTS)
        return [
            pltpu.make_async_copy(
                stage_ref.at[at_slot, p], out_ref.at[p, pl.ds(at_step * group, group)], sems.at[at_slot, p]
            )
            for p in range(2)
        ]

    if final:

        @pl.when(step >= SLOTS)
        def _():
            for copy in copies(step - SLOTS):
                copy.wait()

    def one_tile(ft, _):
        at = pl.ds(pl.multiple_of(ft * LANES, LANES), LANES)
        mine = [(local_ref[0, ft, here ^ mask], local_ref[1, ft, here ^ mask]) for mask in masks]
        theirs = [(ref[0, ft, r, 0, rows, :], ref[0, ft, r, 1, rows, :]) for ref in column_refs]
        for j in range(group):
            re = []
            im = []
            for (lr, li), block in zip(mine, theirs):
                sr, si = (spread_row(part, j, ch) for part in block)
                re.append(sr * lr + si * li)
                im.append(sr * li - si * lr)
            re = pairwise(re)
            im = pairwise(im)
            if added:
                re = re + partial_ref[0, begin + j, ft]
                im = im + partial_ref[1, begin + j, ft]
            if final:
                stage_ref[slot, 0, j, :, at] = re
                stage_ref[slot, 1, j, :, at] = im
            else:
                out_ref[0, begin + j, ft] = re
                out_ref[1, begin + j, ft] = im
        return 0

    lax.fori_loop(0, tiles, one_tile, 0)

    if final:
        for copy in copies(step):
            copy.start()

        @pl.when(step == steps - 1)
        def _():
            for back in range(SLOTS):
                for copy in copies(step - back):
                    copy.wait()


def swap(x, mask, n_chan):
    return lax.ppermute(x, "chan", [(i, i ^ mask) for i in range(n_chan)])


def body(spectra, filter_bank, band_index, window_mask, owner_order, source_offset):
    n_chan = lax.axis_size("chan")
    me = lax.axis_index("chan").astype(jnp.int32)
    _, win, ch, freq = spectra.shape
    banks, taps = filter_bank.shape[1:]
    rounds = owner_order.shape[0]
    count = win * ch
    tiles = freq // LANES
    pieces = win * tiles
    sources = rounds * ch
    in_parts = n_chan == pieces and win == 4 and tiles & (tiles - 1) == 0
    smem = pl.BlockSpec(memory_space=pltpu.SMEM)
    vmem = pl.BlockSpec(memory_space=pltpu.VMEM)

    split = pl.pallas_call(
        split_kernel,
        out_shape=jax.ShapeDtypeStruct((pieces, 2 * ch + 16, LANES), jnp.bfloat16),
        compiler_params=room(56),
        name="split",
    )(spectra, window_mask)
    if in_parts:
        held = lax.all_to_all(split, "chan", 0, 0)[:, None]
        first = me
    else:
        held = lax.all_gather(split, "chan")
        first = jnp.int32(0)
    params = jnp.concatenate([first[None], lax.div(first, jnp.int32(win))[None], owner_order])

    ends = n_chan - 1
    before = lax.ppermute(spectra, "chan", [(i, i + 1) for i in range(ends)])
    after = lax.ppermute(spectra, "chan", [(i + 1, i) for i in range(ends)])

    weight, band, index, valid, pick = pl.pallas_call(
        prep_kernel,
        out_shape=(
            jax.ShapeDtypeStruct((2 * banks * 2 * ch, 2 * LANES), jnp.bfloat16),
            jax.ShapeDtypeStruct((freq, freq), jnp.bfloat16),
            jax.ShapeDtypeStruct((tiles, 1, LANES), jnp.int32),
            jax.ShapeDtypeStruct((count, LANES), jnp.float32),
            jax.ShapeDtypeStruct((rounds, ch, ch), jnp.bfloat16),
        ),
        scratch_shapes=[pltpu.VMEM((2, banks, LANES), jnp.float32)],
        compiler_params=room(8),
        name="prep",
    )(filter_bank, band_index.reshape(tiles, 1, LANES), window_mask, source_offset)

    count_here = held.shape[1]
    filtered = pl.pallas_call(
        functools.partial(source_kernel, win=win),
        grid=(count_here,),
        in_specs=[
            smem,
            pl.BlockSpec((n_chan, 1, 2 * ch + 16, LANES), lambda s: (0, s, 0, 0)),
            vmem,
            vmem,
        ],
        out_specs=pl.BlockSpec((1, rounds, 2, ch, LANES), lambda s: (s, 0, 0, 0, 0)),
        out_shape=jax.ShapeDtypeStruct((count_here, rounds, 2, ch, LANES), jnp.bfloat16),
        compiler_params=room(16),
        name="source_filter",
    )(params, held, weight, index)

    if in_parts:
        zparts = [filtered] + [swap(filtered, win * k, n_chan) for k in range(1, tiles)]

    local = pl.pallas_call(
        own_kernel,
        out_shape=jax.ShapeDtypeStruct((2, tiles, win, ch, LANES), jnp.bfloat16),
        in_specs=[vmem] * 7,
        out_specs=vmem,
        scratch_shapes=[pltpu.VMEM((2, count, freq), jnp.float32)],
        compiler_params=room(16),
        cost_estimate=pl.CostEstimate(
            flops=4 * banks * 2 * ch * 2 * LANES * win * freq, bytes_accessed=3 << 20, transcendentals=0
        ),
        name="own_whiten",
    )(before, spectra, after, weight, band, index, valid)

    shape = (tiles, rounds, 2, ch, LANES)
    if in_parts:
        zparts[-1], local = lax.optimization_barrier((zparts[-1], local))
        windows = 1
        specs = [vmem] * tiles
    else:
        windows = win
        zparts = [filtered.reshape((tiles, win) + shape[1:])]
        specs = [pl.BlockSpec((tiles, 1) + shape[1:], lambda s: (0, s, 0, 0, 0, 0))]
    column = pl.pallas_call(
        functools.partial(column_kernel, win=win),
        grid=(windows,),
        in_specs=[smem] + specs + [vmem, vmem],
        out_specs=pl.BlockSpec((1,) + shape, lambda s: (s, 0, 0, 0, 0, 0)),
        out_shape=jax.ShapeDtypeStruct((windows,) + shape, jnp.bfloat16),
        scratch_shapes=[pltpu.VMEM(shape, jnp.bfloat16)],
        compiler_params=room(16),
        name="column_whiten",
    )(params, *zparts, band, pick)

    def cross(masks, columns, earlier, final):
        group = SRC_STEP
        scratch = []
        spec = vmem
        result = jax.ShapeDtypeStruct((2, sources, tiles, ch, LANES), jnp.bfloat16)
        if final:
            spec = pl.BlockSpec(memory_space=pl.ANY)
            result = jax.ShapeDtypeStruct((2, sources, ch, freq), jnp.bfloat16)
            scratch.append(pltpu.VMEM((SLOTS, 2, group, ch, freq), jnp.bfloat16))
            scratch.append(pltpu.SemaphoreType.DMA((SLOTS, 2)))
        return pl.pallas_call(
            functools.partial(cross_kernel, masks=masks, added=len(earlier) > 0, final=final),
            grid=(sources // group,),
            in_specs=[smem] + [vmem] * (len(columns) + 1 + len(earlier)),
            out_specs=spec,
            out_shape=result,
            scratch_shapes=scratch,
            compiler_params=room(32),
            cost_estimate=pl.CostEstimate(
                flops=16 * len(masks) * sources * ch * freq, bytes_accessed=16 << 20, transcendentals=0
            ),
            name="cross",
        )(params, *columns, local, *earlier)

    if not in_parts:
        return cross(tuple(range(win)), [column[w : w + 1] for w in range(win)], [], True)
    far = swap(column, 2, n_chan)
    beside = swap(column, 1, n_chan)
    partial = cross((0, 1), [column, beside], [], False)
    far, partial = lax.optimization_barrier((far, partial))
    return cross((2, 3), [far, swap(far, 1, n_chan)], [partial], True)


def solution(mesh):
    in_specs = (
        P(None, "groups", "chan", None),
        P(),
        P(),
        P("groups", "chan"),
        P("groups"),
        P("groups", None),
    )
    out_specs = P(None, "groups", "chan", None)
    return jax.shard_map(body, mesh=mesh, in_specs=in_specs, out_specs=out_specs, check_vma=False)
```

```python
import functools

import jax
import jax.numpy as jnp
from jax import lax
from jax.experimental import pallas as pl
from jax.experimental.pallas import tpu as pltpu
from jax.sharding import PartitionSpec as P

SMOOTH = 17
LANES = 128
WATER = 0.05
SRC_STEP = 16
SLOTS = 2


def room(mib):
    return pltpu.CompilerParams(vmem_limit_bytes=mib * 1024 * 1024)


def split_kernel(spectra_ref, flags_ref, piece_ref):
    _, win, ch, freq = spectra_ref.shape
    tiles = freq // LANES
    extra = piece_ref.shape[1] - 2 * ch
    for w in range(win):
        flags = jnp.broadcast_to(flags_ref[w : w + 1, :], (extra, ch)).astype(jnp.float32)
        for t in range(tiles):
            at = slice(t * LANES, (t + 1) * LANES)
            piece_ref[t * win + w, :ch] = spectra_ref[0, w, :, at]
            piece_ref[t * win + w, ch : 2 * ch] = spectra_ref[1, w, :, at]
            piece_ref[t * win + w, 2 * ch :] = jnp.zeros((extra, LANES), jnp.bfloat16)
            piece_ref[t * win + w, 2 * ch :, :ch] = flags.astype(jnp.bfloat16)


def prep_kernel(
    bank_ref, bins_ref, flags_ref, offset_ref, weight_ref, band_ref, index_ref, valid_ref, pick_ref, padded_ref
):
    _, banks, taps = bank_ref.shape
    half = weight_ref.shape[0] // 2
    ch = half // (2 * banks)
    index_ref[...] = bins_ref[...]
    channel = lax.broadcasted_iota(jnp.int32, (ch, ch), 0)
    for r in range(offset_ref.shape[0]):
        picked = channel == offset_ref[r : r + 1, :]
        pick_ref[r] = jnp.where(picked, 1.0, 0.0).astype(jnp.bfloat16)
    for w in range(flags_ref.shape[0]):
        column = flag_column(flags_ref[w : w + 1, :])
        valid_ref[w * ch : (w + 1) * ch, :] = jnp.broadcast_to(column, (ch, LANES))
    padded_ref[...] = jnp.zeros(padded_ref.shape, jnp.float32)
    padded_ref[:, :, :taps] = bank_ref[...]

    def skewed(row):
        tile = jnp.broadcast_to(row, (ch, LANES))
        return pltpu.roll(tile, 0, 1, stride=1, stride_axis=0)

    for b in range(banks):
        real = skewed(padded_ref[0, b : b + 1, :])
        imag = skewed(padded_ref[1, b : b + 1, :])
        base = b * 2 * ch
        for row, left, right in ((base, real, -imag), (base + ch, imag, real)):
            for col, val in ((0, left), (LANES, right)):
                high = val.astype(jnp.bfloat16)
                low = (val - high.astype(jnp.float32)).astype(jnp.bfloat16)
                weight_ref[row : row + ch, col : col + LANES] = high
                weight_ref[half + row : half + row + ch, col : col + LANES] = low
    rows = lax.broadcasted_iota(jnp.int32, band_ref.shape, 0)
    cols = lax.broadcasted_iota(jnp.int32, band_ref.shape, 1)
    near = jnp.abs(rows - cols) <= SMOOTH // 2
    band_ref[...] = jnp.where(near, 1.0, 0.0).astype(jnp.bfloat16)


def flag_column(row):
    ch = row.shape[1]
    rows = lax.broadcasted_iota(jnp.int32, (ch, ch), 0)
    cols = lax.broadcasted_iota(jnp.int32, (ch, ch), 1)
    return jnp.sum(jnp.where(rows == cols, row.astype(jnp.float32), 0.0), axis=1, keepdims=True)


def filtered_block(x, weight_ref, index, ch):
    half = weight_ref.shape[0] // 2
    y = jnp.dot(weight_ref[...], x, preferred_element_type=jnp.float32)
    rows = 2 * ch
    pick = y[:rows] + y[half : half + rows]
    for at in range(rows, half, rows):
        here = y[at : at + rows] + y[half + at : half + at + rows]
        pick = jnp.where(index == at // rows, here, pick)
    return pick


def running_scale(real, imag, band_ref):
    count = real.shape[0]
    power = real * real + imag * imag
    high = power.astype(jnp.bfloat16)
    low = (power - high.astype(jnp.float32)).astype(jnp.bfloat16)
    both = jnp.concatenate([high, low], axis=0)
    total = jnp.dot(both, band_ref[...], preferred_element_type=jnp.float32)
    return lax.rsqrt((total[:count] + total[count:]) * (1.0 / SMOOTH) + WATER)


def source_kernel(params_ref, x_ref, weight_ref, index_ref, out_ref, *, win):
    n_chan = x_ref.shape[0]
    _, rounds, _, ch, _ = out_ref.shape
    tile = lax.div(params_ref[0] + pl.program_id(0), win)
    zero = jnp.zeros((), jnp.bfloat16)
    gap = jnp.zeros((LANES - 3 * ch, LANES), jnp.bfloat16)
    columns = []
    for r in range(rounds):
        block = params_ref[2 + r]
        before = jnp.maximum(block - 1, 0)
        after = jnp.minimum(block + 1, n_chan - 1)
        parts = []
        for p in range(2):
            at = slice(p * ch, (p + 1) * ch)
            parts.append(jnp.where(block > 0, x_ref[before, 0, at], zero))
            parts.append(x_ref[block, 0, at])
            parts.append(jnp.where(block < n_chan - 1, x_ref[after, 0, at], zero))
            parts.append(gap)
        columns.append(jnp.concatenate(parts, axis=0))
    x = jnp.concatenate(columns, axis=1)
    index = jnp.concatenate([index_ref[tile]] * rounds, axis=1)
    pick = filtered_block(x, weight_ref, index, ch)
    for r in range(rounds):
        flags = x_ref[params_ref[2 + r], 0, 2 * ch :].astype(jnp.float32)[:1, :ch]
        valid = flag_column(flags)
        for p in range(2):
            part = pick[p * ch : (p + 1) * ch, r * LANES : (r + 1) * LANES] * valid
            out_ref[0, r, p] = part.astype(jnp.bfloat16)


def own_kernel(prev_ref, cur_ref, next_ref, weight_ref, band_ref, index_ref, valid_ref, out_ref, filt_ref):
    _, win, ch, freq = cur_ref.shape
    tiles = freq // LANES
    gap = jnp.zeros((LANES - 3 * ch, freq), jnp.bfloat16)
    index = jnp.concatenate([index_ref[t] for t in range(tiles)], axis=1)

    def one_window(w, _):
        parts = []
        for p in range(2):
            parts += [prev_ref[p, w], cur_ref[p, w], next_ref[p, w], gap]
        x = jnp.concatenate(parts, axis=0)
        pick = filtered_block(x, weight_ref, index, ch)
        at = pl.ds(pl.multiple_of(w * ch, ch), ch)
        filt_ref[0, at, :] = pick[:ch]
        filt_ref[1, at, :] = pick[ch:]
        return 0

    lax.fori_loop(0, win, one_window, 0)
    valid = jnp.concatenate([valid_ref[...]] * tiles, axis=1)
    scale = running_scale(filt_ref[0], filt_ref[1], band_ref) * valid
    for p in range(2):
        white = (filt_ref[p] * scale).astype(jnp.bfloat16)
        for t in range(tiles):
            for w in range(win):
                out_ref[p, t, w] = white[w * ch : (w + 1) * ch, t * LANES : (t + 1) * LANES]


def column_kernel(params_ref, *refs, win):
    band_ref, pick_ref, out_ref, piece_ref = refs[-4:]
    parts = refs[:-4]
    tiles, rounds, _, ch, _ = piece_ref.shape
    if len(parts) == tiles:
        place = params_ref[1]
        for k, ref in enumerate(parts):
            piece_ref[place ^ k] = ref[0]
    else:
        piece_ref[...] = parts[0][:, 0]
    both = []
    for p in range(2):
        rows = []
        for r in range(rounds):
            row = jnp.concatenate([piece_ref[t, r, p] for t in range(tiles)], axis=1)
            rows.append(
                lax.dot_general(
                    pick_ref[r], row, (((0,), (0,)), ((), ())), preferred_element_type=jnp.float32
                )
            )
        both.append(jnp.concatenate(rows, axis=0))
    scale = running_scale(both[0], both[1], band_ref)
    for p in range(2):
        white = (both[p] * scale).astype(jnp.bfloat16) * jnp.bfloat16(1.0 / win)
        for t in range(tiles):
            for r in range(rounds):
                out_ref[0, t, r, p] = white[r * ch : (r + 1) * ch, t * LANES : (t + 1) * LANES]


def spread_row(block, j, ch):
    return jnp.broadcast_to(block[j : j + 1, :], (ch, block.shape[1]))


def pairwise(terms):
    while len(terms) > 1:
        half = (len(terms) + 1) // 2
        terms = [terms[i] + terms[i + half] if i + half < len(terms) else terms[i] for i in range(half)]
    return terms[0]


def cross_kernel(params_ref, *refs, masks, added, final):
    column_refs = refs[: len(masks)]
    local_ref = refs[len(masks)]
    partial_ref = refs[len(masks) + 1]
    if final:
        out_ref, stage_ref, sems = refs[-3:]
    else:
        out_ref = refs[-1]
    tiles, win, ch = local_ref.shape[1:4]
    rounds = column_refs[0].shape[2]
    group = SRC_STEP
    per_round = ch // group
    steps = rounds * per_round
    step = pl.program_id(0)
    r = step // per_round
    begin = step * group
    rows = pl.ds(pl.multiple_of(lax.rem(step, per_round) * group, group), group)
    here = lax.rem(params_ref[0], win)
    slot = lax.rem(step, SLOTS)

    def copies(at_step):
        at_slot = lax.rem(at_step, SLOTS)
        return [
            pltpu.make_async_copy(
                stage_ref.at[at_slot, p], out_ref.at[p, pl.ds(at_step * group, group)], sems.at[at_slot, p]
            )
            for p in range(2)
        ]

    if final:

        @pl.when(step >= SLOTS)
        def _():
            for copy in copies(step - SLOTS):
                copy.wait()

    def one_tile(ft, _):
        at = pl.ds(pl.multiple_of(ft * LANES, LANES), LANES)
        mine = [(local_ref[0, ft, here ^ mask], local_ref[1, ft, here ^ mask]) for mask in masks]
        theirs = [(ref[0, ft, r, 0, rows, :], ref[0, ft, r, 1, rows, :]) for ref in column_refs]
        for j in range(group):
            re = []
            im = []
            for (lr, li), block in zip(mine, theirs):
                sr, si = (spread_row(part, j, ch) for part in block)
                re.append(sr * lr + si * li)
                im.append(sr * li - si * lr)
            re = pairwise(re)
            im = pairwise(im)
            if added:
                re = re + partial_ref[0, begin + j, ft]
                im = im + partial_ref[1, begin + j, ft]
            if final:
                stage_ref[slot, 0, j, :, at] = re
                stage_ref[slot, 1, j, :, at] = im
            else:
                out_ref[0, begin + j, ft] = re
                out_ref[1, begin + j, ft] = im
        return 0

    lax.fori_loop(0, tiles, one_tile, 0)

    if final:
        for copy in copies(step):
            copy.start()

        @pl.when(step == steps - 1)
        def _():
            for back in range(SLOTS):
                for copy in copies(step - back):
                    copy.wait()


def swap(x, mask, n_chan):
    return lax.ppermute(x, "chan", [(i, i ^ mask) for i in range(n_chan)])


def body(spectra, filter_bank, band_index, window_mask, owner_order, source_offset):
    n_chan = lax.axis_size("chan")
    me = lax.axis_index("chan").astype(jnp.int32)
    _, win, ch, freq = spectra.shape
    banks, taps = filter_bank.shape[1:]
    rounds = owner_order.shape[0]
    count = win * ch
    tiles = freq // LANES
    pieces = win * tiles
    sources = rounds * ch
    in_parts = n_chan == pieces and win == 4 and tiles & (tiles - 1) == 0
    smem = pl.BlockSpec(memory_space=pltpu.SMEM)
    vmem = pl.BlockSpec(memory_space=pltpu.VMEM)

    split = pl.pallas_call(
        split_kernel,
        out_shape=jax.ShapeDtypeStruct((pieces, 2 * ch + 16, LANES), jnp.bfloat16),
        compiler_params=room(56),
        name="split",
    )(spectra, window_mask)
    if in_parts:
        held = lax.all_to_all(split, "chan", 0, 0)[:, None]
        first = me
    else:
        held = lax.all_gather(split, "chan")
        first = jnp.int32(0)
    params = jnp.concatenate([first[None], lax.div(first, jnp.int32(win))[None], owner_order])

    ends = n_chan - 1
    before = lax.ppermute(spectra, "chan", [(i, i + 1) for i in range(ends)])
    after = lax.ppermute(spectra, "chan", [(i + 1, i) for i in range(ends)])

    weight, band, index, valid, pick = pl.pallas_call(
        prep_kernel,
        out_shape=(
            jax.ShapeDtypeStruct((2 * banks * 2 * ch, 2 * LANES), jnp.bfloat16),
            jax.ShapeDtypeStruct((freq, freq), jnp.bfloat16),
            jax.ShapeDtypeStruct((tiles, 1, LANES), jnp.int32),
            jax.ShapeDtypeStruct((count, LANES), jnp.float32),
            jax.ShapeDtypeStruct((rounds, ch, ch), jnp.bfloat16),
        ),
        scratch_shapes=[pltpu.VMEM((2, banks, LANES), jnp.float32)],
        compiler_params=room(8),
        name="prep",
    )(filter_bank, band_index.reshape(tiles, 1, LANES), window_mask, source_offset)

    count_here = held.shape[1]
    filtered = pl.pallas_call(
        functools.partial(source_kernel, win=win),
        grid=(count_here,),
        in_specs=[
            smem,
            pl.BlockSpec((n_chan, 1, 2 * ch + 16, LANES), lambda s: (0, s, 0, 0)),
            vmem,
            vmem,
        ],
        out_specs=pl.BlockSpec((1, rounds, 2, ch, LANES), lambda s: (s, 0, 0, 0, 0)),
        out_shape=jax.ShapeDtypeStruct((count_here, rounds, 2, ch, LANES), jnp.bfloat16),
        compiler_params=room(16),
        name="source_filter",
    )(params, held, weight, index)

    if in_parts:
        zparts = [filtered] + [swap(filtered, win * k, n_chan) for k in range(1, tiles)]

    local = pl.pallas_call(
        own_kernel,
        out_shape=jax.ShapeDtypeStruct((2, tiles, win, ch, LANES), jnp.bfloat16),
        in_specs=[vmem] * 7,
        out_specs=vmem,
        scratch_shapes=[pltpu.VMEM((2, count, freq), jnp.float32)],
        compiler_params=room(16),
        cost_estimate=pl.CostEstimate(
            flops=4 * banks * 2 * ch * 2 * LANES * win * freq, bytes_accessed=3 << 20, transcendentals=0
        ),
        name="own_whiten",
    )(before, spectra, after, weight, band, index, valid)

    shape = (tiles, rounds, 2, ch, LANES)
    if in_parts:
        zparts[-1], local = lax.optimization_barrier((zparts[-1], local))
        windows = 1
        specs = [vmem] * tiles
    else:
        windows = win
        zparts = [filtered.reshape((tiles, win) + shape[1:])]
        specs = [pl.BlockSpec((tiles, 1) + shape[1:], lambda s: (0, s, 0, 0, 0, 0))]
    column = pl.pallas_call(
        functools.partial(column_kernel, win=win),
        grid=(windows,),
        in_specs=[smem] + specs + [vmem, vmem],
        out_specs=pl.BlockSpec((1,) + shape, lambda s: (s, 0, 0, 0, 0, 0)),
        out_shape=jax.ShapeDtypeStruct((windows,) + shape, jnp.bfloat16),
        scratch_shapes=[pltpu.VMEM(shape, jnp.bfloat16)],
        compiler_params=room(16),
        name="column_whiten",
    )(params, *zparts, band, pick)

    def cross(masks, columns, earlier, final):
        group = SRC_STEP
        scratch = []
        spec = vmem
        result = jax.ShapeDtypeStruct((2, sources, tiles, ch, LANES), jnp.bfloat16)
        if final:
            spec = pl.BlockSpec(memory_space=pl.ANY)
            result = jax.ShapeDtypeStruct((2, sources, ch, freq), jnp.bfloat16)
            scratch.append(pltpu.VMEM((SLOTS, 2, group, ch, freq), jnp.bfloat16))
            scratch.append(pltpu.SemaphoreType.DMA((SLOTS, 2)))
        return pl.pallas_call(
            functools.partial(cross_kernel, masks=masks, added=len(earlier) > 0, final=final),
            grid=(sources // group,),
            in_specs=[smem] + [vmem] * (len(columns) + 1 + len(earlier)),
            out_specs=spec,
            out_shape=result,
            scratch_shapes=scratch,
            compiler_params=room(32),
            cost_estimate=pl.CostEstimate(
                flops=16 * len(masks) * sources * ch * freq, bytes_accessed=16 << 20, transcendentals=0
            ),
            name="cross",
        )(params, *columns, local, *earlier)

    if not in_parts:
        return cross(tuple(range(win)), [column[w : w + 1] for w in range(win)], [], True)
    far = swap(column, 2, n_chan)
    beside = swap(column, 1, n_chan)
    partial = cross((0, 1), [column, beside], [], False)
    far, partial = lax.optimization_barrier((far, partial))
    return cross((2, 3), [far, swap(far, 1, n_chan)], [partial], True)


def solution(mesh):
    in_specs = (
        P(None, "groups", "chan", None),
        P(),
        P(),
        P("groups", "chan"),
        P("groups"),
        P("groups", None),
    )
    out_specs = P(None, "groups", "chan", None)
    return jax.shard_map(body, mesh=mesh, in_specs=in_specs, out_specs=out_specs, check_vma=False)
```

```python
import functools

import jax
import jax.numpy as jnp
from jax import lax
from jax.experimental import pallas as pl
from jax.experimental.pallas import tpu as pltpu
from jax.sharding import PartitionSpec as P

SMOOTH = 17
LANES = 128
WATER = 0.05
SRC_STEP = 16
SLOTS = 4


def room(mib):
    return pltpu.CompilerParams(vmem_limit_bytes=mib * 1024 * 1024)


def split_kernel(spectra_ref, flags_ref, piece_ref):
    _, win, ch, freq = spectra_ref.shape
    tiles = freq // LANES
    extra = piece_ref.shape[1] - 2 * ch
    for w in range(win):
        flags = jnp.broadcast_to(flags_ref[w : w + 1, :], (extra, ch)).astype(jnp.float32)
        for t in range(tiles):
            at = slice(t * LANES, (t + 1) * LANES)
            piece_ref[t * win + w, :ch] = spectra_ref[0, w, :, at]
            piece_ref[t * win + w, ch : 2 * ch] = spectra_ref[1, w, :, at]
            piece_ref[t * win + w, 2 * ch :] = jnp.zeros((extra, LANES), jnp.bfloat16)
            piece_ref[t * win + w, 2 * ch :, :ch] = flags.astype(jnp.bfloat16)


def prep_kernel(
    bank_ref, bins_ref, flags_ref, offset_ref, weight_ref, band_ref, index_ref, valid_ref, pick_ref, padded_ref
):
    _, banks, taps = bank_ref.shape
    half = weight_ref.shape[0] // 2
    ch = half // (2 * banks)
    index_ref[...] = bins_ref[...]
    channel = lax.broadcasted_iota(jnp.int32, (ch, ch), 0)
    for r in range(offset_ref.shape[0]):
        picked = channel == offset_ref[r : r + 1, :]
        pick_ref[r] = jnp.where(picked, 1.0, 0.0).astype(jnp.bfloat16)
    for w in range(flags_ref.shape[0]):
        column = flag_column(flags_ref[w : w + 1, :])
        valid_ref[w * ch : (w + 1) * ch, :] = jnp.broadcast_to(column, (ch, LANES))
    padded_ref[...] = jnp.zeros(padded_ref.shape, jnp.float32)
    padded_ref[:, :, :taps] = bank_ref[...]

    def skewed(row):
        tile = jnp.broadcast_to(row, (ch, LANES))
        return pltpu.roll(tile, 0, 1, stride=1, stride_axis=0)

    for b in range(banks):
        real = skewed(padded_ref[0, b : b + 1, :])
        imag = skewed(padded_ref[1, b : b + 1, :])
        base = b * 2 * ch
        for row, left, right in ((base, real, -imag), (base + ch, imag, real)):
            for col, val in ((0, left), (LANES, right)):
                high = val.astype(jnp.bfloat16)
                low = (val - high.astype(jnp.float32)).astype(jnp.bfloat16)
                weight_ref[row : row + ch, col : col + LANES] = high
                weight_ref[half + row : half + row + ch, col : col + LANES] = low
    rows = lax.broadcasted_iota(jnp.int32, band_ref.shape, 0)
    cols = lax.broadcasted_iota(jnp.int32, band_ref.shape, 1)
    near = jnp.abs(rows - cols) <= SMOOTH // 2
    band_ref[...] = jnp.where(near, 1.0, 0.0).astype(jnp.bfloat16)


def flag_column(row):
    ch = row.shape[1]
    rows = lax.broadcasted_iota(jnp.int32, (ch, ch), 0)
    cols = lax.broadcasted_iota(jnp.int32, (ch, ch), 1)
    return jnp.sum(jnp.where(rows == cols, row.astype(jnp.float32), 0.0), axis=1, keepdims=True)


def filtered_block(x, weight_ref, index, ch):
    half = weight_ref.shape[0] // 2
    y = jnp.dot(weight_ref[...], x, preferred_element_type=jnp.float32)
    rows = 2 * ch
    pick = y[:rows] + y[half : half + rows]
    for at in range(rows, half, rows):
        here = y[at : at + rows] + y[half + at : half + at + rows]
        pick = jnp.where(index == at // rows, here, pick)
    return pick


def running_scale(real, imag, band_ref):
    count = real.shape[0]
    power = real * real + imag * imag
    high = power.astype(jnp.bfloat16)
    low = (power - high.astype(jnp.float32)).astype(jnp.bfloat16)
    both = jnp.concatenate([high, low], axis=0)
    total = jnp.dot(both, band_ref[...], preferred_element_type=jnp.float32)
    return lax.rsqrt((total[:count] + total[count:]) * (1.0 / SMOOTH) + WATER)


def source_kernel(params_ref, x_ref, weight_ref, index_ref, out_ref, *, win):
    n_chan = x_ref.shape[0]
    _, rounds, _, ch, _ = out_ref.shape
    tile = lax.div(params_ref[0] + pl.program_id(0), win)
    zero = jnp.zeros((), jnp.bfloat16)
    gap = jnp.zeros((LANES - 3 * ch, LANES), jnp.bfloat16)
    columns = []
    for r in range(rounds):
        block = params_ref[2 + r]
        before = jnp.maximum(block - 1, 0)
        after = jnp.minimum(block + 1, n_chan - 1)
        parts = []
        for p in range(2):
            at = slice(p * ch, (p + 1) * ch)
            parts.append(jnp.where(block > 0, x_ref[before, 0, at], zero))
            parts.append(x_ref[block, 0, at])
            parts.append(jnp.where(block < n_chan - 1, x_ref[after, 0, at], zero))
            parts.append(gap)
        columns.append(jnp.concatenate(parts, axis=0))
    x = jnp.concatenate(columns, axis=1)
    index = jnp.concatenate([index_ref[tile]] * rounds, axis=1)
    pick = filtered_block(x, weight_ref, index, ch)
    for r in range(rounds):
        flags = x_ref[params_ref[2 + r], 0, 2 * ch :].astype(jnp.float32)[:1, :ch]
        valid = flag_column(flags)
        for p in range(2):
            part = pick[p * ch : (p + 1) * ch, r * LANES : (r + 1) * LANES] * valid
            out_ref[0, r, p] = part.astype(jnp.bfloat16)


def own_kernel(prev_ref, cur_ref, next_ref, weight_ref, band_ref, index_ref, valid_ref, out_ref, filt_ref):
    _, win, ch, freq = cur_ref.shape
    tiles = freq // LANES
    gap = jnp.zeros((LANES - 3 * ch, freq), jnp.bfloat16)
    index = jnp.concatenate([index_ref[t] for t in range(tiles)], axis=1)

    def one_window(w, _):
        parts = []
        for p in range(2):
            parts += [prev_ref[p, w], cur_ref[p, w], next_ref[p, w], gap]
        x = jnp.concatenate(parts, axis=0)
        pick = filtered_block(x, weight_ref, index, ch)
        at = pl.ds(pl.multiple_of(w * ch, ch), ch)
        filt_ref[0, at, :] = pick[:ch]
        filt_ref[1, at, :] = pick[ch:]
        return 0

    lax.fori_loop(0, win, one_window, 0)
    valid = jnp.concatenate([valid_ref[...]] * tiles, axis=1)
    scale = running_scale(filt_ref[0], filt_ref[1], band_ref) * valid
    for p in range(2):
        white = (filt_ref[p] * scale).astype(jnp.bfloat16)
        for t in range(tiles):
            for w in range(win):
                out_ref[p, t, w] = white[w * ch : (w + 1) * ch, t * LANES : (t + 1) * LANES]


def column_kernel(params_ref, *refs, win):
    band_ref, pick_ref, out_ref, piece_ref = refs[-4:]
    parts = refs[:-4]
    tiles, rounds, _, ch, _ = piece_ref.shape
    if len(parts) == tiles:
        place = params_ref[1]
        for k, ref in enumerate(parts):
            piece_ref[place ^ k] = ref[0]
    else:
        piece_ref[...] = parts[0][:, 0]
    both = []
    for p in range(2):
        rows = []
        for r in range(rounds):
            row = jnp.concatenate([piece_ref[t, r, p] for t in range(tiles)], axis=1)
            rows.append(
                lax.dot_general(
                    pick_ref[r], row, (((0,), (0,)), ((), ())), preferred_element_type=jnp.float32
                )
            )
        both.append(jnp.concatenate(rows, axis=0))
    scale = running_scale(both[0], both[1], band_ref)
    for p in range(2):
        white = (both[p] * scale).astype(jnp.bfloat16) * jnp.bfloat16(1.0 / win)
        for t in range(tiles):
            for r in range(rounds):
                out_ref[0, t, r, p] = white[r * ch : (r + 1) * ch, t * LANES : (t + 1) * LANES]


def spread_row(block, j, ch):
    return jnp.broadcast_to(block[j : j + 1, :], (ch, block.shape[1]))


def pairwise(terms):
    while len(terms) > 1:
        half = (len(terms) + 1) // 2
        terms = [terms[i] + terms[i + half] if i + half < len(terms) else terms[i] for i in range(half)]
    return terms[0]


def cross_kernel(params_ref, *refs, masks, added, final):
    column_refs = refs[: len(masks)]
    local_ref = refs[len(masks)]
    partial_ref = refs[len(masks) + 1]
    if final:
        out_ref, stage_ref, sems = refs[-3:]
    else:
        out_ref = refs[-1]
    tiles, win, ch = local_ref.shape[1:4]
    rounds = column_refs[0].shape[2]
    group = SRC_STEP
    per_round = ch // group
    steps = rounds * per_round
    step = pl.program_id(0)
    r = step // per_round
    begin = step * group
    rows = pl.ds(pl.multiple_of(lax.rem(step, per_round) * group, group), group)
    here = lax.rem(params_ref[0], win)
    slot = lax.rem(step, SLOTS)

    def copies(at_step):
        at_slot = lax.rem(at_step, SLOTS)
        return [
            pltpu.make_async_copy(
                stage_ref.at[at_slot, p], out_ref.at[p, pl.ds(at_step * group, group)], sems.at[at_slot, p]
            )
            for p in range(2)
        ]

    if final:

        @pl.when(step >= SLOTS)
        def _():
            for copy in copies(step - SLOTS):
                copy.wait()

    def one_tile(ft, _):
        at = pl.ds(pl.multiple_of(ft * LANES, LANES), LANES)
        mine = [(local_ref[0, ft, here ^ mask], local_ref[1, ft, here ^ mask]) for mask in masks]
        theirs = [(ref[0, ft, r, 0, rows, :], ref[0, ft, r, 1, rows, :]) for ref in column_refs]
        for j in range(group):
            re = []
            im = []
            for (lr, li), block in zip(mine, theirs):
                sr, si = (spread_row(part, j, ch) for part in block)
                re.append(sr * lr + si * li)
                im.append(sr * li - si * lr)
            re = pairwise(re)
            im = pairwise(im)
            if added:
                re = re + partial_ref[0, begin + j, ft]
                im = im + partial_ref[1, begin + j, ft]
            if final:
                stage_ref[slot, 0, j, :, at] = re
                stage_ref[slot, 1, j, :, at] = im
            else:
                out_ref[0, begin + j, ft] = re
                out_ref[1, begin + j, ft] = im
        return 0

    lax.fori_loop(0, tiles, one_tile, 0)

    if final:
        for copy in copies(step):
            copy.start()

        @pl.when(step == steps - 1)
        def _():
            for back in range(SLOTS):
                for copy in copies(step - back):
                    copy.wait()


def swap(x, mask, n_chan):
    return lax.ppermute(x, "chan", [(i, i ^ mask) for i in range(n_chan)])


def body(spectra, filter_bank, band_index, window_mask, owner_order, source_offset):
    n_chan = lax.axis_size("chan")
    me = lax.axis_index("chan").astype(jnp.int32)
    _, win, ch, freq = spectra.shape
    banks, taps = filter_bank.shape[1:]
    rounds = owner_order.shape[0]
    count = win * ch
    tiles = freq // LANES
    pieces = win * tiles
    sources = rounds * ch
    in_parts = n_chan == pieces and win == 4 and tiles & (tiles - 1) == 0
    smem = pl.BlockSpec(memory_space=pltpu.SMEM)
    vmem = pl.BlockSpec(memory_space=pltpu.VMEM)

    split = pl.pallas_call(
        split_kernel,
        out_shape=jax.ShapeDtypeStruct((pieces, 2 * ch + 16, LANES), jnp.bfloat16),
        compiler_params=room(56),
        name="split",
    )(spectra, window_mask)
    if in_parts:
        held = lax.all_to_all(split, "chan", 0, 0)[:, None]
        first = me
    else:
        held = lax.all_gather(split, "chan")
        first = jnp.int32(0)
    params = jnp.concatenate([first[None], lax.div(first, jnp.int32(win))[None], owner_order])

    ends = n_chan - 1
    before = lax.ppermute(spectra, "chan", [(i, i + 1) for i in range(ends)])
    after = lax.ppermute(spectra, "chan", [(i + 1, i) for i in range(ends)])

    weight, band, index, valid, pick = pl.pallas_call(
        prep_kernel,
        out_shape=(
            jax.ShapeDtypeStruct((2 * banks * 2 * ch, 2 * LANES), jnp.bfloat16),
            jax.ShapeDtypeStruct((freq, freq), jnp.bfloat16),
            jax.ShapeDtypeStruct((tiles, 1, LANES), jnp.int32),
            jax.ShapeDtypeStruct((count, LANES), jnp.float32),
            jax.ShapeDtypeStruct((rounds, ch, ch), jnp.bfloat16),
        ),
        scratch_shapes=[pltpu.VMEM((2, banks, LANES), jnp.float32)],
        compiler_params=room(8),
        name="prep",
    )(filter_bank, band_index.reshape(tiles, 1, LANES), window_mask, source_offset)

    count_here = held.shape[1]
    filtered = pl.pallas_call(
        functools.partial(source_kernel, win=win),
        grid=(count_here,),
        in_specs=[
            smem,
            pl.BlockSpec((n_chan, 1, 2 * ch + 16, LANES), lambda s: (0, s, 0, 0)),
            vmem,
            vmem,
        ],
        out_specs=pl.BlockSpec((1, rounds, 2, ch, LANES), lambda s: (s, 0, 0, 0, 0)),
        out_shape=jax.ShapeDtypeStruct((count_here, rounds, 2, ch, LANES), jnp.bfloat16),
        compiler_params=room(16),
        name="source_filter",
    )(params, held, weight, index)

    if in_parts:
        zparts = [filtered] + [swap(filtered, win * k, n_chan) for k in range(1, tiles)]

    local = pl.pallas_call(
        own_kernel,
        out_shape=jax.ShapeDtypeStruct((2, tiles, win, ch, LANES), jnp.bfloat16),
        in_specs=[vmem] * 7,
        out_specs=vmem,
        scratch_shapes=[pltpu.VMEM((2, count, freq), jnp.float32)],
        compiler_params=room(16),
        cost_estimate=pl.CostEstimate(
            flops=4 * banks * 2 * ch * 2 * LANES * win * freq, bytes_accessed=3 << 20, transcendentals=0
        ),
        name="own_whiten",
    )(before, spectra, after, weight, band, index, valid)

    shape = (tiles, rounds, 2, ch, LANES)
    if in_parts:
        zparts[-1], local = lax.optimization_barrier((zparts[-1], local))
        windows = 1
        specs = [vmem] * tiles
    else:
        windows = win
        zparts = [filtered.reshape((tiles, win) + shape[1:])]
        specs = [pl.BlockSpec((tiles, 1) + shape[1:], lambda s: (0, s, 0, 0, 0, 0))]
    column = pl.pallas_call(
        functools.partial(column_kernel, win=win),
        grid=(windows,),
        in_specs=[smem] + specs + [vmem, vmem],
        out_specs=pl.BlockSpec((1,) + shape, lambda s: (s, 0, 0, 0, 0, 0)),
        out_shape=jax.ShapeDtypeStruct((windows,) + shape, jnp.bfloat16),
        scratch_shapes=[pltpu.VMEM(shape, jnp.bfloat16)],
        compiler_params=room(16),
        name="column_whiten",
    )(params, *zparts, band, pick)

    def cross(masks, columns, earlier, final):
        group = SRC_STEP
        scratch = []
        spec = vmem
        result = jax.ShapeDtypeStruct((2, sources, tiles, ch, LANES), jnp.bfloat16)
        if final:
            spec = pl.BlockSpec(memory_space=pl.ANY)
            result = jax.ShapeDtypeStruct((2, sources, ch, freq), jnp.bfloat16)
            scratch.append(pltpu.VMEM((SLOTS, 2, group, ch, freq), jnp.bfloat16))
            scratch.append(pltpu.SemaphoreType.DMA((SLOTS, 2)))
        return pl.pallas_call(
            functools.partial(cross_kernel, masks=masks, added=len(earlier) > 0, final=final),
            grid=(sources // group,),
            in_specs=[smem] + [vmem] * (len(columns) + 1 + len(earlier)),
            out_specs=spec,
            out_shape=result,
            scratch_shapes=scratch,
            compiler_params=room(32),
            cost_estimate=pl.CostEstimate(
                flops=16 * len(masks) * sources * ch * freq, bytes_accessed=16 << 20, transcendentals=0
            ),
            name="cross",
        )(params, *columns, local, *earlier)

    if not in_parts:
        return cross(tuple(range(win)), [column[w : w + 1] for w in range(win)], [], True)
    far = swap(column, 2, n_chan)
    beside = swap(column, 1, n_chan)
    partial = cross((0, 1), [column, beside], [], False)
    far, partial = lax.optimization_barrier((far, partial))
    return cross((2, 3), [far, swap(far, 1, n_chan)], [partial], True)


def solution(mesh):
    in_specs = (
        P(None, "groups", "chan", None),
        P(),
        P(),
        P("groups", "chan"),
        P("groups"),
        P("groups", None),
    )
    out_specs = P(None, "groups", "chan", None)
    return jax.shard_map(body, mesh=mesh, in_specs=in_specs, out_specs=out_specs, check_vma=False)
```

```python
import functools

import jax
import jax.numpy as jnp
from jax import lax
from jax.experimental import pallas as pl
from jax.experimental.pallas import tpu as pltpu
from jax.sharding import PartitionSpec as P

SMOOTH = 17
LANES = 128
WATER = 0.05
SRC_STEP = 16
SLOTS = 5


def room(mib):
    return pltpu.CompilerParams(vmem_limit_bytes=mib * 1024 * 1024)


def split_kernel(spectra_ref, flags_ref, piece_ref):
    _, win, ch, freq = spectra_ref.shape
    tiles = freq // LANES
    extra = piece_ref.shape[1] - 2 * ch
    for w in range(win):
        flags = jnp.broadcast_to(flags_ref[w : w + 1, :], (extra, ch)).astype(jnp.float32)
        for t in range(tiles):
            at = slice(t * LANES, (t + 1) * LANES)
            piece_ref[t * win + w, :ch] = spectra_ref[0, w, :, at]
            piece_ref[t * win + w, ch : 2 * ch] = spectra_ref[1, w, :, at]
            piece_ref[t * win + w, 2 * ch :] = jnp.zeros((extra, LANES), jnp.bfloat16)
            piece_ref[t * win + w, 2 * ch :, :ch] = flags.astype(jnp.bfloat16)


def prep_kernel(
    bank_ref, bins_ref, flags_ref, offset_ref, weight_ref, band_ref, index_ref, valid_ref, pick_ref, padded_ref
):
    _, banks, taps = bank_ref.shape
    half = weight_ref.shape[0] // 2
    ch = half // (2 * banks)
    index_ref[...] = bins_ref[...]
    channel = lax.broadcasted_iota(jnp.int32, (ch, ch), 0)
    for r in range(offset_ref.shape[0]):
        picked = channel == offset_ref[r : r + 1, :]
        pick_ref[r] = jnp.where(picked, 1.0, 0.0).astype(jnp.bfloat16)
    for w in range(flags_ref.shape[0]):
        column = flag_column(flags_ref[w : w + 1, :])
        valid_ref[w * ch : (w + 1) * ch, :] = jnp.broadcast_to(column, (ch, LANES))
    padded_ref[...] = jnp.zeros(padded_ref.shape, jnp.float32)
    padded_ref[:, :, :taps] = bank_ref[...]

    def skewed(row):
        tile = jnp.broadcast_to(row, (ch, LANES))
        return pltpu.roll(tile, 0, 1, stride=1, stride_axis=0)

    for b in range(banks):
        real = skewed(padded_ref[0, b : b + 1, :])
        imag = skewed(padded_ref[1, b : b + 1, :])
        base = b * 2 * ch
        for row, left, right in ((base, real, -imag), (base + ch, imag, real)):
            for col, val in ((0, left), (LANES, right)):
                high = val.astype(jnp.bfloat16)
                low = (val - high.astype(jnp.float32)).astype(jnp.bfloat16)
                weight_ref[row : row + ch, col : col + LANES] = high
                weight_ref[half + row : half + row + ch, col : col + LANES] = low
    rows = lax.broadcasted_iota(jnp.int32, band_ref.shape, 0)
    cols = lax.broadcasted_iota(jnp.int32, band_ref.shape, 1)
    near = jnp.abs(rows - cols) <= SMOOTH // 2
    band_ref[...] = jnp.where(near, 1.0, 0.0).astype(jnp.bfloat16)


def flag_column(row):
    ch = row.shape[1]
    rows = lax.broadcasted_iota(jnp.int32, (ch, ch), 0)
    cols = lax.broadcasted_iota(jnp.int32, (ch, ch), 1)
    return jnp.sum(jnp.where(rows == cols, row.astype(jnp.float32), 0.0), axis=1, keepdims=True)


def filtered_block(x, weight_ref, index, ch):
    half = weight_ref.shape[0] // 2
    y = jnp.dot(weight_ref[...], x, preferred_element_type=jnp.float32)
    rows = 2 * ch
    pick = y[:rows] + y[half : half + rows]
    for at in range(rows, half, rows):
        here = y[at : at + rows] + y[half + at : half + at + rows]
        pick = jnp.where(index == at // rows, here, pick)
    return pick


def running_scale(real, imag, band_ref):
    count = real.shape[0]
    power = real * real + imag * imag
    high = power.astype(jnp.bfloat16)
    low = (power - high.astype(jnp.float32)).astype(jnp.bfloat16)
    both = jnp.concatenate([high, low], axis=0)
    total = jnp.dot(both, band_ref[...], preferred_element_type=jnp.float32)
    return lax.rsqrt((total[:count] + total[count:]) * (1.0 / SMOOTH) + WATER)


def source_kernel(params_ref, x_ref, weight_ref, index_ref, out_ref, *, win):
    n_chan = x_ref.shape[0]
    _, rounds, _, ch, _ = out_ref.shape
    tile = lax.div(params_ref[0] + pl.program_id(0), win)
    zero = jnp.zeros((), jnp.bfloat16)
    gap = jnp.zeros((LANES - 3 * ch, LANES), jnp.bfloat16)
    columns = []
    for r in range(rounds):
        block = params_ref[2 + r]
        before = jnp.maximum(block - 1, 0)
        after = jnp.minimum(block + 1, n_chan - 1)
        parts = []
        for p in range(2):
            at = slice(p * ch, (p + 1) * ch)
            parts.append(jnp.where(block > 0, x_ref[before, 0, at], zero))
            parts.append(x_ref[block, 0, at])
            parts.append(jnp.where(block < n_chan - 1, x_ref[after, 0, at], zero))
            parts.append(gap)
        columns.append(jnp.concatenate(parts, axis=0))
    x = jnp.concatenate(columns, axis=1)
    index = jnp.concatenate([index_ref[tile]] * rounds, axis=1)
    pick = filtered_block(x, weight_ref, index, ch)
    for r in range(rounds):
        flags = x_ref[params_ref[2 + r], 0, 2 * ch :].astype(jnp.float32)[:1, :ch]
        valid = flag_column(flags)
        for p in range(2):
            part = pick[p * ch : (p + 1) * ch, r * LANES : (r + 1) * LANES] * valid
            out_ref[0, r, p] = part.astype(jnp.bfloat16)


def own_kernel(prev_ref, cur_ref, next_ref, weight_ref, band_ref, index_ref, valid_ref, out_ref, filt_ref):
    _, win, ch, freq = cur_ref.shape
    tiles = freq // LANES
    gap = jnp.zeros((LANES - 3 * ch, freq), jnp.bfloat16)
    index = jnp.concatenate([index_ref[t] for t in range(tiles)], axis=1)

    def one_window(w, _):
        parts = []
        for p in range(2):
            parts += [prev_ref[p, w], cur_ref[p, w], next_ref[p, w], gap]
        x = jnp.concatenate(parts, axis=0)
        pick = filtered_block(x, weight_ref, index, ch)
        at = pl.ds(pl.multiple_of(w * ch, ch), ch)
        filt_ref[0, at, :] = pick[:ch]
        filt_ref[1, at, :] = pick[ch:]
        return 0

    lax.fori_loop(0, win, one_window, 0)
    valid = jnp.concatenate([valid_ref[...]] * tiles, axis=1)
    scale = running_scale(filt_ref[0], filt_ref[1], band_ref) * valid
    for p in range(2):
        white = (filt_ref[p] * scale).astype(jnp.bfloat16)
        for t in range(tiles):
            for w in range(win):
                out_ref[p, t, w] = white[w * ch : (w + 1) * ch, t * LANES : (t + 1) * LANES]


def column_kernel(params_ref, *refs, win):
    band_ref, pick_ref, out_ref, piece_ref = refs[-4:]
    parts = refs[:-4]
    tiles, rounds, _, ch, _ = piece_ref.shape
    if len(parts) == tiles:
        place = params_ref[1]
        for k, ref in enumerate(parts):
            piece_ref[place ^ k] = ref[0]
    else:
        piece_ref[...] = parts[0][:, 0]
    both = []
    for p in range(2):
        rows = []
        for r in range(rounds):
            row = jnp.concatenate([piece_ref[t, r, p] for t in range(tiles)], axis=1)
            rows.append(
                lax.dot_general(
                    pick_ref[r], row, (((0,), (0,)), ((), ())), preferred_element_type=jnp.float32
                )
            )
        both.append(jnp.concatenate(rows, axis=0))
    scale = running_scale(both[0], both[1], band_ref)
    for p in range(2):
        white = (both[p] * scale).astype(jnp.bfloat16) * jnp.bfloat16(1.0 / win)
        for t in range(tiles):
            for r in range(rounds):
                out_ref[0, t, r, p] = white[r * ch : (r + 1) * ch, t * LANES : (t + 1) * LANES]


def spread_row(block, j, ch):
    return jnp.broadcast_to(block[j : j + 1, :], (ch, block.shape[1]))


def pairwise(terms):
    while len(terms) > 1:
        half = (len(terms) + 1) // 2
        terms = [terms[i] + terms[i + half] if i + half < len(terms) else terms[i] for i in range(half)]
    return terms[0]


def cross_kernel(params_ref, *refs, masks, added, final):
    column_refs = refs[: len(masks)]
    local_ref = refs[len(masks)]
    partial_ref = refs[len(masks) + 1]
    if final:
        out_ref, stage_ref, sems = refs[-3:]
    else:
        out_ref = refs[-1]
    tiles, win, ch = local_ref.shape[1:4]
    rounds = column_refs[0].shape[2]
    group = SRC_STEP
    per_round = ch // group
    steps = rounds * per_round
    step = pl.program_id(0)
    r = step // per_round
    begin = step * group
    rows = pl.ds(pl.multiple_of(lax.rem(step, per_round) * group, group), group)
    here = lax.rem(params_ref[0], win)
    slot = lax.rem(step, SLOTS)

    def copies(at_step):
        at_slot = lax.rem(at_step, SLOTS)
        return [
            pltpu.make_async_copy(
                stage_ref.at[at_slot, p], out_ref.at[p, pl.ds(at_step * group, group)], sems.at[at_slot, p]
            )
            for p in range(2)
        ]

    if final:

        @pl.when(step >= SLOTS)
        def _():
            for copy in copies(step - SLOTS):
                copy.wait()

    def one_tile(ft, _):
        at = pl.ds(pl.multiple_of(ft * LANES, LANES), LANES)
        mine = [(local_ref[0, ft, here ^ mask], local_ref[1, ft, here ^ mask]) for mask in masks]
        theirs = [(ref[0, ft, r, 0, rows, :], ref[0, ft, r, 1, rows, :]) for ref in column_refs]
        for j in range(group):
            re = []
            im = []
            for (lr, li), block in zip(mine, theirs):
                sr, si = (spread_row(part, j, ch) for part in block)
                re.append(sr * lr + si * li)
                im.append(sr * li - si * lr)
            re = pairwise(re)
            im = pairwise(im)
            if added:
                re = re + partial_ref[0, begin + j, ft]
                im = im + partial_ref[1, begin + j, ft]
            if final:
                stage_ref[slot, 0, j, :, at] = re
                stage_ref[slot, 1, j, :, at] = im
            else:
                out_ref[0, begin + j, ft] = re
                out_ref[1, begin + j, ft] = im
        return 0

    lax.fori_loop(0, tiles, one_tile, 0)

    if final:
        for copy in copies(step):
            copy.start()

        @pl.when(step == steps - 1)
        def _():
            for back in range(SLOTS):
                for copy in copies(step - back):
                    copy.wait()


def swap(x, mask, n_chan):
    return lax.ppermute(x, "chan", [(i, i ^ mask) for i in range(n_chan)])


def body(spectra, filter_bank, band_index, window_mask, owner_order, source_offset):
    n_chan = lax.axis_size("chan")
    me = lax.axis_index("chan").astype(jnp.int32)
    _, win, ch, freq = spectra.shape
    banks, taps = filter_bank.shape[1:]
    rounds = owner_order.shape[0]
    count = win * ch
    tiles = freq // LANES
    pieces = win * tiles
    sources = rounds * ch
    in_parts = n_chan == pieces and win == 4 and tiles & (tiles - 1) == 0
    smem = pl.BlockSpec(memory_space=pltpu.SMEM)
    vmem = pl.BlockSpec(memory_space=pltpu.VMEM)

    split = pl.pallas_call(
        split_kernel,
        out_shape=jax.ShapeDtypeStruct((pieces, 2 * ch + 16, LANES), jnp.bfloat16),
        compiler_params=room(56),
        name="split",
    )(spectra, window_mask)
    if in_parts:
        held = lax.all_to_all(split, "chan", 0, 0)[:, None]
        first = me
    else:
        held = lax.all_gather(split, "chan")
        first = jnp.int32(0)
    params = jnp.concatenate([first[None], lax.div(first, jnp.int32(win))[None], owner_order])

    ends = n_chan - 1
    before = lax.ppermute(spectra, "chan", [(i, i + 1) for i in range(ends)])
    after = lax.ppermute(spectra, "chan", [(i + 1, i) for i in range(ends)])

    weight, band, index, valid, pick = pl.pallas_call(
        prep_kernel,
        out_shape=(
            jax.ShapeDtypeStruct((2 * banks * 2 * ch, 2 * LANES), jnp.bfloat16),
            jax.ShapeDtypeStruct((freq, freq), jnp.bfloat16),
            jax.ShapeDtypeStruct((tiles, 1, LANES), jnp.int32),
            jax.ShapeDtypeStruct((count, LANES), jnp.float32),
            jax.ShapeDtypeStruct((rounds, ch, ch), jnp.bfloat16),
        ),
        scratch_shapes=[pltpu.VMEM((2, banks, LANES), jnp.float32)],
        compiler_params=room(8),
        name="prep",
    )(filter_bank, band_index.reshape(tiles, 1, LANES), window_mask, source_offset)

    count_here = held.shape[1]
    filtered = pl.pallas_call(
        functools.partial(source_kernel, win=win),
        grid=(count_here,),
        in_specs=[
            smem,
            pl.BlockSpec((n_chan, 1, 2 * ch + 16, LANES), lambda s: (0, s, 0, 0)),
            vmem,
            vmem,
        ],
        out_specs=pl.BlockSpec((1, rounds, 2, ch, LANES), lambda s: (s, 0, 0, 0, 0)),
        out_shape=jax.ShapeDtypeStruct((count_here, rounds, 2, ch, LANES), jnp.bfloat16),
        compiler_params=room(16),
        name="source_filter",
    )(params, held, weight, index)

    if in_parts:
        zparts = [filtered] + [swap(filtered, win * k, n_chan) for k in range(1, tiles)]

    local = pl.pallas_call(
        own_kernel,
        out_shape=jax.ShapeDtypeStruct((2, tiles, win, ch, LANES), jnp.bfloat16),
        in_specs=[vmem] * 7,
        out_specs=vmem,
        scratch_shapes=[pltpu.VMEM((2, count, freq), jnp.float32)],
        compiler_params=room(16),
        cost_estimate=pl.CostEstimate(
            flops=4 * banks * 2 * ch * 2 * LANES * win * freq, bytes_accessed=3 << 20, transcendentals=0
        ),
        name="own_whiten",
    )(before, spectra, after, weight, band, index, valid)

    shape = (tiles, rounds, 2, ch, LANES)
    if in_parts:
        zparts[-1], local = lax.optimization_barrier((zparts[-1], local))
        windows = 1
        specs = [vmem] * tiles
    else:
        windows = win
        zparts = [filtered.reshape((tiles, win) + shape[1:])]
        specs = [pl.BlockSpec((tiles, 1) + shape[1:], lambda s: (0, s, 0, 0, 0, 0))]
    column = pl.pallas_call(
        functools.partial(column_kernel, win=win),
        grid=(windows,),
        in_specs=[smem] + specs + [vmem, vmem],
        out_specs=pl.BlockSpec((1,) + shape, lambda s: (s, 0, 0, 0, 0, 0)),
        out_shape=jax.ShapeDtypeStruct((windows,) + shape, jnp.bfloat16),
        scratch_shapes=[pltpu.VMEM(shape, jnp.bfloat16)],
        compiler_params=room(16),
        name="column_whiten",
    )(params, *zparts, band, pick)

    def cross(masks, columns, earlier, final):
        group = SRC_STEP
        scratch = []
        spec = vmem
        result = jax.ShapeDtypeStruct((2, sources, tiles, ch, LANES), jnp.bfloat16)
        if final:
            spec = pl.BlockSpec(memory_space=pl.ANY)
            result = jax.ShapeDtypeStruct((2, sources, ch, freq), jnp.bfloat16)
            scratch.append(pltpu.VMEM((SLOTS, 2, group, ch, freq), jnp.bfloat16))
            scratch.append(pltpu.SemaphoreType.DMA((SLOTS, 2)))
        return pl.pallas_call(
            functools.partial(cross_kernel, masks=masks, added=len(earlier) > 0, final=final),
            grid=(sources // group,),
            in_specs=[smem] + [vmem] * (len(columns) + 1 + len(earlier)),
            out_specs=spec,
            out_shape=result,
            scratch_shapes=scratch,
            compiler_params=room(32),
            cost_estimate=pl.CostEstimate(
                flops=16 * len(masks) * sources * ch * freq, bytes_accessed=16 << 20, transcendentals=0
            ),
            name="cross",
        )(params, *columns, local, *earlier)

    if not in_parts:
        return cross(tuple(range(win)), [column[w : w + 1] for w in range(win)], [], True)
    far = swap(column, 2, n_chan)
    beside = swap(column, 1, n_chan)
    partial = cross((0, 1), [column, beside], [], False)
    far, partial = lax.optimization_barrier((far, partial))
    return cross((2, 3), [far, swap(far, 1, n_chan)], [partial], True)


def solution(mesh):
    in_specs = (
        P(None, "groups", "chan", None),
        P(),
        P(),
        P("groups", "chan"),
        P("groups"),
        P("groups", None),
    )
    out_specs = P(None, "groups", "chan", None)
    return jax.shard_map(body, mesh=mesh, in_specs=in_specs, out_specs=out_specs, check_vma=False)
```
